32 devices in a mesh: dp: 8 (over y, x, core), tp: 4 (over z).
Axes of the slice: x: 2, y: 2, z: 4, core: 2. Of those that a mesh axis runs over, the one named last changes fastest.
Arguments:
- tokens: bfloat16 [8, 1536, 1536], P('dp'), may hold values from -6 to 6
- attn_in: bfloat16 [4, 1536, 1536], P(None, 'dp', 'tp'), may hold values from -0.15625 to 0.15625
- head_gates: bfloat16 [3, 1536, 24], P(None, 'dp', 'tp'), may hold values from -0.15625 to 0.15625
- out_proj: bfloat16 [1536, 1536], P('tp', 'dp'), may hold values from -0.875 to 0.875
- norm_gains: bfloat16 [2, 1536], P(None, 'dp'), may hold values from 0.5 to 1.5
- qk_gains: bfloat16 [2, 64], replicated, may hold values from 0.5 to 1.5
- forget_bias: bfloat16 [24], replicated, may hold values from -1 to 8
- gate_up: bfloat16 [2, 1536, 4096], P(None, 'dp', 'tp'), may hold values from -0.15625 to 0.15625
- down_proj: bfloat16 [4096, 1536], P('tp', 'dp'), may hold values from -0.09375 to 0.09375
- carried_offset: float32 [8, 24], P('dp'), may hold values from -2 to 2
- reset_flag: int32 [8], P('dp'), may hold values from 0 to 1
- cotangent: bfloat16 [8, 1536, 1536], P('dp'), may hold values from -6 to 6
Outputs:
- layer_out: bfloat16 [8, 1536, 1536], P('dp', 'tp')
- grad_tokens: float32 [8, 1536, 1536], P('dp', 'tp')
- grad_attn_in: float32 [4, 1536, 1536], P(None, 'dp', 'tp')
- grad_head_gates: float32 [3, 1536, 24], P(None, 'dp', 'tp')
- grad_out_proj: float32 [1536, 1536], P('tp', 'dp')
- grad_gate_up: float32 [2, 1536, 4096], P(None, 'dp', 'tp')
- grad_down_proj: float32 [4096, 1536], P('tp', 'dp')
- grad_norm_gains: float32 [2, 1536], replicated
- grad_qk_gains: float32 [2, 64], replicated
- grad_forget_bias: float32 [24], replicated
The draws below stay inside these ranges and needn't reach their ends.
All inputs are finite; a program needn't handle non-finite values.
Results may differ from the reference program's by a relative error of at most 0.014.
Values may be sent and summed in bfloat16 or wider, within the bound.
No kernel may reach another device: no remote copies, remote signals or barrier semaphores. Data moves between devices by JAX's collectives and lax.ppermute only.
A program may use at most 320 MiB of HBM per device.

```python
from functools import partial
import jax
import jax.numpy as jnp
from jax import lax

D = 1536
H = 24
DH = 64
FF = 4096
SEQ = 1536
QBLOCK = 512
ITEMS = 8


def plant(entries, own_key, smallest, high):
    longest = entries.shape.index(max(entries.shape))
    spots = []
    for shift in (0, 1):
        where = [jax.random.randint(jax.random.fold_in(own_key, axis), (), 0, length) for axis, length in enumerate(entries.shape)]
        where[longest] = (where[longest] + shift) % entries.shape[longest]
        spots.append(tuple(where))
    return entries.at[spots[0]].set(smallest).at[spots[1]].set(high)


def spiked(entries, own_key, source, target, blocks, factor):
    owner, partner = [(jnp.arange(entries.shape[position]) // (entries.shape[position] // blocks)).reshape([-1 if axis == position else 1 for axis in range(entries.ndim)]) for position in (source, target)]
    chosen = jax.random.permutation(own_key, blocks)[partner]
    strong = (owner == chosen) | (owner == (partner + blocks // 2) % blocks)
    return jnp.where(strong, factor * entries, entries)


def block_scale(own_key, shape, split, low, high):
    factor_of, own = 1.0, jax.random.fold_in(own_key, 6)
    for position, parts in split:
        steps = jnp.exp(jax.random.uniform(jax.random.fold_in(own, position), (parts,), jnp.float32, low / len(split), high / len(split)))
        factor_of = factor_of * jnp.repeat(steps, shape[position] // parts).reshape([-1 if axis == position else 1 for axis in range(len(shape))])
    return factor_of


def noise(rng, extent, deviation, most, pieces=(), kind=jnp.bfloat16):
    values = deviation * jax.random.normal(rng, extent, jnp.float32)
    if pieces:
        values = values * block_scale(rng, extent, pieces, -0.22, 0.18)
    return jnp.clip(values, -most, most).astype(kind)


def heavy_noise(rng, extent, deviation, bound, split, heavy, kind=jnp.bfloat16):
    entries = deviation * jax.random.normal(rng, extent, jnp.float32)
    if split:
        entries = entries * block_scale(rng, extent, split, -0.22, 0.18)
    return jnp.clip(spiked(entries, jax.random.fold_in(rng, 3), *heavy), -bound, bound).astype(kind)


def setup_inputs(seed: int = 0) -> dict:
    keys = jax.random.split(jax.random.key(seed), 13)
    tokens = heavy_noise(keys[0], (ITEMS, SEQ, D), 1.0, 6.0, ((0, 8),), (0, 2, 8, 2.0))
    attn_in = noise(keys[1], (4, D, D), D ** -0.5, 0.15625, ((1, 8), (2, 4)))
    head_gates = noise(keys[2], (3, D, H), D ** -0.5, 0.15625, ((1, 8), (2, 4)))
    out_proj = noise(keys[3], (D, D), (D // 32) ** -0.5, 0.875, ((0, 4), (1, 8)))
    norm_gains = jnp.clip(1.0 + 0.1 * jax.random.normal(keys[4], (2, D), jnp.float32), 0.5, 1.5).astype(jnp.bfloat16)
    qk_gains = jnp.clip(1.0 + 0.1 * jax.random.normal(keys[5], (2, DH), jnp.float32), 0.5, 1.5).astype(jnp.bfloat16)
    forget_bias = jnp.clip(jax.random.uniform(keys[6], (H,), jnp.float32, -1.0, 8.0), -1.0, 8.0).astype(jnp.bfloat16)
    gate_up = noise(keys[7], (2, D, FF), D ** -0.5, 0.15625, ((1, 8), (2, 4)))
    down_proj = noise(keys[8], (FF, D), FF ** -0.5, 0.09375, ((0, 4), (1, 8)))
    carried_offset = jnp.clip(jax.random.uniform(keys[9], (ITEMS, H), jnp.float32, -2.0, 2.0) * block_scale(keys[9], (ITEMS, H), ((0, 8),), -0.4, 0.0), -2.0, 2.0)
    reset_flag = plant(jax.random.randint(keys[10], (ITEMS,), 0, 2), jax.random.fold_in(keys[10], 1), 0, 1).astype(jnp.int32)
    cotangent = noise(keys[11], (ITEMS, SEQ, D), 1.0, 6.0, ((0, 8),))
    return {"tokens": tokens, "attn_in": attn_in, "head_gates": head_gates, "out_proj": out_proj, "norm_gains": norm_gains, "qk_gains": qk_gains, "forget_bias": forget_bias, "gate_up": gate_up, "down_proj": down_proj, "carried_offset": carried_offset, "reset_flag": reset_flag, "cotangent": cotangent}


EPSILON = 1e-06
HIGHEST = lax.Precision.HIGHEST

@jax.custom_vjp
def low(v):
    return lax.optimization_barrier(v.astype(jnp.bfloat16)).astype(jnp.float32)

@jax.custom_vjp
def low_back(v):
    return v

def low_keep(v):
    return (low(v), None)

def low_pass(kept, grad):
    return (grad,)

def back_keep(v):
    return (v, None)

def back_low(kept, grad):
    return (low(grad),)
low.defvjp(low_keep, low_pass)
low_back.defvjp(back_keep, back_low)

def rms_apply(values, gain_row):
    return values * lax.rsqrt(lax.optimization_barrier(jnp.mean(values * values, -1, keepdims=True)) + EPSILON) * gain_row

def token_shift(values, mixing):
    earlier = jnp.concatenate([jnp.zeros_like(values[:, :1]), values[:, :-1]], axis=1)
    return mixing[..., None] * earlier + (1.0 - mixing[..., None]) * values

def attend_item(packed):
    query_item, key_item, value_item, cum_item = packed
    seq_len = query_item.shape[0]
    head_scale = query_item.shape[2] ** (-0.5)
    key_pos = jnp.arange(seq_len).astype(jnp.int32)

    def one_block(block_start):
        q_block = lax.dynamic_slice_in_dim(query_item, block_start, QBLOCK, 0)
        c_block = lax.dynamic_slice_in_dim(cum_item, block_start, QBLOCK, 0)
        raw_scores = low_back(jnp.einsum('qhd,khd->hqk', q_block, key_item, precision=HIGHEST) * head_scale)
        scores = raw_scores + jnp.transpose(c_block)[:, :, None] - jnp.transpose(cum_item)[:, None, :]
        allowed = (block_start + jnp.arange(QBLOCK).astype(jnp.int32))[:, None] >= key_pos[None, :]
        scores = jnp.where(allowed[None], scores, -1e+30)
        weights = jnp.exp(scores - lax.optimization_barrier(jnp.max(scores, -1, keepdims=True)))
        prob_low = low(weights / lax.optimization_barrier(jnp.sum(weights, -1, keepdims=True)))
        return jnp.einsum('hqk,khd->qhd', prob_low, value_item, precision=HIGHEST)
    starts = (jnp.arange(seq_len // QBLOCK) * QBLOCK).astype(jnp.int32)
    blocks = lax.map(jax.checkpoint(one_block), starts)
    return blocks.reshape(query_item.shape)

def forward(inputs, attn_in, head_gates, out_proj, norm_gains, qk_gains, forget_bias, gate_up, down_proj, offset_term):
    item_count, seq_len, model_width = inputs.shape
    head_count = forget_bias.shape[0]
    head_size = qk_gains.shape[1]
    head_shape = (item_count, seq_len, head_count, head_size)
    normed = low(rms_apply(inputs, norm_gains[0]))
    projected = low_back(jnp.einsum('bsd,mde->mbse', normed, attn_in, precision=HIGHEST))
    gate_logits = low_back(jnp.einsum('bsd,mdh->mbsh', normed, head_gates, precision=HIGHEST))
    query_raw = projected[0].reshape(head_shape)
    key_raw = projected[1].reshape(head_shape)
    value_raw = projected[2].reshape(head_shape)
    key_mix = jax.nn.sigmoid(gate_logits[0])
    value_mix = jax.nn.sigmoid(gate_logits[1])
    query_normed = low(rms_apply(query_raw, qk_gains[0]))
    key_normed = low(rms_apply(token_shift(key_raw, key_mix), qk_gains[1]))
    value_shifted = low(token_shift(value_raw, value_mix))
    cumulative = jnp.cumsum(jax.nn.log_sigmoid(gate_logits[2] + forget_bias + offset_term), axis=1)
    attended = low_back(lax.map(attend_item, (query_normed, key_normed, value_shifted, cumulative)))
    out_gate = jax.nn.sigmoid(projected[3])
    gated = low(attended.reshape(item_count, seq_len, model_width) * out_gate)
    mixed = inputs + low_back(jnp.einsum('bse,ed->bsd', gated, out_proj, precision=HIGHEST))
    mid_normed = low(rms_apply(mixed, norm_gains[1]))
    gate_pre = low_back(jnp.einsum('bsd,mdf->mbsf', mid_normed, gate_up, precision=HIGHEST))
    hidden = low(jax.nn.silu(gate_pre[0]) * gate_pre[1])
    return mixed + low_back(jnp.einsum('bsf,fd->bsd', hidden, down_proj, precision=HIGHEST))

def reference(tokens, attn_in, head_gates, out_proj, norm_gains, qk_gains, forget_bias, gate_up, down_proj, carried_offset, reset_flag, cotangent):
    offset_term = (1 - reset_flag).astype(jnp.float32)[:, None, None] * carried_offset.astype(jnp.float32)[:, None, :]
    params = [tokens.astype(jnp.float32), attn_in.astype(jnp.float32), head_gates.astype(jnp.float32), out_proj.astype(jnp.float32), norm_gains.astype(jnp.float32), qk_gains.astype(jnp.float32), forget_bias.astype(jnp.float32), gate_up.astype(jnp.float32), down_proj.astype(jnp.float32)]
    result, pullback = jax.vjp(partial(forward, offset_term=offset_term), *params)
    grad_list = pullback(cotangent.astype(jnp.float32))
    return (result.astype(jnp.bfloat16), grad_list[0], grad_list[1], grad_list[2], grad_list[3], grad_list[7], grad_list[8], grad_list[4], grad_list[5], grad_list[6])
```

```python
import functools

import jax
import jax.numpy as jnp
import numpy as np
from jax import lax
from jax.experimental import pallas as pl
from jax.experimental.pallas import tpu as pltpu
from jax.sharding import PartitionSpec as P

EPS = 1e-06
BF = jnp.bfloat16
F32 = jnp.float32
VMEM_LIMIT = 58 * 1024 * 1024
NT = (((1,), (1,)), ((), ()))
TN = (((0,), (0,)), ((), ()))


def dot(a, b, dims=(((1,), (0,)), ((), ()))):
    return lax.dot_general(a, b, dims, preferred_element_type=F32)


def params():
    return pltpu.CompilerParams(vmem_limit_bytes=VMEM_LIMIT)


def split2(v):
    hi = v.astype(BF)
    return hi, (v - hi.astype(F32)).astype(BF)


def split3(v):
    hi = v.astype(BF)
    rest = v - hi.astype(F32)
    mid = rest.astype(BF)
    return hi, mid, (rest - mid.astype(F32)).astype(BF)


def lanes(shape):
    return lax.broadcasted_iota(jnp.int32, shape, len(shape) - 1)


def rows_of(shape):
    return lax.broadcasted_iota(jnp.int32, shape, 0)


def const(array, dtype=BF):
    return jnp.asarray(array.astype(np.float32), dtype)


def full(shape):
    return pl.BlockSpec(shape, lambda *_: tuple(0 for _ in shape), pipeline_mode=pl.Buffered(1))


ANY = pl.BlockSpec(memory_space=pl.ANY)
SMEM = pl.BlockSpec(memory_space=pltpu.SMEM)


def pre_kernel(
    heads, x_ref, we_ref, wo_ref, ba_ref, g64_ref, tri_ref, mq_ref, mk_ref, rows_ref, gqk_ref,
    hn_ref, gain_ref, q8_ref, kn_ref, vl_ref, aq_ref, ak_ref, og_ref, q_ref, ks_ref, kd_ref, vd_ref, lg_ref,
    gain_s, carry_k, carry_v, carry_c,
):
    step = pl.program_id(0)
    half = we_ref.shape[0]
    width = q8_ref.shape[1]
    wide = 4 * width

    @pl.when(step == 0)
    def _():
        pick = (lanes((8, 128)) == 3 * heads + rows_of((8, 128))).astype(F32)
        pick = jnp.where(rows_of((8, 128)) < 2, pick, 0.0).astype(BF)
        gain_s[:, :half] = dot(pick, we_ref[:, wide:], NT)
        gain_s[:, half:] = dot(pick, wo_ref[:, wide:], NT)
        carry_k[...] = jnp.zeros_like(carry_k)
        carry_v[...] = jnp.zeros_like(carry_v)
        carry_c[...] = jnp.zeros_like(carry_c)
        gain_ref[...] = gain_s[...]

    x = x_ref[...].astype(F32)
    factor = lax.rsqrt(jnp.mean(x * x, -1, keepdims=True) + EPS)
    hn = (x * factor * gain_s[0:1, :]).astype(BF)
    hn_ref[...] = hn
    proj = dot(hn[:, :half], we_ref[...]) + dot(hn[:, half:], wo_ref[...])
    q = proj[:, :width]
    k = proj[:, width : 2 * width]
    v = proj[:, 2 * width : 3 * width]
    og_ref[...] = jax.nn.sigmoid(proj[:, 3 * width : wide])
    logits = proj[:, wide:]
    lg_ref[...] = logits
    mix = dot(jnp.concatenate(split2(jax.nn.sigmoid(logits)), 1), ba_ref[...])
    first = rows_of(k.shape) == 0
    kd = jnp.where(first, carry_k[0:1, :], pltpu.roll(k, 1, 0)) - k
    vd = jnp.where(first, carry_v[0:1, :], pltpu.roll(v, 1, 0)) - v
    last = k.shape[0] - 1
    carry_k[0:1, :] = k[last:, :]
    carry_v[0:1, :] = v[last:, :]
    ks = k + mix[:, :width] * kd
    vl_ref[...] = (v + mix[:, width:] * vd).astype(BF)
    q_ref[...] = q.astype(BF)
    ks_ref[...] = ks.astype(BF)
    kd_ref[...] = kd.astype(BF)
    vd_ref[...] = vd.astype(BF)
    rq = lax.rsqrt(dot((q * q).astype(BF), g64_ref[...]) + EPS)
    rk = lax.rsqrt(dot((ks * ks).astype(BF), g64_ref[...]) + EPS)
    q8_ref[...] = ((q * rq * gqk_ref[0:1, :]).astype(BF).astype(F32) * 0.125).astype(BF)
    kn_ref[...] = (ks * rk * gqk_ref[1:2, :]).astype(BF)
    z = logits + rows_ref[0:1, :]
    ls = jnp.minimum(z, 0.0) - jnp.log1p(jnp.exp(-jnp.abs(z)))
    sums = dot(tri_ref[...], jnp.concatenate(split3(ls), 1))
    cum = sums[:, :128] + sums[:, 128:256] + sums[:, 256:] + carry_c[0:1, :]
    carry_c[0:1, :] = cum[last:, :]
    parts = jnp.concatenate(split3(cum), 1)
    aq_ref[...] = (dot(parts, mq_ref[...]) + rows_ref[1:2, :]).astype(BF)
    ak_ref[...] = (dot(parts, mk_ref[...]) + rows_ref[2:3, :]).astype(BF)


def pre(x, we, wo, bias_row, gqk, heads):
    seq, model = x.shape
    wide = we.shape[1]
    width = (wide - 128) // 4
    block = min(256, seq)
    ba = np.zeros((256, 2 * width))
    for lane in range(2 * width):
        head = (lane % width) // 64 + (lane // width) * heads
        ba[head, lane] = ba[128 + head, lane] = 1.0
    g64 = np.kron(np.eye(width // 64), np.full((64, 64), 1 / 64))
    tri = np.tril(np.ones((block, block)))
    mq, mk = np.zeros((384, 128)), np.zeros((384, 128))
    ones_q, ones_k = np.zeros((1, 128)), np.zeros((1, 128))
    for head in range(heads):
        for piece in range(3):
            mq[128 * piece + 2 * heads + head, 6 * head + piece] = 1.0
            mk[128 * piece + 2 * heads + head, 6 * head + 3 + piece] = -1.0
            ones_q[0, 6 * head + 3 + piece] = 1.0
            ones_k[0, 6 * head + piece] = 1.0
    rows = jnp.concatenate([bias_row, const(ones_q, F32), const(ones_k, F32), jnp.zeros((5, 128), F32)], 0)

    def row(cols):
        return pl.BlockSpec((block, cols), lambda i: (i, 0))

    def shape(cols, dtype):
        return jax.ShapeDtypeStruct((seq, cols), dtype)

    return pl.pallas_call(
        functools.partial(pre_kernel, heads),
        grid=(seq // block,),
        in_specs=[row(model), full(we.shape), full(wo.shape), full(ba.shape), full(g64.shape), full(tri.shape),
                  full(mq.shape), full(mk.shape), full((8, 128)), full(gqk.shape)],
        out_specs=[row(model), full((8, model))] + [row(width)] * 3 + [row(128)] * 2 + [row(width)] * 5 + [row(128)],
        out_shape=[shape(model, BF), jax.ShapeDtypeStruct((8, model), F32)] + [shape(width, BF)] * 3
        + [shape(128, BF)] * 2 + [shape(width, F32)] + [shape(width, BF)] * 4 + [shape(128, F32)],
        scratch_shapes=[pltpu.VMEM((8, model), F32), pltpu.VMEM((8, width), F32), pltpu.VMEM((8, width), F32),
                        pltpu.VMEM((8, 128), F32)],
        compiler_params=params(),
        cost_estimate=pl.CostEstimate(flops=2 * seq * model * wide, bytes_accessed=30_000_000, transcendentals=0),
        name="pre",
    )(x, we, wo, const(ba), const(g64), const(tri), const(mq), const(mk), rows, gqk)


def fwd_kernel(chunk, block, q_ref, aq_ref, k_ref, ak_ref, v_ref, og_ref, *refs):
    u_ref, att_ref, li_ref = refs[-3:]
    pair = pl.program_id(0)
    q, aq = q_ref[...], aq_ref[...]
    lane = lanes(q.shape)
    ones = jnp.ones((block, 128), BF)
    out = []
    for side in range(2):
        head = 2 * pair + side
        mine = (lane >= 64 * side) & (lane < 64 * side + 64)
        aug = (lane >= 6 * head) & (lane < 6 * head + 6)
        zero = jnp.zeros_like(q)
        qa = jnp.concatenate([jnp.where(mine, q, zero), jnp.where(aug, aq, zero)], 1)
        acc = jnp.zeros((block, 256), F32)
        for j in range(chunk + 1):
            at = slice(j * block, (j + 1) * block)
            e = jnp.exp(dot(qa, jnp.concatenate([k_ref[at, :], ak_ref[at, :]], 1), NT))
            if j == chunk:
                e = jnp.where(rows_of(e.shape) >= lanes(e.shape), e, 0.0)
            acc = acc + dot(e.astype(BF), jnp.concatenate([v_ref[at, :], ones], 1))
        out.append(acc)
    low = lane < 64
    total = jnp.where(low, out[0][:, 128:], out[1][:, 128:])
    inverse = 1.0 / total
    att = jnp.where(low, out[0][:, :128], out[1][:, :128]) * inverse
    u_ref[...] = (att * og_ref[...]).astype(BF)
    att_ref[...] = att
    li_ref[...] = inverse


def attend(chunk, block, q8, aq, kn, ak, vl, og, kept):
    seq, width = q8.shape
    keys = (chunk + 1) * block
    grid = (width // 128,)
    mine = pl.BlockSpec((block, 128), lambda p: (chunk, p))
    other = pl.BlockSpec((keys, 128), lambda p: (0, p))
    return pl.pallas_call(
        functools.partial(fwd_kernel, chunk, block),
        grid=grid,
        in_specs=[mine, pl.BlockSpec((block, 128), lambda p: (chunk, 0)), other,
                  pl.BlockSpec((keys, 128), lambda p: (0, 0)), other, mine] + [ANY] * len(kept),
        out_specs=[pl.BlockSpec((block, 128), lambda p: (0, p)), mine, mine],
        out_shape=[jax.ShapeDtypeStruct((block, width), BF)] + [jax.ShapeDtypeStruct((seq, width), F32)] * 2,
        input_output_aliases={6 + i: 1 + i for i in range(len(kept))},
        compiler_params=params(),
        cost_estimate=pl.CostEstimate(flops=2 * 2 * block * keys * 256 * width // 64, bytes_accessed=5_000_000,
                                      transcendentals=block * keys * width // 64),
        name="attend",
    )(q8, aq, kn, ak, vl, og, *kept)


def ffn_kernel(
    count, chunk, block, step_rows, own, at_ref, x_ref, cot_ref, gain_ref, oe_ref, oo_ref, fe_ref, fo_ref, *refs
):
    us, outs = refs[:count], refs[-8:]
    h2_ref, hid_ref, dgu_ref, res_ref, uc_ref, part_ref, du_ref, gmid_ref = outs
    half = oe_ref.shape[0]
    hidden = hid_ref.shape[1]
    u = jnp.concatenate([r[...] for r in us], 1)
    uc_ref[...] = u
    x = x_ref[...].astype(F32)
    cot = cot_ref[...]
    y1 = x + jnp.concatenate([dot(u, oe_ref[...], NT), dot(u, oo_ref[...], NT)], 1)
    factor = lax.rsqrt(jnp.mean(y1 * y1, -1, keepdims=True) + EPS)
    n = y1 * factor
    gain = gain_ref[1:2, :]
    h2 = (n * gain).astype(BF)
    h2_ref[...] = h2
    gu = dot(h2[:, :half], fe_ref[:, : 2 * hidden]) + dot(h2[:, half:], fo_ref[:, : 2 * hidden])
    g, up = gu[:, :hidden], gu[:, hidden:]
    sg = jax.nn.sigmoid(g)
    act = g * sg
    hid = (act * up).astype(BF)
    hid_ref[...] = hid
    dhid = dot(cot[:, :half], fe_ref[:, 2 * hidden :]) + dot(cot[:, half:], fo_ref[:, 2 * hidden :])
    dg = dhid * up * sg * (1.0 + g * (1.0 - sg))
    dgu = jnp.concatenate([dg.astype(BF), (dhid * act).astype(BF)], 1)
    dgu_ref[...] = dgu
    part = jnp.concatenate([dot(hid, fe_ref[:, 2 * hidden :], NT), dot(hid, fo_ref[:, 2 * hidden :], NT)], 1)
    token = chunk * block + pl.program_id(0) * step_rows + rows_of((step_rows, 1))
    owned = (token >= at_ref[0] * own) & (token < (at_ref[0] + 1) * own)
    part_ref[...] = (part + jnp.where(owned, y1, 0.0)).astype(BF)
    dh2 = jnp.concatenate([dot(dgu, fe_ref[:, : 2 * hidden], NT), dot(dgu, fo_ref[:, : 2 * hidden], NT)], 1)
    gmid = jnp.sum(dh2 * n, 0, keepdims=True)

    @pl.when(pl.program_id(0) == 0)
    def _():
        gmid_ref[...] = jnp.zeros_like(gmid_ref)

    gmid_ref[0:1, :] += gmid
    wd = gain * dh2
    res = factor * (wd - n * jnp.mean(wd * n, -1, keepdims=True))
    res = jnp.where(at_ref[0] == 0, res + cot.astype(F32), res).astype(BF)
    res_ref[...] = res
    du_ref[...] = (dot(res[:, :half], oe_ref[...]) + dot(res[:, half:], oo_ref[...])).astype(BF)


def feed(chunk, block, own, place, x, cot, gains, oe, oo, fe, fo, us, kept):
    seq, model = x.shape
    hidden = fe.shape[1] // 3
    count = len(us)
    width = us[0].shape[1]
    step_rows = min(256, block)
    per = block // step_rows

    def mine(cols):
        return pl.BlockSpec((step_rows, cols), lambda i: (chunk * per + i, 0))

    def local(cols):
        return pl.BlockSpec((step_rows, cols), lambda i: (i, 0))

    kept_cols = [model, hidden, 2 * hidden, model, count * width, model]
    return pl.pallas_call(
        functools.partial(ffn_kernel, count, chunk, block, step_rows, own),
        grid=(per,),
        in_specs=[SMEM, mine(model), mine(model), full(gains.shape), full(oe.shape), full(oo.shape), full(fe.shape),
                  full(fo.shape)] + [local(width)] * count + [ANY] * len(kept),
        out_specs=[mine(c) for c in kept_cols] + [local(count * width), full((8, model))],
        out_shape=[jax.ShapeDtypeStruct((seq, c), BF) for c in kept_cols]
        + [jax.ShapeDtypeStruct((block, count * width), BF), jax.ShapeDtypeStruct((8, model), F32)],
        input_output_aliases={8 + count + i: i for i in range(len(kept))},
        compiler_params=params(),
        cost_estimate=pl.CostEstimate(flops=2 * block * model * (2 * count * width + 6 * hidden),
                                      bytes_accessed=30_000_000, transcendentals=0),
        name="feed",
    )(place, x, cot, gains, oe, oo, fe, fo, *us, *kept)


def bwd_kernel(
    heads, block, q_ref, aq_ref, k_ref, ak_ref, v_ref, og_ref, att_ref, li_ref, du_ref, ms_ref,
    dq_ref, dk_ref, dv_ref, dc_ref, da_s, ad_s,
):
    pair = pl.program_id(0)
    seq = q_ref.shape[0]
    count = seq // block
    lane = lanes((block, 128))
    zero = jnp.zeros((block, 128), BF)
    ones = jnp.ones((block, 128), BF)
    third = lane - 3 * (lane // 3)
    for i in range(count):
        at = slice(i * block, (i + 1) * block)
        da = (du_ref[at, :].astype(F32) * og_ref[at, :] * li_ref[at, :]).astype(BF)
        da_s[at, :] = da
        delta = dot(jnp.concatenate(split2(da.astype(F32) * att_ref[at, :]), 1), ms_ref[...])
        hi, mid, rest = split3(-delta)
        ad_s[at, :] = jnp.where(third == 0, hi, jnp.where(third == 1, mid, rest))
    dk_ref[...] = jnp.zeros_like(dk_ref)
    dv_ref[...] = jnp.zeros_like(dv_ref)

    @pl.when(pair == 0)
    def _():
        dc_ref[...] = jnp.zeros_like(dc_ref)

    vone = jnp.where(lane < 6, ones, zero)
    for i in range(count):
        at = slice(i * block, (i + 1) * block)
        q, aq, da, ad = q_ref[at, :], aq_ref[at, :], da_s[at, :], ad_s[at, :]
        dq = []
        for side in range(2):
            head = 2 * pair + side
            mine = (lane >= 64 * side) & (lane < 64 * side + 64)
            aug = (lane >= 6 * head) & (lane < 6 * head + 6)
            column = lane == 2 * heads + head
            qh = jnp.where(mine, q, zero)
            qa = jnp.concatenate([qh, jnp.where(aug, aq, zero)], 1)
            qo = jnp.concatenate([qh, ones], 1)
            dah = jnp.where(mine, da, zero)
            daa = jnp.concatenate([dah, jnp.where((lane >= 3 * side) & (lane < 3 * side + 3), ad, zero)], 1)
            acc = jnp.zeros((block, 256), F32)
            for j in range(i + 1):
                to = slice(j * block, (j + 1) * block)
                k = k_ref[to, :]
                e = jnp.exp(dot(jnp.concatenate([k, ak_ref[to, :]], 1), qa, NT))
                if j == i:
                    e = jnp.where(rows_of(e.shape) <= lanes(e.shape), e, 0.0)
                dv_ref[to, :] += dot(e.astype(BF), dah)
                ds = (e * dot(jnp.concatenate([v_ref[to, :], vone], 1), daa, NT)).astype(BF)
                dk = dot(ds, qo)
                dk_ref[to, :] += dk[:, :128]
                dc_ref[to, :] -= jnp.where(column, dk[:, 128:], 0.0)
                acc = acc + dot(ds, jnp.concatenate([k, ones], 1), TN)
            dq.append(acc[:, :128])
            dc_ref[at, :] += jnp.where(column, acc[:, 128:], 0.0)
        dq_ref[at, :] = jnp.where(lane < 64, dq[0], dq[1]) * 0.125


def attend_back(block, heads, q8, aq, kn, ak, vl, og, att, li, du):
    seq, width = q8.shape
    ms = np.zeros((256, 128))
    for lane in range(256):
        ms[lane, 3 * ((lane % 128) // 64) : 3 * ((lane % 128) // 64) + 3] = 1.0
    pair = pl.BlockSpec((seq, 128), lambda p: (0, p))
    one = pl.BlockSpec((seq, 128), lambda p: (0, 0))
    return pl.pallas_call(
        functools.partial(bwd_kernel, heads, block),
        grid=(width // 128,),
        in_specs=[pair, one, pair, one, pair, pair, pair, pair, pair, full((256, 128))],
        out_specs=[pair, pair, pair, one],
        out_shape=[jax.ShapeDtypeStruct((seq, width), F32)] * 3 + [jax.ShapeDtypeStruct((seq, 128), F32)],
        scratch_shapes=[pltpu.VMEM((seq, 128), BF), pltpu.VMEM((seq, 128), BF)],
        compiler_params=params(),
        cost_estimate=pl.CostEstimate(flops=5 * seq * seq * 256 * width // 64, bytes_accessed=25_000_000,
                                      transcendentals=seq * seq * width // 128),
        name="attend_back",
    )(q8, aq, kn, ak, vl, og, att, li, du, const(ms))


def post_kernel(
    heads, dq_ref, dk_ref, dv_ref, dc_ref, q_ref, ks_ref, kd_ref, vd_ref, lg_ref, du_ref, att_ref, og_ref, x_ref,
    res_ref, gain_ref, we_ref, wo_ref, ba_ref, g64_ref, tri_ref, ms_ref, rows_ref, gqk_ref,
    dp_ref, gt_ref, g0_ref, gq_ref, gb_ref, carry_k, carry_v, carry_c,
):
    step = pl.program_id(0)
    half = we_ref.shape[0]
    width = dq_ref.shape[1]
    rows = dq_ref.shape[0]

    @pl.when(step == 0)
    def _():
        carry_k[...] = jnp.zeros_like(carry_k)
        carry_v[...] = jnp.zeros_like(carry_v)
        carry_c[...] = jnp.zeros_like(carry_c)
        g0_ref[...] = jnp.zeros_like(g0_ref)
        gq_ref[...] = jnp.zeros_like(gq_ref)
        gb_ref[...] = jnp.zeros_like(gb_ref)

    def norm_back(raw, gain, grad):
        r = lax.rsqrt(dot((raw * raw).astype(BF), g64_ref[...]) + EPS)
        n = raw * r
        wd = grad * gain
        return r * (wd - n * dot((wd * n).astype(BF), g64_ref[...])), jnp.sum(grad * n, 0, keepdims=True)

    dq, gq = norm_back(q_ref[...].astype(F32), gqk_ref[0:1, :], dq_ref[...])
    dks, gk = norm_back(ks_ref[...].astype(F32), gqk_ref[1:2, :], dk_ref[...])
    gq_ref[0:1, :] += gq
    gq_ref[1:2, :] += gk
    dvs = dv_ref[...]
    logits = lg_ref[...]
    sg = jax.nn.sigmoid(logits)
    mix = dot(jnp.concatenate(split2(sg), 1), ba_ref[...])
    end = rows_of(dks.shape) == rows - 1

    def shift_back(grad, part, carry):
        w = part * grad
        later = jnp.where(end, carry[0:1, :], pltpu.roll(w, rows - 1, 0))
        carry[0:1, :] = w[0:1, :]
        return grad - w + later

    dk = shift_back(dks, mix[:, :width], carry_k)
    dv = shift_back(dvs, mix[:, width:], carry_v)
    terms = jnp.concatenate([dks * kd_ref[...].astype(F32), dvs * vd_ref[...].astype(F32)], 1)
    hi, rest = split2(terms)
    dmix = dot(hi, ms_ref[...]) + dot(rest, ms_ref[...])
    sums = dot(tri_ref[...], jnp.concatenate(split3(dc_ref[...]), 1))
    dls = sums[:, :128] + sums[:, 128:256] + sums[:, 256:] + carry_c[0:1, :]
    carry_c[0:1, :] = dls[0:1, :]
    lane = lanes(logits.shape)
    dz = dls * jax.nn.sigmoid(-(logits + rows_ref[0:1, :]))
    dgl = jnp.where(lane < 2 * heads, dmix * sg * (1.0 - sg), jnp.where(lane < 3 * heads, dz, 0.0))
    gb_ref[0:1, :] += jnp.sum(dgl, 0, keepdims=True)
    og = og_ref[...]
    do = du_ref[...].astype(F32) * att_ref[...] * og * (1.0 - og)
    dp = jnp.concatenate([dq.astype(BF), dk.astype(BF), dv.astype(BF), do.astype(BF), dgl.astype(BF)], 1)
    dp_ref[...] = dp
    dhn = jnp.concatenate([dot(dp, we_ref[...], NT), dot(dp, wo_ref[...], NT)], 1)
    x = x_ref[...].astype(F32)
    factor = lax.rsqrt(jnp.mean(x * x, -1, keepdims=True) + EPS)
    n = x * factor
    g0_ref[0:1, :] += jnp.sum(dhn * n, 0, keepdims=True)
    wd = dhn * gain_ref[0:1, :]
    back = factor * (wd - n * jnp.mean(wd * n, -1, keepdims=True))
    gt_ref[...] = (back + res_ref[...].astype(F32)).astype(BF)


def post(heads, dq, dk, dv, dc, q, ks, kd, vd, lg, du, att, og, x, res, gains, we, wo, bias_row, gqk):
    seq, width = dq.shape
    model = x.shape[1]
    wide = we.shape[1]
    block = min(256, seq)
    count = seq // block
    ba = np.zeros((256, 2 * width))
    ms = np.zeros((2 * width, 128))
    for lane in range(2 * width):
        head = (lane % width) // 64 + (lane // width) * heads
        ba[head, lane] = ba[128 + head, lane] = 1.0
        ms[lane, head] = 1.0
    g64 = np.kron(np.eye(width // 64), np.full((64, 64), 1 / 64))
    tri = np.triu(np.ones((block, block)))
    rows = jnp.concatenate([bias_row, jnp.zeros((7, 128), F32)], 0)

    def row(cols):
        return pl.BlockSpec((block, cols), lambda i: (count - 1 - i, 0))

    return pl.pallas_call(
        functools.partial(post_kernel, heads),
        grid=(count,),
        in_specs=[row(width)] * 3 + [row(128)] + [row(width)] * 4 + [row(128)] + [row(width)] * 3 + [row(model)] * 2
        + [full(gains.shape), full(we.shape), full(wo.shape), full(ba.shape), full(g64.shape), full(tri.shape),
           full(ms.shape), full((8, 128)), full(gqk.shape)],
        out_specs=[row(wide), row(model), full((8, model)), full((8, width)), full((8, 128))],
        out_shape=[jax.ShapeDtypeStruct((seq, wide), BF), jax.ShapeDtypeStruct((seq, model), BF),
                   jax.ShapeDtypeStruct((8, model), F32), jax.ShapeDtypeStruct((8, width), F32),
                   jax.ShapeDtypeStruct((8, 128), F32)],
        scratch_shapes=[pltpu.VMEM((8, width), F32), pltpu.VMEM((8, width), F32), pltpu.VMEM((8, 128), F32)],
        compiler_params=params(),
        cost_estimate=pl.CostEstimate(flops=2 * seq * model * wide, bytes_accessed=40_000_000, transcendentals=0),
        name="post",
    )(dq, dk, dv, dc, q, ks, kd, vd, lg, du, att, og, x, res, gains, we, wo, const(ba), const(g64), const(tri),
      const(ms), rows, gqk)


def swap(value, axis, bit):
    size = lax.axis_size(axis)
    return lax.ppermute(value, axis, [(i, i ^ bit) for i in range(size)])


def turn(value):
    size = lax.axis_size("tp")
    return lax.ppermute(value, "tp", [(i, (i + 1) % size) for i in range(size)])


def add(a, b):
    return (a.astype(F32) + b.astype(F32)).astype(BF)


def high_bits(size):
    bits, bit = [], 2
    while bit < size:
        bits.append(bit)
        bit *= 2
    return bits


def dp_gather(shard):
    size = lax.axis_size("dp")
    pieces = {0: shard}
    if size == 8:
        half = shard.shape[0] // 2
        pieces[2] = swap(shard, "dp", 2)
        pieces[4] = swap(shard, "dp", 4)
        pieces[6] = jnp.concatenate(
            [swap(pieces[2][:half], "dp", 4), swap(pieces[4][half:], "dp", 2)], 0
        )
    else:
        for bit in high_bits(size):
            pieces.update({r | bit: swap(p, "dp", bit) for r, p in list(pieces.items())})
    even = jnp.concatenate([pieces[r] for r in range(0, size, 2)], 0)
    return even, swap(even, "dp", 1)


def dp_scatter(even, odd):
    size = lax.axis_size("dp")
    total = add(even, swap(odd, "dp", 1))
    rows = total.shape[0] // (size // 2)
    pieces = {r: total[rows * (r // 2) : rows * (r // 2 + 1)] for r in range(0, size, 2)}
    if size == 8:
        half = rows // 2
        from_x = swap(pieces[6][:half], "dp", 2)
        from_y = swap(pieces[6][half:], "dp", 4)
        to_y = jnp.concatenate([add(pieces[4][:half], from_x), pieces[4][half:]], 0)
        to_x = jnp.concatenate([pieces[2][:half], add(pieces[2][half:], from_y)], 0)
        got_x, got_y = swap(to_x, "dp", 2), swap(to_y, "dp", 4)
        return pieces[0].astype(F32) + got_x.astype(F32) + got_y.astype(F32)
    for bit in reversed(high_bits(size)):
        got = {r: swap(pieces[r], "dp", bit) for r in pieces if r & bit}
        pieces = {r: add(p, got[r | bit]) for r, p in pieces.items() if not r & bit}
    return pieces[0].astype(F32)


def ring_gather(value):
    out = [value]
    for _ in range(lax.axis_size("tp") - 1):
        out.append(turn(out[-1]))
    return out


def ring_scatter_parts(parts):
    acc = parts[1]
    for part in parts[2:]:
        acc = add(turn(acc), part)
    return turn(acc)


def pad_to(value, size, axis):
    extra = size - value.shape[axis]
    if not extra:
        return value
    return jnp.pad(value, [(0, extra if a == axis else 0) for a in range(value.ndim)])


def shards(
    tokens, attn_in, head_gates, out_proj, norm_gains, qk_gains, forget_bias, gate_up, down_proj, carried_offset,
    reset_flag, cotangent,
):
    dp, tp = lax.axis_size("dp"), lax.axis_size("tp")
    me_d, me_t = lax.axis_index("dp"), lax.axis_index("tp")
    _, seq, model = tokens.shape
    own = seq // tp
    cut = attn_in.shape[1]
    width_real = attn_in.shape[2]
    heads_real = head_gates.shape[2]
    heads = heads_real + heads_real % 2
    width = 64 * heads
    hidden = gate_up.shape[2]
    block = 512 if seq % 512 == 0 else seq
    chunks = seq // block

    attn_rows = jnp.transpose(pad_to(attn_in, width, 2), (1, 0, 2)).reshape(cut, 4 * width)
    gate_rows = jnp.transpose(pad_to(head_gates, heads, 2), (1, 0, 2)).reshape(cut, 3 * heads)
    gate_rows = pad_to(jnp.concatenate([gate_rows, jnp.transpose(norm_gains)], 1), 128, 1)
    we, wo = dp_gather(jnp.concatenate([attn_rows, gate_rows], 1))
    out_rows = jnp.concatenate(ring_gather(pad_to(jnp.transpose(out_proj), width, 1)), 1)
    ffn_rows = jnp.concatenate([gate_up[0], gate_up[1], jnp.transpose(down_proj)], 1)
    we, wo, out_rows = lax.optimization_barrier((we, wo, out_rows))
    oe, oo = dp_gather(out_rows)
    oe, oo, ffn_rows = lax.optimization_barrier((oe, oo, ffn_rows))
    fe, fo = dp_gather(ffn_rows)

    order = [r for r in range(0, dp, 2)] + [r for r in range(1, dp, 2)]
    source = jnp.concatenate([(me_d ^ r) * cut + jnp.arange(cut, dtype=jnp.int32) for r in order])
    place = (jnp.arange(model, dtype=jnp.int32)[:, None] == source[None, :]).astype(BF)
    x = dot(tokens[0], place).astype(BF)
    cot = dot(cotangent[0], place).astype(BF)

    bias = lax.dynamic_slice_in_dim(forget_bias.astype(F32), me_t * heads_real, heads_real, 0)
    offset = lax.dynamic_slice_in_dim(carried_offset[0], me_t * heads_real, heads_real, 0)
    bias = bias + (1 - reset_flag[0]).astype(F32) * offset
    bias_row = jnp.pad(bias, (2 * heads, 128 - 2 * heads - heads_real))[None, :]
    gqk = pad_to(jnp.tile(qk_gains.astype(F32), (1, heads)), 8, 0)

    hn, gains, q8, kn, vl, aq, ak, og, q, ks, kd, vd, lg = pre(x, we, wo, bias_row, gqk, heads)
    at = me_t.astype(jnp.int32)[None]
    kept_att, kept_ffn, gmids, dus = (), (), [], []
    for chunk in range(chunks):
        u, *kept_att = attend(chunk, block, q8, aq, kn, ak, vl, og, kept_att)
        *kept_ffn, du, gmid = feed(chunk, block, own, at, x, cot, gains, oe, oo, fe, fo, ring_gather(u), kept_ffn)
        parts = [du[:, s * width : (s + 1) * width] for s in range(tp)]
        dus.append(add(ring_scatter_parts(parts), parts[0]))
        gmids.append(gmid[0:1])
    att, li = kept_att
    h2, hid, dgu, res, uc, part = kept_ffn
    du = jnp.concatenate(dus, 0)

    part, du = lax.optimization_barrier((part, du))

    def token_parts(values):
        return [
            lax.dynamic_slice_in_dim(values, lax.rem(me_t - s + tp, tp) * own, own, 0) for s in range(tp)
        ]

    parts = token_parts(part)
    result = dot(add(ring_scatter_parts(parts), parts[0]), place, NT).astype(BF)

    mid = model // 2

    def weight_grad(left, right):
        return dp_scatter(dot(left[:, :mid], right, TN).astype(BF), dot(left[:, mid:], right, TN).astype(BF))

    grad_down = weight_grad(cot, hid)
    grad_gu = weight_grad(h2, dgu)
    grad_out = weight_grad(res, uc)

    dq, dk, dv, dc = attend_back(block, heads, q8, aq, kn, ak, vl, og, att, li, du)
    dp_all, gt, g0, gq, gb = post(
        heads, dq, dk, dv, dc, q, ks, kd, vd, lg, du, att, og, x, res, gains, we, wo, bias_row, gqk
    )
    parts = token_parts(gt)
    grad_tokens = dot(parts[0], place, NT) + dot(ring_scatter_parts(parts), place, NT)
    grad_attn = weight_grad(hn, dp_all)

    out_low = grad_out.astype(BF)
    out_parts = [out_low[:, s * width : (s + 1) * width] for s in range(tp)]
    grad_out_own = out_parts[0].astype(F32) + ring_scatter_parts(out_parts).astype(F32)

    norm_rows = jnp.concatenate([g0[0:1], sum(gmids)], 0)
    norm_rows = sum(dot(part, place, NT) for part in split3(norm_rows))
    gq = gq[0:2].reshape(2, heads, 64).sum(1)
    gb = lax.dynamic_update_slice_in_dim(
        jnp.zeros(forget_bias.shape, F32), gb[0, 2 * heads : 2 * heads + heads_real], me_t * heads_real, 0
    )
    sizes = [2 * model, 2 * 64, forget_bias.shape[0]]
    flat = jnp.concatenate([norm_rows.reshape(-1), gq.reshape(-1), gb])
    flat = jnp.pad(flat, (0, -flat.shape[0] % 1024)).reshape(-1, 128)
    for axis, size in (("tp", tp), ("dp", dp)):
        bit = 1
        while bit < size:
            flat = flat + swap(flat, axis, bit)
            bit *= 2
    flat = flat.reshape(-1)
    norm_grad = flat[: sizes[0]].reshape(2, model)
    qk_grad = flat[sizes[0] : sizes[0] + sizes[1]].reshape(2, 64)
    bias_grad = flat[sizes[0] + sizes[1] : sum(sizes)]

    grad_attn_in = jnp.transpose(grad_attn[:, : 4 * width].reshape(cut, 4, width)[:, :, :width_real], (1, 0, 2))
    grad_gates = grad_attn[:, 4 * width : 4 * width + 3 * heads].reshape(cut, 3, heads)[:, :, :heads_real]
    return (
        result[None],
        grad_tokens[None],
        grad_attn_in,
        jnp.transpose(grad_gates, (1, 0, 2)),
        jnp.transpose(grad_out_own[:, :width_real]),
        jnp.stack([grad_gu[:, :hidden], grad_gu[:, hidden:]]),
        jnp.transpose(grad_down),
        norm_grad,
        qk_grad,
        bias_grad,
    )


def solution(mesh):
    return jax.shard_map(
        shards,
        mesh=mesh,
        in_specs=(
            P("dp", None, None), P(None, "dp", "tp"), P(None, "dp", "tp"), P("tp", "dp"), P(None, "dp"), P(), P(),
            P(None, "dp", "tp"), P("tp", "dp"), P("dp", None), P("dp"), P("dp", None, None),
        ),
        out_specs=(
            P("dp", "tp", None), P("dp", "tp", None), P(None, "dp", "tp"), P(None, "dp", "tp"), P("tp", "dp"),
            P(None, "dp", "tp"), P("tp", "dp"), P(), P(), P(),
        ),
        check_vma=False,
    )
```

```python
import functools

import jax
import jax.numpy as jnp
import numpy as np
from jax import lax
from jax.experimental import pallas as pl
from jax.experimental.pallas import tpu as pltpu
from jax.sharding import PartitionSpec as P

EPS = 1e-06
BF = jnp.bfloat16
F32 = jnp.float32
VMEM_LIMIT = 58 * 1024 * 1024
NT = (((1,), (1,)), ((), ()))
TN = (((0,), (0,)), ((), ()))


COST = pl.CostEstimate(flops=1, bytes_accessed=1, transcendentals=0)


def dot(a, b, dims=(((1,), (0,)), ((), ()))):
    return lax.dot_general(a, b, dims, preferred_element_type=F32)


def params():
    return pltpu.CompilerParams(vmem_limit_bytes=VMEM_LIMIT)


def split2(v):
    hi = v.astype(BF)
    return hi, (v - hi.astype(F32)).astype(BF)


def split3(v):
    hi = v.astype(BF)
    rest = v - hi.astype(F32)
    mid = rest.astype(BF)
    return hi, mid, (rest - mid.astype(F32)).astype(BF)


def lanes(shape):
    return lax.broadcasted_iota(jnp.int32, shape, len(shape) - 1)


def rows_of(shape):
    return lax.broadcasted_iota(jnp.int32, shape, 0)


def const(array, dtype=BF):
    return jnp.asarray(array.astype(np.float32), dtype)


def full(shape):
    return pl.BlockSpec(shape, lambda *_: tuple(0 for _ in shape), pipeline_mode=pl.Buffered(1))


ANY = pl.BlockSpec(memory_space=pl.ANY)
SMEM = pl.BlockSpec(memory_space=pltpu.SMEM)


def pre_kernel(
    heads, spots, me_ref, x_ref, ba_ref, g64_ref, tri_ref, mq_ref, mk_ref, rows_ref, gqk_ref, *refs,
):
    pieces, refs = refs[: len(spots)], refs[len(spots) :]
    (hn_ref, w_ref, gain_ref, q8_ref, kn_ref, vl_ref, aq_ref, ak_ref, og_ref, q_ref, ks_ref, kd_ref, vd_ref, lg_ref,
     gain_s, carry_k, carry_v, carry_c, sems) = refs
    step = pl.program_id(0)
    width = q8_ref.shape[1]
    wide = 4 * width

    @pl.when(step == 0)
    def _():
        copies = []
        for i, (far, start, count, cut) in enumerate(spots):
            row = pl.multiple_of((me_ref[0] ^ far) * cut + start, 16)
            copies.append(pltpu.make_async_copy(pieces[i], w_ref.at[pl.ds(row, count), :], sems.at[i]))
        for copy in copies:
            copy.start()
        for copy in copies:
            copy.wait()
        pick = (lanes((8, 128)) == 3 * heads + rows_of((8, 128))).astype(F32)
        pick = jnp.where(rows_of((8, 128)) < 2, pick, 0.0).astype(BF)
        gain_s[...] = dot(pick, w_ref[:, wide:], NT)
        carry_k[...] = jnp.zeros_like(carry_k)
        carry_v[...] = jnp.zeros_like(carry_v)
        carry_c[...] = jnp.zeros_like(carry_c)
        gain_ref[...] = gain_s[...]

    x = x_ref[...].astype(F32)
    factor = lax.rsqrt(jnp.mean(x * x, -1, keepdims=True) + EPS)
    hn = (x * factor * gain_s[0:1, :]).astype(BF)
    hn_ref[...] = hn
    proj = dot(hn, w_ref[...])
    q = proj[:, :width]
    k = proj[:, width : 2 * width]
    v = proj[:, 2 * width : 3 * width]
    og_ref[...] = jax.nn.sigmoid(proj[:, 3 * width : wide])
    logits = proj[:, wide:]
    lg_ref[...] = logits
    mix = dot(jnp.concatenate(split2(jax.nn.sigmoid(logits)), 1), ba_ref[...])
    first = rows_of(k.shape) == 0
    kd = jnp.where(first, carry_k[0:1, :], pltpu.roll(k, 1, 0)) - k
    vd = jnp.where(first, carry_v[0:1, :], pltpu.roll(v, 1, 0)) - v
    last = k.shape[0] - 1
    carry_k[0:1, :] = k[last:, :]
    carry_v[0:1, :] = v[last:, :]
    ks = k + mix[:, :width] * kd
    vl_ref[...] = (v + mix[:, width:] * vd).astype(BF)
    q_ref[...] = q.astype(BF)
    ks_ref[...] = ks.astype(BF)
    kd_ref[...] = kd.astype(BF)
    vd_ref[...] = vd.astype(BF)
    rq = lax.rsqrt(dot((q * q).astype(BF), g64_ref[...]) + EPS)
    rk = lax.rsqrt(dot((ks * ks).astype(BF), g64_ref[...]) + EPS)
    q8_ref[...] = ((q * rq * gqk_ref[0:1, :]).astype(BF).astype(F32) * 0.125).astype(BF)
    kn_ref[...] = (ks * rk * gqk_ref[1:2, :]).astype(BF)
    z = logits + rows_ref[0:1, :]
    ls = jnp.minimum(z, 0.0) - jnp.log1p(jnp.exp(-jnp.abs(z)))
    sums = dot(tri_ref[...], jnp.concatenate(split3(ls), 1))
    cum = sums[:, :128] + sums[:, 128:256] + sums[:, 256:] + carry_c[0:1, :]
    carry_c[0:1, :] = cum[last:, :]
    parts = jnp.concatenate(split3(cum), 1)
    aq_ref[...] = (dot(parts, mq_ref[...]) + rows_ref[1:2, :]).astype(BF)
    ak_ref[...] = (dot(parts, mk_ref[...]) + rows_ref[2:3, :]).astype(BF)


def pre(x, place, pieces, bias_row, gqk, heads):
    seq, model = x.shape
    cut = pieces[0, 0].shape[0]
    spots = [(far, start, p.shape[0], cut) for (far, start), p in sorted(pieces.items())]
    wide = pieces[0, 0].shape[1]
    width = (wide - 128) // 4
    block = min(256, seq)
    ba = np.zeros((256, 2 * width))
    for lane in range(2 * width):
        head = (lane % width) // 64 + (lane // width) * heads
        ba[head, lane] = ba[128 + head, lane] = 1.0
    g64 = np.kron(np.eye(width // 64), np.full((64, 64), 1 / 64))
    tri = np.tril(np.ones((block, block)))
    mq, mk = np.zeros((384, 128)), np.zeros((384, 128))
    ones_q, ones_k = np.zeros((1, 128)), np.zeros((1, 128))
    for head in range(heads):
        for piece in range(3):
            mq[128 * piece + 2 * heads + head, 6 * head + piece] = 1.0
            mk[128 * piece + 2 * heads + head, 6 * head + 3 + piece] = -1.0
            ones_q[0, 6 * head + 3 + piece] = 1.0
            ones_k[0, 6 * head + piece] = 1.0
    rows = jnp.concatenate([bias_row, const(ones_q, F32), const(ones_k, F32), jnp.zeros((5, 128), F32)], 0)

    def row(cols):
        return pl.BlockSpec((block, cols), lambda i: (i, 0))

    def shape(cols, dtype):
        return jax.ShapeDtypeStruct((seq, cols), dtype)

    return pl.pallas_call(
        functools.partial(pre_kernel, heads, spots),
        grid=(seq // block,),
        in_specs=[SMEM, row(model), full(ba.shape), full(g64.shape), full(tri.shape), full(mq.shape), full(mk.shape),
                  full((8, 128)), full(gqk.shape)] + [ANY] * len(spots),
        out_specs=[row(model), full((model, wide)), full((8, model))] + [row(width)] * 3 + [row(128)] * 2 + [row(width)] * 5 + [row(128)],
        out_shape=[shape(model, BF), jax.ShapeDtypeStruct((model, wide), BF), jax.ShapeDtypeStruct((8, model), F32)]
        + [shape(width, BF)] * 3
        + [shape(128, BF)] * 2 + [shape(width, F32)] + [shape(width, BF)] * 4 + [shape(128, F32)],
        scratch_shapes=[pltpu.VMEM((8, model), F32), pltpu.VMEM((8, width), F32), pltpu.VMEM((8, width), F32),
                        pltpu.VMEM((8, 128), F32), pltpu.SemaphoreType.DMA((len(spots),))],
        compiler_params=params(),
        cost_estimate=COST,
        name="pre",
    )(place, x, const(ba), const(g64), const(tri), const(mq), const(mk), rows, gqk,
      *[p for _, p in sorted(pieces.items())])


def fwd_kernel(chunk, block, q_ref, aq_ref, k_ref, ak_ref, v_ref, og_ref, *refs):
    u_ref, att_ref, li_ref = refs[-3:]
    pair = pl.program_id(0)
    q, aq = q_ref[...], aq_ref[...]
    lane = lanes(q.shape)
    ones = jnp.ones((block, 128), BF)
    out = []
    for side in range(2):
        head = 2 * pair + side
        mine = (lane >= 64 * side) & (lane < 64 * side + 64)
        aug = (lane >= 6 * head) & (lane < 6 * head + 6)
        zero = jnp.zeros_like(q)
        qa = jnp.concatenate([jnp.where(mine, q, zero), jnp.where(aug, aq, zero)], 1)
        acc = jnp.zeros((block, 256), F32)
        for j in range(chunk + 1):
            at = slice(j * block, (j + 1) * block)
            e = jnp.exp(dot(qa, jnp.concatenate([k_ref[at, :], ak_ref[at, :]], 1), NT))
            if j == chunk:
                e = jnp.where(rows_of(e.shape) >= lanes(e.shape), e, 0.0)
            acc = acc + dot(e.astype(BF), jnp.concatenate([v_ref[at, :], ones], 1))
        out.append(acc)
    low = lane < 64
    total = jnp.where(low, out[0][:, 128:], out[1][:, 128:])
    inverse = 1.0 / total
    att = jnp.where(low, out[0][:, :128], out[1][:, :128]) * inverse
    u_ref[...] = (att * og_ref[...]).astype(BF)
    att_ref[...] = att
    li_ref[...] = inverse


def attend(chunk, block, q8, aq, kn, ak, vl, og, kept):
    seq, width = q8.shape
    keys = (chunk + 1) * block
    grid = (width // 128,)
    mine = pl.BlockSpec((block, 128), lambda p: (chunk, p))
    other = pl.BlockSpec((keys, 128), lambda p: (0, p))
    return pl.pallas_call(
        functools.partial(fwd_kernel, chunk, block),
        grid=grid,
        in_specs=[mine, pl.BlockSpec((block, 128), lambda p: (chunk, 0)), other,
                  pl.BlockSpec((keys, 128), lambda p: (0, 0)), other, mine] + [ANY] * len(kept),
        out_specs=[pl.BlockSpec((block, 128), lambda p: (0, p)), mine, mine],
        out_shape=[jax.ShapeDtypeStruct((block, width), BF)] + [jax.ShapeDtypeStruct((seq, width), F32)] * 2,
        input_output_aliases={6 + i: 1 + i for i in range(len(kept))},
        compiler_params=params(),
        cost_estimate=COST,
        name="attend",
    )(q8, aq, kn, ak, vl, og, *kept)


def ffn_kernel(
    count, chunk, block, step_rows, own, at_ref, x_ref, cot_ref, gain_ref, o_ref, f_ref, *refs
):
    us, outs = refs[:count], refs[-7 - count :]
    h2_ref, hid_ref, dgu_ref, res_ref, uc_ref, part_ref = outs[:6]
    dus, gmid_ref = outs[6:-1], outs[-1]
    hidden = hid_ref.shape[1]
    u = jnp.concatenate([r[...] for r in us], 1)
    uc_ref[...] = u
    x = x_ref[...].astype(F32)
    cot = cot_ref[...]
    y1 = x + dot(u, o_ref[...], NT)
    factor = lax.rsqrt(jnp.mean(y1 * y1, -1, keepdims=True) + EPS)
    n = y1 * factor
    gain = gain_ref[1:2, :]
    h2 = (n * gain).astype(BF)
    h2_ref[...] = h2
    gu = dot(h2, f_ref[:, : 2 * hidden])
    g, up = gu[:, :hidden], gu[:, hidden:]
    sg = jax.nn.sigmoid(g)
    act = g * sg
    hid = (act * up).astype(BF)
    hid_ref[...] = hid
    dhid = dot(cot, f_ref[:, 2 * hidden :])
    dg = dhid * up * sg * (1.0 + g * (1.0 - sg))
    dgu = jnp.concatenate([dg.astype(BF), (dhid * act).astype(BF)], 1)
    dgu_ref[...] = dgu
    part = dot(hid, f_ref[:, 2 * hidden :], NT)
    token = chunk * block + pl.program_id(0) * step_rows + rows_of((step_rows, 1))
    owned = (token >= at_ref[0] * own) & (token < (at_ref[0] + 1) * own)
    part_ref[...] = (part + jnp.where(owned, y1, 0.0)).astype(BF)
    dh2 = dot(dgu, f_ref[:, : 2 * hidden], NT)
    gmid = jnp.sum(dh2 * n, 0, keepdims=True)

    @pl.when(pl.program_id(0) == 0)
    def _():
        gmid_ref[...] = jnp.zeros_like(gmid_ref)

    gmid_ref[0:1, :] += gmid
    wd = gain * dh2
    res = factor * (wd - n * jnp.mean(wd * n, -1, keepdims=True))
    res = jnp.where(at_ref[0] == 0, res + cot.astype(F32), res).astype(BF)
    res_ref[...] = res
    du = dot(res, o_ref[...]).astype(BF)
    width = du.shape[1] // count
    for s in range(count):
        dus[s][...] = du[:, s * width : (s + 1) * width]


def feed(chunk, block, own, place, x, cot, gains, o, f, us, kept):
    seq, model = x.shape
    hidden = f.shape[1] // 3
    count = len(us)
    width = us[0].shape[1]
    step_rows = min(256, block)
    per = block // step_rows

    def mine(cols):
        return pl.BlockSpec((step_rows, cols), lambda i: (chunk * per + i, 0))

    def local(cols):
        return pl.BlockSpec((step_rows, cols), lambda i: (i, 0))

    kept_cols = [model, hidden, 2 * hidden, model, count * width, model]
    return pl.pallas_call(
        functools.partial(ffn_kernel, count, chunk, block, step_rows, own),
        grid=(per,),
        in_specs=[SMEM, mine(model), mine(model), full(gains.shape), full(o.shape), full(f.shape)]
        + [local(width)] * count + [ANY] * len(kept),
        out_specs=[mine(c) for c in kept_cols] + [local(width)] * count + [full((8, model))],
        out_shape=[jax.ShapeDtypeStruct((seq, c), BF) for c in kept_cols]
        + [jax.ShapeDtypeStruct((block, width), BF)] * count + [jax.ShapeDtypeStruct((8, model), F32)],
        input_output_aliases={6 + count + i: i for i in range(len(kept))},
        compiler_params=params(),
        cost_estimate=COST,
        name="feed",
    )(place, x, cot, gains, o, f, *us, *kept)


def bwd_kernel(
    pair, heads, block, q_ref, aq_ref, k_ref, ak_ref, v_ref, og_ref, att_ref, li_ref, du_ref, ms_ref,
    dq_ref, dk_ref, dv_ref, dc_ref, da_s, ad_s,
):
    seq = q_ref.shape[0]
    count = seq // block
    lane = lanes((block, 128))
    zero = jnp.zeros((block, 128), BF)
    ones = jnp.ones((block, 128), BF)
    third = lane - 3 * (lane // 3)
    for i in range(count):
        at = slice(i * block, (i + 1) * block)
        da = (du_ref[at, :].astype(F32) * og_ref[at, :] * li_ref[at, :]).astype(BF)
        da_s[at, :] = da
        delta = dot(jnp.concatenate(split2(da.astype(F32) * att_ref[at, :]), 1), ms_ref[...])
        hi, mid, rest = split3(-delta)
        ad_s[at, :] = jnp.where(third == 0, hi, jnp.where(third == 1, mid, rest))
    dk_ref[...] = jnp.zeros_like(dk_ref)
    dv_ref[...] = jnp.zeros_like(dv_ref)
    dc_ref[...] = jnp.zeros_like(dc_ref)

    vone = jnp.where(lane < 6, ones, zero)
    for i in range(count):
        at = slice(i * block, (i + 1) * block)
        q, aq, da, ad = q_ref[at, :], aq_ref[at, :], da_s[at, :], ad_s[at, :]
        dq = []
        for side in range(2):
            head = 2 * pair + side
            mine = (lane >= 64 * side) & (lane < 64 * side + 64)
            aug = (lane >= 6 * head) & (lane < 6 * head + 6)
            column = lane == 2 * heads + head
            qh = jnp.where(mine, q, zero)
            qa = jnp.concatenate([qh, jnp.where(aug, aq, zero)], 1)
            qo = jnp.concatenate([qh, ones], 1)
            dah = jnp.where(mine, da, zero)
            daa = jnp.concatenate([dah, jnp.where((lane >= 3 * side) & (lane < 3 * side + 3), ad, zero)], 1)
            acc = jnp.zeros((block, 256), F32)
            for j in range(i + 1):
                to = slice(j * block, (j + 1) * block)
                k = k_ref[to, :]
                e = jnp.exp(dot(jnp.concatenate([k, ak_ref[to, :]], 1), qa, NT))
                if j == i:
                    e = jnp.where(rows_of(e.shape) <= lanes(e.shape), e, 0.0)
                dv_ref[to, :] += dot(e.astype(BF), dah)
                ds = (e * dot(jnp.concatenate([v_ref[to, :], vone], 1), daa, NT)).astype(BF)
                dk = dot(ds, qo)
                dk_ref[to, :] += dk[:, :128]
                dc_ref[to, :] -= jnp.where(column, dk[:, 128:], 0.0)
                acc = acc + dot(ds, jnp.concatenate([k, ones], 1), TN)
            dq.append(acc[:, :128])
            dc_ref[at, :] += jnp.where(column, acc[:, 128:], 0.0)
        dq_ref[at, :] = jnp.where(lane < 64, dq[0], dq[1]) * 0.125


def attend_back(pair, block, heads, q8, aq, kn, ak, vl, og, att, li, du):
    seq, width = q8.shape
    ms = np.zeros((256, 128))
    for lane in range(256):
        ms[lane, 3 * ((lane % 128) // 64) : 3 * ((lane % 128) // 64) + 3] = 1.0
    mine = pl.BlockSpec((seq, 128), lambda p: (0, pair))
    one = pl.BlockSpec((seq, 128), lambda p: (0, 0))
    return pl.pallas_call(
        functools.partial(bwd_kernel, pair, heads, block),
        grid=(1,),
        in_specs=[mine, one, mine, one, mine, mine, mine, mine, mine, full((256, 128))],
        out_specs=[one] * 4,
        out_shape=[jax.ShapeDtypeStruct((seq, 128), F32)] * 4,
        scratch_shapes=[pltpu.VMEM((seq, 128), BF), pltpu.VMEM((seq, 128), BF)],
        compiler_params=params(),
        cost_estimate=COST,
        name="attend_back",
    )(q8, aq, kn, ak, vl, og, att, li, du, const(ms))


def post_kernel(
    heads, pairs, q_ref, ks_ref, kd_ref, vd_ref, lg_ref, du_ref, att_ref, og_ref, x_ref,
    res_ref, gain_ref, w_ref, ba_ref, g64_ref, tri_ref, ms_ref, rows_ref, gqk_ref, *refs,
):
    grads, refs = refs[: 4 * pairs], refs[4 * pairs :]
    dp_ref, gt_ref, g0_ref, gq_ref, gb_ref, carry_k, carry_v, carry_c = refs
    dq_raw, dk_raw, dvs = [
        jnp.concatenate([r[...] for r in grads[i * pairs : (i + 1) * pairs]], 1) for i in range(3)
    ]
    dc = sum(r[...] for r in grads[3 * pairs :])
    step = pl.program_id(0)
    rows, width = q_ref.shape

    @pl.when(step == 0)
    def _():
        carry_k[...] = jnp.zeros_like(carry_k)
        carry_v[...] = jnp.zeros_like(carry_v)
        carry_c[...] = jnp.zeros_like(carry_c)
        g0_ref[...] = jnp.zeros_like(g0_ref)
        gq_ref[...] = jnp.zeros_like(gq_ref)
        gb_ref[...] = jnp.zeros_like(gb_ref)

    def norm_back(raw, gain, grad):
        r = lax.rsqrt(dot((raw * raw).astype(BF), g64_ref[...]) + EPS)
        n = raw * r
        wd = grad * gain
        return r * (wd - n * dot((wd * n).astype(BF), g64_ref[...])), jnp.sum(grad * n, 0, keepdims=True)

    dq, gq = norm_back(q_ref[...].astype(F32), gqk_ref[0:1, :], dq_raw)
    dks, gk = norm_back(ks_ref[...].astype(F32), gqk_ref[1:2, :], dk_raw)
    gq_ref[0:1, :] += gq
    gq_ref[1:2, :] += gk
    logits = lg_ref[...]
    sg = jax.nn.sigmoid(logits)
    mix = dot(jnp.concatenate(split2(sg), 1), ba_ref[...])
    end = rows_of(dks.shape) == rows - 1

    def shift_back(grad, part, carry):
        w = part * grad
        later = jnp.where(end, carry[0:1, :], pltpu.roll(w, rows - 1, 0))
        carry[0:1, :] = w[0:1, :]
        return grad - w + later

    dk = shift_back(dks, mix[:, :width], carry_k)
    dv = shift_back(dvs, mix[:, width:], carry_v)
    terms = jnp.concatenate([dks * kd_ref[...].astype(F32), dvs * vd_ref[...].astype(F32)], 1)
    hi, rest = split2(terms)
    dmix = dot(hi, ms_ref[...]) + dot(rest, ms_ref[...])
    sums = dot(tri_ref[...], jnp.concatenate(split3(dc), 1))
    dls = sums[:, :128] + sums[:, 128:256] + sums[:, 256:] + carry_c[0:1, :]
    carry_c[0:1, :] = dls[0:1, :]
    lane = lanes(logits.shape)
    dz = dls * jax.nn.sigmoid(-(logits + rows_ref[0:1, :]))
    dgl = jnp.where(lane < 2 * heads, dmix * sg * (1.0 - sg), jnp.where(lane < 3 * heads, dz, 0.0))
    gb_ref[0:1, :] += jnp.sum(dgl, 0, keepdims=True)
    og = og_ref[...]
    do = du_ref[...].astype(F32) * att_ref[...] * og * (1.0 - og)
    dp = jnp.concatenate([dq.astype(BF), dk.astype(BF), dv.astype(BF), do.astype(BF), dgl.astype(BF)], 1)
    dp_ref[...] = dp
    dhn = dot(dp, w_ref[...], NT)
    x = x_ref[...].astype(F32)
    factor = lax.rsqrt(jnp.mean(x * x, -1, keepdims=True) + EPS)
    n = x * factor
    g0_ref[0:1, :] += jnp.sum(dhn * n, 0, keepdims=True)
    wd = dhn * gain_ref[0:1, :]
    back = factor * (wd - n * jnp.mean(wd * n, -1, keepdims=True))
    gt_ref[...] = (back + res_ref[...].astype(F32)).astype(BF)


def post(heads, dq, dk, dv, dc, q, ks, kd, vd, lg, du, att, og, x, res, gains, w, bias_row, gqk):
    seq, width = q.shape
    pairs = len(dq)
    model = x.shape[1]
    wide = w.shape[1]
    block = min(256, seq)
    count = seq // block
    ba = np.zeros((256, 2 * width))
    ms = np.zeros((2 * width, 128))
    for lane in range(2 * width):
        head = (lane % width) // 64 + (lane // width) * heads
        ba[head, lane] = ba[128 + head, lane] = 1.0
        ms[lane, head] = 1.0
    g64 = np.kron(np.eye(width // 64), np.full((64, 64), 1 / 64))
    tri = np.triu(np.ones((block, block)))
    rows = jnp.concatenate([bias_row, jnp.zeros((7, 128), F32)], 0)

    def row(cols):
        return pl.BlockSpec((block, cols), lambda i: (count - 1 - i, 0))

    return pl.pallas_call(
        functools.partial(post_kernel, heads, pairs),
        grid=(count,),
        in_specs=[row(width)] * 4 + [row(128)] + [row(width)] * 3 + [row(model)] * 2
        + [full(gains.shape), full(w.shape), full(ba.shape), full(g64.shape), full(tri.shape),
           full(ms.shape), full((8, 128)), full(gqk.shape)] + [row(128)] * (4 * pairs),
        out_specs=[row(wide), row(model), full((8, model)), full((8, width)), full((8, 128))],
        out_shape=[jax.ShapeDtypeStruct((seq, wide), BF), jax.ShapeDtypeStruct((seq, model), BF),
                   jax.ShapeDtypeStruct((8, model), F32), jax.ShapeDtypeStruct((8, width), F32),
                   jax.ShapeDtypeStruct((8, 128), F32)],
        scratch_shapes=[pltpu.VMEM((8, width), F32), pltpu.VMEM((8, width), F32), pltpu.VMEM((8, 128), F32)],
        compiler_params=params(),
        cost_estimate=COST,
        name="post",
    )(q, ks, kd, vd, lg, du, att, og, x, res, gains, w, const(ba), const(g64), const(tri),
      const(ms), rows, gqk, *dq, *dk, *dv, *dc)


def swap(value, axis, bit):
    size = lax.axis_size(axis)
    return lax.ppermute(value, axis, [(i, i ^ bit) for i in range(size)])


def turn(value):
    size = lax.axis_size("tp")
    return lax.ppermute(value, "tp", [(i, (i + 1) % size) for i in range(size)])


def add(a, b):
    return (a.astype(F32) + b.astype(F32)).astype(BF)


def high_bits(size):
    bits, bit = [], 2
    while bit < size:
        bits.append(bit)
        bit *= 2
    return bits


def gather_1(shard):
    pieces = {(0, 0): shard, (2, 0): swap(shard, "dp", 2)}
    if lax.axis_size("dp") == 8:
        pieces[4, 0] = swap(shard, "dp", 4)
    pieces[1, 0] = swap(shard, "dp", 1)
    return pieces


def gather_2(pieces):
    size = lax.axis_size("dp")
    pieces = dict(pieces)
    if size == 8:
        half = pieces[0, 0].shape[0] // 2
        pieces[6, 0] = swap(pieces[2, 0][:half], "dp", 4)
        pieces[6, half] = swap(pieces[4, 0][half:], "dp", 2)
        pieces[3, 0] = swap(pieces[2, 0], "dp", 1)
        pieces[5, 0] = swap(pieces[4, 0], "dp", 1)
        return pieces
    for bit in high_bits(size)[1:]:
        pieces.update({(r | bit, 0): swap(p, "dp", bit) for (r, _), p in list(pieces.items()) if not r & 1})
    return pieces


def gather_3(pieces):
    pieces = dict(pieces)
    pieces.update({(r | 1, s): swap(p, "dp", 1) for (r, s), p in list(pieces.items()) if (r | 1, s) not in pieces})
    return pieces


def assemble(pieces, me):
    cut, cols = pieces[0, 0].shape
    whole = jnp.zeros((cut * lax.axis_size("dp"), cols), BF)
    for (far, start), piece in sorted(pieces.items()):
        whole = lax.dynamic_update_slice_in_dim(whole, piece, (me ^ far) * cut + start, 0)
    return whole


def scatter(whole):
    return lax.psum_scatter(whole, "dp", scatter_dimension=0, tiled=True)


def total_of(terms):
    return sum(term.astype(F32) for term in terms)


tie = lax.optimization_barrier


def pad_to(value, size, axis):
    extra = size - value.shape[axis]
    if not extra:
        return value
    return jnp.pad(value, [(0, extra if a == axis else 0) for a in range(value.ndim)])


def shards(
    tokens, attn_in, head_gates, out_proj, norm_gains, qk_gains, forget_bias, gate_up, down_proj, carried_offset,
    reset_flag, cotangent,
):
    dp, tp = lax.axis_size("dp"), lax.axis_size("tp")
    me_d, me_t = lax.axis_index("dp"), lax.axis_index("tp")
    _, seq, model = tokens.shape
    own = seq // tp
    cut = attn_in.shape[1]
    width_real = attn_in.shape[2]
    heads_real = head_gates.shape[2]
    heads = heads_real + heads_real % 2
    width = 64 * heads
    hidden = gate_up.shape[2]
    block = 512 if seq % 512 == 0 else seq
    chunks = seq // block

    attn_rows = jnp.transpose(pad_to(attn_in, width, 2), (1, 0, 2)).reshape(cut, 4 * width)
    gate_rows = jnp.transpose(pad_to(head_gates, heads, 2), (1, 0, 2)).reshape(cut, 3 * heads)
    gate_rows = pad_to(jnp.concatenate([gate_rows, jnp.transpose(norm_gains)], 1), 128, 1)
    attn_rows = jnp.concatenate([attn_rows, gate_rows], 1)
    out_own = pad_to(jnp.transpose(out_proj), width, 1)
    ffn_rows = jnp.concatenate([gate_up[0], gate_up[1], jnp.transpose(down_proj)], 1)

    bias = lax.dynamic_slice_in_dim(forget_bias.astype(F32), me_t * heads_real, heads_real, 0)
    offset = lax.dynamic_slice_in_dim(carried_offset[0], me_t * heads_real, heads_real, 0)
    bias = bias + (1 - reset_flag[0]).astype(F32) * offset
    bias_row = jnp.pad(bias, (2 * heads, 128 - 2 * heads - heads_real))[None, :]
    gqk = pad_to(jnp.tile(qk_gains.astype(F32), (1, heads)), 8, 0)
    at = me_t.astype(jnp.int32)[None]

    here = me_d.astype(jnp.int32)[None]
    x, cot = tokens[0], cotangent[0]

    def token_part(values, s):
        return lax.dynamic_slice_in_dim(values, lax.rem(me_t - s + tp, tp) * own, own, 0)

    def product(left, right):
        return dot(left, right, TN).astype(BF)

    attn_p = gather_1(attn_rows)
    out_rows = [out_own, turn(out_own)]
    while len(out_rows) < tp - 1:
        out_rows.append(turn(out_rows[-1]))
    attn_p, out_rows, ffn_rows = tie((attn_p, out_rows, ffn_rows))
    attn_p = gather_2(attn_p)
    out_rows.append(turn(out_rows[-1]))
    attn_p, out_rows, ffn_rows = tie((attn_p, out_rows, ffn_rows))
    out_whole = jnp.concatenate(out_rows, 1)
    attn_p, out_whole, ffn_rows = tie((attn_p, out_whole, ffn_rows))
    ffn_all = lax.all_gather(ffn_rows, "dp", axis=0, tiled=True)
    out_p = gather_1(out_whole)
    attn_p = gather_3(attn_p)
    hn, w, gains, q8, kn, vl, aq, ak, og, q, ks, kd, vd, lg = pre(x, here, attn_p, bias_row, gqk, heads)
    q8, out_p = tie((q8, out_p))
    out_p = gather_2(out_p)
    u, *kept_att = attend(0, block, q8, aq, kn, ak, vl, og, ())
    u, kept_att, q8 = tie((u, kept_att, q8))
    us = [[u]]

    first = tp - 1
    kept_ffn, gmids = (), []
    parts, got = [None] * chunks, [None] * chunks

    made = first + chunks
    sums = []
    out_all = None
    for t in range(first + chunks - 1 + first + 1):
        send = {}
        for c in range(chunks):
            step = t - first - c
            if 1 <= step <= first:
                send[c] = parts[c][1] if step == 1 else add(got[c], parts[c][step])
        y_send = token_part(kept_ffn[5], 1) if t == made + first - 1 else None
        send, q8, kept_ffn, x, y_send = tie((send, q8, kept_ffn, x, y_send))
        new_u = {c: turn(us[c][-1]) for c in range(len(us)) if 1 <= t - c + 1 <= first}
        new_du = {c: turn(value) for c, value in send.items()}
        fresh = None
        if t + 1 < chunks:
            fresh, *kept_att = attend(t + 1, block, q8, aq, kn, ak, vl, og, kept_att)
        if t == 1:
            out_p = gather_3(out_p)
        if t == 2:
            out_all = assemble(out_p, me_d)
        chunk = t - first
        if 0 <= chunk < chunks:
            outs = feed(chunk, block, own, at, x, cot, gains, out_all, ffn_all, us[chunk], kept_ffn)
            kept_ffn, parts[chunk] = outs[:6], outs[6:-1]
            gmids.append(outs[-1][0:1])
        h2, hid, dgu, res, uc, part = kept_ffn if kept_ffn else [None] * 6
        if t == made + first - 1:
            y_acc = turn(y_send)
        fill = None
        for i, pair in enumerate(((res, uc), (h2, dgu), (cot, hid))):
            if t == made + i:
                fill = product(*pair)
        new_u, new_du, fresh, kept_att, kept_ffn, parts, fill, out_p, out_all, q8 = tie(
            (new_u, new_du, fresh, kept_att, kept_ffn, parts, fill, out_p, out_all, q8)
        )
        if fill is not None:
            sums.append(scatter(fill))
        for c, value in new_u.items():
            us[c].append(value)
        if fresh is not None:
            us.append([fresh])
        got = [new_du.get(c, got[c]) for c in range(chunks)]
    att, li = kept_att
    h2, hid, dgu, res, uc, part = kept_ffn

    du = jnp.concatenate([add(got[c], parts[c][0]) for c in range(chunks)], 0)
    du, gmid = tie((du, sum(gmids)))
    pairs, back_parts = width // 128, []
    cuts = [0, 1, pairs] if pairs > 1 else [0, pairs]
    y_step = 2
    for begin, end in zip(cuts, cuts[1:]):
        for pair in range(begin, end):
            back_parts.append(attend_back(pair, block, heads, q8, aq, kn, ak, vl, og, att, li, du))
        y_acc, back_parts = tie((y_acc, back_parts))
        if y_step < tp:
            send, y_step = add(y_acc, token_part(part, y_step)), y_step + 1
            send, du = tie((send, du))
            y_acc = turn(send)
    dq, dk, dv, dc = zip(*back_parts)
    dp_all, gt, g0, gq, gb = post(
        heads, dq, dk, dv, dc, q, ks, kd, vd, lg, du, att, og, x, res, gains, w, bias_row, gqk
    )
    y_acc, dp_all, gt, g0 = tie((y_acc, dp_all, gt, g0))

    gq = gq[0:2].reshape(2, heads, 64).sum(1)
    gb = lax.dynamic_update_slice_in_dim(
        jnp.zeros(forget_bias.shape, F32), gb[0, 2 * heads : 2 * heads + heads_real], me_t * heads_real, 0
    )
    small = jnp.concatenate([gq.reshape(-1), gb])
    small = jnp.pad(small, (0, model - small.shape[0]))[None]
    flat = jnp.concatenate([g0[0:1], gmid, small, jnp.zeros((5, model), F32)], 0)
    ring = [sums[0][:, i * width : (i + 1) * width] for i in range(tp)]
    low, high = slice(0, model // 2), slice(model // 2, model)
    send, out_send = [token_part(gt[:, cols], 1) for cols in (low, high)], ring[1]
    send, out_send, flat, dp_all = tie((send, out_send, flat, dp_all))
    while y_step < tp:
        y_acc, y_step = turn(add(y_acc, token_part(part, y_step))), y_step + 1
    back = [turn(value) for value in send]
    fill = product(hn, dp_all)
    back, fill = tie((back, fill))
    sums.append(scatter(fill))
    for s in range(2, tp):
        back = [turn(add(value, token_part(gt[:, cols], s))) for value, cols in zip(back, (low, high))]
    out_acc = turn(out_send)
    for s in range(2, tp):
        out_acc = turn(add(out_acc, ring[s]))
    for axis, size in (("tp", tp), ("dp", dp)):
        for bit in range(size.bit_length() - 1):
            flat = flat + swap(flat, axis, 1 << bit)
    result = total_of((y_acc, token_part(part, 0))).astype(BF)
    grad_tokens = total_of((token_part(gt, 0), jnp.concatenate(back, 1)))
    grad_gu, grad_down, grad_attn = [value.astype(F32) for value in sums[1:]]
    grad_out_own = total_of((ring[0], out_acc))
    norm_grad = flat[0:2]
    qk_grad = flat[2, : 2 * 64].reshape(2, 64)
    bias_grad = flat[2, 2 * 64 : 2 * 64 + forget_bias.shape[0]]

    grad_attn_in = jnp.transpose(grad_attn[:, : 4 * width].reshape(cut, 4, width)[:, :, :width_real], (1, 0, 2))
    grad_gates = grad_attn[:, 4 * width : 4 * width + 3 * heads].reshape(cut, 3, heads)[:, :, :heads_real]
    return (
        result[None],
        grad_tokens[None],
        grad_attn_in,
        jnp.transpose(grad_gates, (1, 0, 2)),
        jnp.transpose(grad_out_own[:, :width_real]),
        jnp.stack([grad_gu[:, :hidden], grad_gu[:, hidden:]]),
        jnp.transpose(grad_down),
        norm_grad,
        qk_grad,
        bias_grad,
    )


def solution(mesh):
    return jax.shard_map(
        shards,
        mesh=mesh,
        in_specs=(
            P("dp", None, None), P(None, "dp", "tp"), P(None, "dp", "tp"), P("tp", "dp"), P(None, "dp"), P(), P(),
            P(None, "dp", "tp"), P("tp", "dp"), P("dp", None), P("dp"), P("dp", None, None),
        ),
        out_specs=(
            P("dp", "tp", None), P("dp", "tp", None), P(None, "dp", "tp"), P(None, "dp", "tp"), P("tp", "dp"),
            P(None, "dp", "tp"), P("tp", "dp"), P(), P(), P(),
        ),
        check_vma=False,
    )
```

```python
import functools

import jax
import jax.numpy as jnp
import numpy as np
from jax import lax
from jax.experimental import pallas as pl
from jax.experimental.layout import Layout, with_layout_constraint
from jax.experimental.pallas import tpu as pltpu
from jax.sharding import PartitionSpec as P

EPS = 1e-06
BF = jnp.bfloat16
F32 = jnp.float32
VMEM_LIMIT = 58 * 1024 * 1024
NT = (((1,), (1,)), ((), ()))
TN = (((0,), (0,)), ((), ()))


COST = pl.CostEstimate(flops=1, bytes_accessed=1, transcendentals=0)


def dot(a, b, dims=(((1,), (0,)), ((), ()))):
    return lax.dot_general(a, b, dims, preferred_element_type=F32)


def params():
    return pltpu.CompilerParams(vmem_limit_bytes=VMEM_LIMIT)


def split2(v):
    hi = v.astype(BF)
    return hi, (v - hi.astype(F32)).astype(BF)


def split3(v):
    hi = v.astype(BF)
    rest = v - hi.astype(F32)
    mid = rest.astype(BF)
    return hi, mid, (rest - mid.astype(F32)).astype(BF)


def lanes(shape):
    return lax.broadcasted_iota(jnp.int32, shape, len(shape) - 1)


def rows_of(shape):
    return lax.broadcasted_iota(jnp.int32, shape, 0)


def const(array, dtype=BF):
    return jnp.asarray(array.astype(np.float32), dtype)


def full(shape):
    return pl.BlockSpec(shape, lambda *_: tuple(0 for _ in shape), pipeline_mode=pl.Buffered(1))


ANY = pl.BlockSpec(memory_space=pl.ANY)
SMEM = pl.BlockSpec(memory_space=pltpu.SMEM)


def pre_kernel(
    heads, spots, me_ref, x_ref, ba_ref, g64_ref, tri_ref, mq_ref, mk_ref, rows_ref, gqk_ref, *refs,
):
    pieces, refs = refs[: len(spots)], refs[len(spots) :]
    (hn_ref, w_ref, gain_ref, q8_ref, kn_ref, vl_ref, aq_ref, ak_ref, og_ref, q_ref, ks_ref, kd_ref, vd_ref, lg_ref,
     gain_s, carry_k, carry_v, carry_c, sems) = refs
    step = pl.program_id(0)
    width = q8_ref.shape[1]
    wide = 4 * width

    @pl.when(step == 0)
    def _():
        copies = []
        for i, (far, start, count, cut) in enumerate(spots):
            row = pl.multiple_of((me_ref[0] ^ far) * cut + start, 16)
            copies.append(pltpu.make_async_copy(pieces[i], w_ref.at[pl.ds(row, count), :], sems.at[i]))
        for copy in copies:
            copy.start()
        for copy in copies:
            copy.wait()
        pick = (lanes((8, 128)) == 3 * heads + rows_of((8, 128))).astype(F32)
        pick = jnp.where(rows_of((8, 128)) < 2, pick, 0.0).astype(BF)
        gain_s[...] = dot(pick, w_ref[:, wide:], NT)
        carry_k[...] = jnp.zeros_like(carry_k)
        carry_v[...] = jnp.zeros_like(carry_v)
        carry_c[...] = jnp.zeros_like(carry_c)
        gain_ref[...] = gain_s[...]

    x = x_ref[...].astype(F32)
    factor = lax.rsqrt(jnp.mean(x * x, -1, keepdims=True) + EPS)
    hn = (x * factor * gain_s[0:1, :]).astype(BF)
    hn_ref[...] = hn
    proj = dot(hn, w_ref[...])
    q = proj[:, :width]
    k = proj[:, width : 2 * width]
    v = proj[:, 2 * width : 3 * width]
    og_ref[...] = jax.nn.sigmoid(proj[:, 3 * width : wide])
    logits = proj[:, wide:]
    lg_ref[...] = logits
    mix = dot(jnp.concatenate(split2(jax.nn.sigmoid(logits)), 1), ba_ref[...])
    first = rows_of(k.shape) == 0
    kd = jnp.where(first, carry_k[0:1, :], pltpu.roll(k, 1, 0)) - k
    vd = jnp.where(first, carry_v[0:1, :], pltpu.roll(v, 1, 0)) - v
    last = k.shape[0] - 1
    carry_k[0:1, :] = k[last:, :]
    carry_v[0:1, :] = v[last:, :]
    ks = k + mix[:, :width] * kd
    vl_ref[...] = (v + mix[:, width:] * vd).astype(BF)
    q_ref[...] = q.astype(BF)
    ks_ref[...] = ks.astype(BF)
    kd_ref[...] = kd.astype(BF)
    vd_ref[...] = vd.astype(BF)
    rq = lax.rsqrt(dot((q * q).astype(BF), g64_ref[...]) + EPS)
    rk = lax.rsqrt(dot((ks * ks).astype(BF), g64_ref[...]) + EPS)
    q8_ref[...] = ((q * rq * gqk_ref[0:1, :]).astype(BF).astype(F32) * 0.125).astype(BF)
    kn_ref[...] = (ks * rk * gqk_ref[1:2, :]).astype(BF)
    z = logits + rows_ref[0:1, :]
    ls = jnp.minimum(z, 0.0) - jnp.log1p(jnp.exp(-jnp.abs(z)))
    sums = dot(tri_ref[...], jnp.concatenate(split3(ls), 1))
    cum = sums[:, :128] + sums[:, 128:256] + sums[:, 256:] + carry_c[0:1, :]
    carry_c[0:1, :] = cum[last:, :]
    parts = jnp.concatenate(split3(cum), 1)
    aq_ref[...] = (dot(parts, mq_ref[...]) + rows_ref[1:2, :]).astype(BF)
    ak_ref[...] = (dot(parts, mk_ref[...]) + rows_ref[2:3, :]).astype(BF)


def pre(x, place, pieces, bias_row, gqk, heads):
    seq, model = x.shape
    cut = pieces[0, 0].shape[0]
    spots = [(far, start, p.shape[0], cut) for (far, start), p in sorted(pieces.items())]
    wide = pieces[0, 0].shape[1]
    width = (wide - 128) // 4
    block = min(256, seq)
    ba = np.zeros((256, 2 * width))
    for lane in range(2 * width):
        head = (lane % width) // 64 + (lane // width) * heads
        ba[head, lane] = ba[128 + head, lane] = 1.0
    g64 = np.kron(np.eye(width // 64), np.full((64, 64), 1 / 64))
    tri = np.tril(np.ones((block, block)))
    mq, mk = np.zeros((384, 128)), np.zeros((384, 128))
    ones_q, ones_k = np.zeros((1, 128)), np.zeros((1, 128))
    for head in range(heads):
        for piece in range(3):
            mq[128 * piece + 2 * heads + head, 6 * head + piece] = 1.0
            mk[128 * piece + 2 * heads + head, 6 * head + 3 + piece] = -1.0
            ones_q[0, 6 * head + 3 + piece] = 1.0
            ones_k[0, 6 * head + piece] = 1.0
    rows = jnp.concatenate([bias_row, const(ones_q, F32), const(ones_k, F32), jnp.zeros((5, 128), F32)], 0)

    def row(cols):
        return pl.BlockSpec((block, cols), lambda i: (i, 0))

    def shape(cols, dtype):
        return jax.ShapeDtypeStruct((seq, cols), dtype)

    return pl.pallas_call(
        functools.partial(pre_kernel, heads, spots),
        grid=(seq // block,),
        in_specs=[SMEM, row(model), full(ba.shape), full(g64.shape), full(tri.shape), full(mq.shape), full(mk.shape),
                  full((8, 128)), full(gqk.shape)] + [ANY] * len(spots),
        out_specs=[row(model), full((model, wide)), full((8, model))] + [row(width)] * 3 + [row(128)] * 2 + [row(width)] * 5 + [row(128)],
        out_shape=[shape(model, BF), jax.ShapeDtypeStruct((model, wide), BF), jax.ShapeDtypeStruct((8, model), F32)]
        + [shape(width, BF)] * 3
        + [shape(128, BF)] * 2 + [shape(width, F32)] + [shape(width, BF)] * 4 + [shape(128, F32)],
        scratch_shapes=[pltpu.VMEM((8, model), F32), pltpu.VMEM((8, width), F32), pltpu.VMEM((8, width), F32),
                        pltpu.VMEM((8, 128), F32), pltpu.SemaphoreType.DMA((len(spots),))],
        compiler_params=params(),
        cost_estimate=COST,
        name="pre",
    )(place, x, const(ba), const(g64), const(tri), const(mq), const(mk), rows, gqk,
      *[p for _, p in sorted(pieces.items())])


def fwd_kernel(chunk, block, q_ref, aq_ref, k_ref, ak_ref, v_ref, og_ref, *refs):
    u_ref, att_ref, li_ref = refs[-3:]
    pair = pl.program_id(0)
    q, aq = q_ref[...], aq_ref[...]
    lane = lanes(q.shape)
    ones = jnp.ones((block, 128), BF)
    fine = block // 2
    out = []
    for side in range(2):
        head = 2 * pair + side
        mine = (lane >= 64 * side) & (lane < 64 * side + 64)
        aug = (lane >= 6 * head) & (lane < 6 * head + 6)
        zero = jnp.zeros_like(q)
        qa = jnp.concatenate([jnp.where(mine, q, zero), jnp.where(aug, aq, zero)], 1)
        acc = jnp.zeros((block, 256), F32)
        for j in range(chunk):
            at = slice(j * block, (j + 1) * block)
            e = jnp.exp(dot(qa, jnp.concatenate([k_ref[at, :], ak_ref[at, :]], 1), NT))
            acc = acc + dot(e.astype(BF), jnp.concatenate([v_ref[at, :], ones], 1))
        tops = []
        for begin in range(0, block, fine):
            at = slice(chunk * block, chunk * block + begin + fine)
            rows = slice(begin, begin + fine)
            e = jnp.exp(dot(qa[rows], jnp.concatenate([k_ref[at, :], ak_ref[at, :]], 1), NT))
            e = jnp.where(rows_of(e.shape) + begin >= lanes(e.shape), e, 0.0)
            tops.append(acc[rows] + dot(e.astype(BF), jnp.concatenate([v_ref[at, :], ones[: begin + fine]], 1)))
        out.append(jnp.concatenate(tops, 0))
    low = lane < 64
    total = jnp.where(low, out[0][:, 128:], out[1][:, 128:])
    inverse = 1.0 / total
    att = jnp.where(low, out[0][:, :128], out[1][:, :128]) * inverse
    u_ref[...] = (att * og_ref[...]).astype(BF)
    att_ref[...] = att
    li_ref[...] = inverse


def attend(chunk, block, q8, aq, kn, ak, vl, og, kept):
    seq, width = q8.shape
    keys = (chunk + 1) * block
    grid = (width // 128,)
    mine = pl.BlockSpec((block, 128), lambda p: (chunk, p))
    other = pl.BlockSpec((keys, 128), lambda p: (0, p))
    return pl.pallas_call(
        functools.partial(fwd_kernel, chunk, block),
        grid=grid,
        in_specs=[mine, pl.BlockSpec((block, 128), lambda p: (chunk, 0)), other,
                  pl.BlockSpec((keys, 128), lambda p: (0, 0)), other, mine] + [ANY] * len(kept),
        out_specs=[pl.BlockSpec((block, 128), lambda p: (0, p)), mine, mine],
        out_shape=[jax.ShapeDtypeStruct((block, width), BF)] + [jax.ShapeDtypeStruct((seq, width), F32)] * 2,
        input_output_aliases={6 + i: 1 + i for i in range(len(kept))},
        compiler_params=params(),
        cost_estimate=COST,
        name="attend",
    )(q8, aq, kn, ak, vl, og, *kept)


def ffn_kernel(
    count, chunk, block, step_rows, own, at_ref, x_ref, cot_ref, gain_ref, o_any, f_any, *refs
):
    us, outs = refs[:count], refs[-10 - count : -3]
    o_ref, f_ref, sems = refs[-3:]
    copies = [pltpu.make_async_copy(a, b, sems.at[i]) for i, (a, b) in enumerate(((o_any, o_ref), (f_any, f_ref)))]

    copies[0].start()
    copies[1].start()
    h2_ref, hid_ref, dgu_ref, res_ref, uc_ref, part_ref = outs[:6]
    dus, gmid_ref = outs[6:-1], outs[-1]
    hidden = hid_ref.shape[1]
    gain = gain_ref[1:2, :]
    rows = x_ref.shape[0]
    size = rows // 2
    width = o_ref.shape[1] // count
    subs = [slice(i * size, (i + 1) * size) for i in range(2)]
    y1, n, factor, h2, gu, dhid, hid, dgu, dh2, res = [[None, None] for _ in range(10)]

    def first(i):
        u = jnp.concatenate([r[subs[i], :] for r in us], 1)
        uc_ref[subs[i], :] = u
        y1[i] = x_ref[subs[i], :].astype(F32) + dot(u, o_ref[...], NT)

    def normed(i):
        factor[i] = lax.rsqrt(jnp.mean(y1[i] * y1[i], -1, keepdims=True) + EPS)
        n[i] = y1[i] * factor[i]
        h2[i] = (n[i] * gain).astype(BF)
        h2_ref[subs[i], :] = h2[i]

    def gates(i):
        gu[i] = dot(h2[i], f_ref[:, : 2 * hidden])

    def hidden_back(i):
        dhid[i] = dot(cot_ref[subs[i], :], f_ref[:, 2 * hidden :])

    def activated(i):
        g, up = gu[i][:, :hidden], gu[i][:, hidden:]
        sg = jax.nn.sigmoid(g)
        act = g * sg
        hid[i] = (act * up).astype(BF)
        hid_ref[subs[i], :] = hid[i]
        dg = dhid[i] * up * sg * (1.0 + g * (1.0 - sg))
        dgu[i] = jnp.concatenate([dg.astype(BF), (dhid[i] * act).astype(BF)], 1)
        dgu_ref[subs[i], :] = dgu[i]

    def normed_back(i):
        dh2[i] = dot(dgu[i], f_ref[:, : 2 * hidden], NT)

    def part(i):
        token = chunk * block + pl.program_id(0) * step_rows + i * size + rows_of((size, 1))
        owned = (token >= at_ref[0] * own) & (token < (at_ref[0] + 1) * own)
        total = dot(hid[i], f_ref[:, 2 * hidden :], NT) + jnp.where(owned, y1[i], 0.0)
        part_ref[subs[i], :] = total.astype(BF)

    def residual(i):
        gmid_ref[i : i + 1, :] = jnp.sum(dh2[i] * n[i], 0, keepdims=True)
        wd = gain * dh2[i]
        back = factor[i] * (wd - n[i] * jnp.mean(wd * n[i], -1, keepdims=True))
        res[i] = jnp.where(at_ref[0] == 0, back + cot_ref[subs[i], :].astype(F32), back).astype(BF)
        res_ref[subs[i], :] = res[i]

    def last(i):
        du = dot(res[i], o_ref[...]).astype(BF)
        for s in range(count):
            dus[s][subs[i], :] = du[:, s * width : (s + 1) * width]

    gmid_ref[...] = jnp.zeros_like(gmid_ref)
    copies[0].wait()
    first(0)
    first(1)
    copies[1].wait()
    normed(0)
    hidden_back(0)
    gates(0)
    normed(1)
    hidden_back(1)
    gates(1)
    activated(0)
    normed_back(0)
    activated(1)
    normed_back(1)
    residual(0)
    part(0)
    last(0)
    residual(1)
    part(1)
    last(1)


def feed(chunk, block, own, place, x, cot, gains, o, f, us, kept):
    seq, model = x.shape
    hidden = f.shape[1] // 3
    count = len(us)
    width = us[0].shape[1]
    step_rows = block
    per = 1

    def mine(cols):
        return pl.BlockSpec((step_rows, cols), lambda i: (chunk * per + i, 0))

    def local(cols):
        return pl.BlockSpec((step_rows, cols), lambda i: (i, 0))

    kept_cols = [model, hidden, 2 * hidden, model, count * width, model]
    return pl.pallas_call(
        functools.partial(ffn_kernel, count, chunk, block, step_rows, own),
        grid=(per,),
        in_specs=[SMEM, mine(model), mine(model), full(gains.shape), ANY, ANY]
        + [local(width)] * count + [ANY] * len(kept),
        out_specs=[mine(c) for c in kept_cols] + [local(width)] * count + [full((8, model))],
        out_shape=[jax.ShapeDtypeStruct((seq, c), BF) for c in kept_cols]
        + [jax.ShapeDtypeStruct((block, width), BF)] * count + [jax.ShapeDtypeStruct((8, model), F32)],
        scratch_shapes=[pltpu.VMEM(o.shape, BF), pltpu.VMEM(f.shape, BF), pltpu.SemaphoreType.DMA((2,))],
        input_output_aliases={6 + count + i: i for i in range(len(kept))},
        compiler_params=params(),
        cost_estimate=COST,
        name="feed",
    )(place, x, cot, gains, o, f, *us, *kept)


def bwd_kernel(
    begin, heads, block, q_ref, aq_ref, k_ref, ak_ref, v_ref, og_ref, att_ref, li_ref, du_ref, ms_ref,
    dq_ref, dk_ref, dv_ref, dc_ref, da_s, ad_s,
):
    pair = begin + pl.program_id(0)
    seq = q_ref.shape[0]
    count = seq // block
    lane = lanes((block, 128))
    zero = jnp.zeros((block, 128), BF)
    ones = jnp.ones((block, 128), BF)
    third = lane - 3 * (lane // 3)
    for i in range(count):
        at = slice(i * block, (i + 1) * block)
        da = (du_ref[at, :].astype(F32) * og_ref[at, :] * li_ref[at, :]).astype(BF)
        da_s[at, :] = da
        delta = dot(jnp.concatenate(split2(da.astype(F32) * att_ref[at, :]), 1), ms_ref[...])
        hi, mid, rest = split3(-delta)
        ad_s[at, :] = jnp.where(third == 0, hi, jnp.where(third == 1, mid, rest))
    dk_ref[...] = jnp.zeros_like(dk_ref)
    dv_ref[...] = jnp.zeros_like(dv_ref)

    @pl.when(pl.program_id(0) == 0)
    def _():
        dc_ref[...] = jnp.zeros_like(dc_ref)


    vone = jnp.where(lane < 6, ones, zero)
    for i in range(count):
        at = slice(i * block, (i + 1) * block)
        q, aq, da, ad = q_ref[at, :], aq_ref[at, :], da_s[at, :], ad_s[at, :]
        dq = []
        for side in range(2):
            head = 2 * pair + side
            mine = (lane >= 64 * side) & (lane < 64 * side + 64)
            aug = (lane >= 6 * head) & (lane < 6 * head + 6)
            column = lane == 2 * heads + head
            qh = jnp.where(mine, q, zero)
            qa = jnp.concatenate([qh, jnp.where(aug, aq, zero)], 1)
            qo = jnp.concatenate([qh, ones], 1)
            dah = jnp.where(mine, da, zero)
            daa = jnp.concatenate([dah, jnp.where((lane >= 3 * side) & (lane < 3 * side + 3), ad, zero)], 1)
            acc = jnp.zeros((block, 256), F32)

            def pair_of(to, first):
                size = to.stop - to.start
                k = k_ref[to, :]
                e = jnp.exp(dot(jnp.concatenate([k, ak_ref[to, :]], 1), qa[first:], NT))
                if to.stop > i * block:
                    shift = to.start - i * block - first
                    e = jnp.where(rows_of(e.shape) + shift <= lanes(e.shape), e, 0.0)
                dv_ref[to, :] += dot(e.astype(BF), dah[first:])
                ds = (e * dot(jnp.concatenate([v_ref[to, :], vone[:size]], 1), daa[first:], NT)).astype(BF)
                dk = dot(ds, qo[first:])
                dk_ref[to, :] += dk[:, :128]
                dc_ref[to, :] -= jnp.where(column[:size], dk[:, 128:], 0.0)
                return dot(ds, jnp.concatenate([k, ones[:size]], 1), TN)

            for j in range(i):
                acc = acc + pair_of(slice(j * block, (j + 1) * block), 0)
            half = block // 2
            acc = acc + pair_of(slice(i * block, i * block + half), 0)
            acc = jnp.concatenate(
                [acc[:half], acc[half:] + pair_of(slice(i * block + half, (i + 1) * block), half)], 0
            )
            dq.append(acc[:, :128])
            dc_ref[at, :] += jnp.where(column, acc[:, 128:], 0.0)
        dq_ref[at, :] = jnp.where(lane < 64, dq[0], dq[1]) * 0.125


def attend_back(begin, end, block, heads, q8, aq, kn, ak, vl, og, att, li, du):
    seq, width = q8.shape
    ms = np.zeros((256, 128))
    for lane in range(256):
        ms[lane, 3 * ((lane % 128) // 64) : 3 * ((lane % 128) // 64) + 3] = 1.0
    mine = pl.BlockSpec((seq, 128), lambda p: (0, begin + p))
    own = pl.BlockSpec((seq, 128), lambda p: (0, p))
    one = pl.BlockSpec((seq, 128), lambda p: (0, 0))
    return pl.pallas_call(
        functools.partial(bwd_kernel, begin, heads, block),
        grid=(end - begin,),
        in_specs=[mine, one, mine, one, mine, mine, mine, mine, mine, full((256, 128))],
        out_specs=[own, own, own, one],
        out_shape=[jax.ShapeDtypeStruct((seq, 128 * (end - begin)), F32)] * 3 + [jax.ShapeDtypeStruct((seq, 128), F32)],
        scratch_shapes=[pltpu.VMEM((seq, 128), BF), pltpu.VMEM((seq, 128), BF)],
        compiler_params=params(),
        cost_estimate=COST,
        name="attend_back",
    )(q8, aq, kn, ak, vl, og, att, li, du, const(ms))


def post_kernel(
    heads, groups, q_ref, ks_ref, kd_ref, vd_ref, lg_ref, du_ref, att_ref, og_ref, x_ref,
    res_ref, gain_ref, w_ref, ba_ref, g64_ref, tri_ref, ms_ref, rows_ref, gqk_ref, *refs,
):
    grads, refs = refs[: 4 * groups], refs[4 * groups :]
    dp_ref, gt_ref, g0_ref, gq_ref, gb_ref, carry_k, carry_v, carry_c = refs
    dq_raw, dk_raw, dvs = [
        jnp.concatenate([r[...] for r in grads[i * groups : (i + 1) * groups]], 1) for i in range(3)
    ]
    dc = sum(r[...] for r in grads[3 * groups :])
    step = pl.program_id(0)
    rows, width = q_ref.shape

    @pl.when(step == 0)
    def _():
        carry_k[...] = jnp.zeros_like(carry_k)
        carry_v[...] = jnp.zeros_like(carry_v)
        carry_c[...] = jnp.zeros_like(carry_c)
        g0_ref[...] = jnp.zeros_like(g0_ref)
        gq_ref[...] = jnp.zeros_like(gq_ref)
        gb_ref[...] = jnp.zeros_like(gb_ref)

    def norm_back(raw, gain, grad):
        r = lax.rsqrt(dot((raw * raw).astype(BF), g64_ref[...]) + EPS)
        n = raw * r
        wd = grad * gain
        return r * (wd - n * dot((wd * n).astype(BF), g64_ref[...])), jnp.sum(grad * n, 0, keepdims=True)

    dq, gq = norm_back(q_ref[...].astype(F32), gqk_ref[0:1, :], dq_raw)
    dks, gk = norm_back(ks_ref[...].astype(F32), gqk_ref[1:2, :], dk_raw)
    gq_ref[0:1, :] += gq
    gq_ref[1:2, :] += gk
    logits = lg_ref[...]
    sg = jax.nn.sigmoid(logits)
    mix = dot(jnp.concatenate(split2(sg), 1), ba_ref[...])
    end = rows_of(dks.shape) == rows - 1

    def shift_back(grad, part, carry):
        w = part * grad
        later = jnp.where(end, carry[0:1, :], pltpu.roll(w, rows - 1, 0))
        carry[0:1, :] = w[0:1, :]
        return grad - w + later

    dk = shift_back(dks, mix[:, :width], carry_k)
    dv = shift_back(dvs, mix[:, width:], carry_v)
    terms = jnp.concatenate([dks * kd_ref[...].astype(F32), dvs * vd_ref[...].astype(F32)], 1)
    hi, rest = split2(terms)
    dmix = dot(hi, ms_ref[...]) + dot(rest, ms_ref[...])
    sums = dot(tri_ref[...], jnp.concatenate(split3(dc), 1))
    dls = sums[:, :128] + sums[:, 128:256] + sums[:, 256:] + carry_c[0:1, :]
    carry_c[0:1, :] = dls[0:1, :]
    lane = lanes(logits.shape)
    dz = dls * jax.nn.sigmoid(-(logits + rows_ref[0:1, :]))
    dgl = jnp.where(lane < 2 * heads, dmix * sg * (1.0 - sg), jnp.where(lane < 3 * heads, dz, 0.0))
    gb_ref[0:1, :] += jnp.sum(dgl, 0, keepdims=True)
    og = og_ref[...]
    do = du_ref[...].astype(F32) * att_ref[...] * og * (1.0 - og)
    dp = jnp.concatenate([dq.astype(BF), dk.astype(BF), dv.astype(BF), do.astype(BF), dgl.astype(BF)], 1)
    dp_ref[...] = dp
    dhn = dot(dp, w_ref[...], NT)
    x = x_ref[...].astype(F32)
    factor = lax.rsqrt(jnp.mean(x * x, -1, keepdims=True) + EPS)
    n = x * factor
    g0_ref[0:1, :] += jnp.sum(dhn * n, 0, keepdims=True)
    wd = dhn * gain_ref[0:1, :]
    back = factor * (wd - n * jnp.mean(wd * n, -1, keepdims=True))
    gt_ref[...] = (back + res_ref[...].astype(F32)).astype(BF)


def post(heads, dq, dk, dv, dc, q, ks, kd, vd, lg, du, att, og, x, res, gains, w, bias_row, gqk):
    seq, width = q.shape
    groups = len(dq)
    model = x.shape[1]
    wide = w.shape[1]
    block = min(256, seq)
    count = seq // block
    ba = np.zeros((256, 2 * width))
    ms = np.zeros((2 * width, 128))
    for lane in range(2 * width):
        head = (lane % width) // 64 + (lane // width) * heads
        ba[head, lane] = ba[128 + head, lane] = 1.0
        ms[lane, head] = 1.0
    g64 = np.kron(np.eye(width // 64), np.full((64, 64), 1 / 64))
    tri = np.triu(np.ones((block, block)))
    rows = jnp.concatenate([bias_row, jnp.zeros((7, 128), F32)], 0)

    def row(cols):
        return pl.BlockSpec((block, cols), lambda i: (count - 1 - i, 0))

    return pl.pallas_call(
        functools.partial(post_kernel, heads, groups),
        grid=(count,),
        in_specs=[row(width)] * 4 + [row(128)] + [row(width)] * 3 + [row(model)] * 2
        + [full(gains.shape), full(w.shape), full(ba.shape), full(g64.shape), full(tri.shape),
           full(ms.shape), full((8, 128)), full(gqk.shape)] + [row(g.shape[1]) for g in dq + dk + dv + dc],
        out_specs=[row(wide), row(model), full((8, model)), full((8, width)), full((8, 128))],
        out_shape=[jax.ShapeDtypeStruct((seq, wide), BF), jax.ShapeDtypeStruct((seq, model), BF),
                   jax.ShapeDtypeStruct((8, model), F32), jax.ShapeDtypeStruct((8, width), F32),
                   jax.ShapeDtypeStruct((8, 128), F32)],
        scratch_shapes=[pltpu.VMEM((8, width), F32), pltpu.VMEM((8, width), F32), pltpu.VMEM((8, 128), F32)],
        compiler_params=params(),
        cost_estimate=COST,
        name="post",
    )(q, ks, kd, vd, lg, du, att, og, x, res, gains, w, const(ba), const(g64), const(tri),
      const(ms), rows, gqk, *dq, *dk, *dv, *dc)


def swap(value, axis, bit):
    size = lax.axis_size(axis)
    return lax.ppermute(value, axis, [(i, i ^ bit) for i in range(size)])


def turn(value):
    size = lax.axis_size("tp")
    return lax.ppermute(value, "tp", [(i, (i + 1) % size) for i in range(size)])


def add(a, b):
    return (a.astype(F32) + b.astype(F32)).astype(BF)


def high_bits(size):
    bits, bit = [], 2
    while bit < size:
        bits.append(bit)
        bit *= 2
    return bits


def gather_1(shard):
    pieces = {(0, 0): shard, (2, 0): swap(shard, "dp", 2)}
    if lax.axis_size("dp") == 8:
        pieces[4, 0] = swap(shard, "dp", 4)
    pieces[1, 0] = swap(shard, "dp", 1)
    return pieces


def gather_2(pieces):
    size = lax.axis_size("dp")
    pieces = dict(pieces)
    if size == 8:
        half = pieces[0, 0].shape[0] // 2
        pieces[6, 0] = swap(pieces[2, 0][:half], "dp", 4)
        pieces[6, half] = swap(pieces[4, 0][half:], "dp", 2)
        pieces[3, 0] = swap(pieces[2, 0], "dp", 1)
        pieces[5, 0] = swap(pieces[4, 0], "dp", 1)
        return pieces
    for bit in high_bits(size)[1:]:
        pieces.update({(r | bit, 0): swap(p, "dp", bit) for (r, _), p in list(pieces.items()) if not r & 1})
    return pieces


def gather_3(pieces):
    pieces = dict(pieces)
    pieces.update({(r | 1, s): swap(p, "dp", 1) for (r, s), p in list(pieces.items()) if (r | 1, s) not in pieces})
    return pieces


def assemble(pieces, me):
    cut, cols = pieces[0, 0].shape
    whole = jnp.zeros((cut * lax.axis_size("dp"), cols), BF)
    for (far, start), piece in sorted(pieces.items()):
        whole = lax.dynamic_update_slice_in_dim(whole, piece, (me ^ far) * cut + start, 0)
    return whole


def cut_out(whole, me, far):
    rows = whole.shape[0] // lax.axis_size("dp")
    return lax.dynamic_slice_in_dim(whole, (me ^ far) * rows, rows, 0)


def odd_rows(whole, me):
    return jnp.concatenate([cut_out(whole, me, r) for r in range(1, lax.axis_size("dp"), 2)], 0)


def scatter_2_add(whole, got, me):
    size = lax.axis_size("dp")
    rows = whole.shape[0] // size
    return {r: add(cut_out(whole, me, r), got[rows * (r // 2) : rows * (r // 2 + 1)]) for r in range(0, size, 2)}


def scatter_2_send(pieces):
    pieces = dict(pieces)
    if lax.axis_size("dp") == 8:
        half = pieces[0].shape[0] // 2
        pieces[-1] = swap(pieces[6][:half], "dp", 2)
        pieces[-2] = swap(pieces[6][half:], "dp", 4)
    return pieces


def scatter_3_add(pieces):
    if lax.axis_size("dp") == 8:
        half = pieces[0].shape[0] // 2
        to_y = jnp.concatenate([add(pieces[4][:half], pieces[-1]), pieces[4][half:]], 0)
        to_x = jnp.concatenate([pieces[2][:half], add(pieces[2][half:], pieces[-2])], 0)
        return {0: pieces[0], 2: to_x, 4: to_y}
    return pieces


def scatter_3_send(pieces):
    size = lax.axis_size("dp")
    if size == 8:
        return [pieces[0], swap(pieces[2], "dp", 2), swap(pieces[4], "dp", 4)]
    for bit in reversed(high_bits(size)):
        got = {r: swap(pieces[r], "dp", bit) for r in pieces if r & bit}
        pieces = {r: add(p, got[r | bit]) for r, p in pieces.items() if not r & bit}
    return [pieces[0]]


def rows_major(value):
    return with_layout_constraint(value, Layout(major_to_minor=(0, 1)))


def scatter(whole):
    return lax.psum_scatter(whole, "dp", scatter_dimension=0, tiled=True)


def total_of(terms):
    return sum(term.astype(F32) for term in terms)


tie = lax.optimization_barrier


def pad_to(value, size, axis):
    extra = size - value.shape[axis]
    if not extra:
        return value
    return jnp.pad(value, [(0, extra if a == axis else 0) for a in range(value.ndim)])


def shards(
    tokens, attn_in, head_gates, out_proj, norm_gains, qk_gains, forget_bias, gate_up, down_proj, carried_offset,
    reset_flag, cotangent,
):
    dp, tp = lax.axis_size("dp"), lax.axis_size("tp")
    me_d, me_t = lax.axis_index("dp"), lax.axis_index("tp")
    _, seq, model = tokens.shape
    own = seq // tp
    cut = attn_in.shape[1]
    width_real = attn_in.shape[2]
    heads_real = head_gates.shape[2]
    heads = heads_real + heads_real % 2
    width = 64 * heads
    hidden = gate_up.shape[2]
    block = 512 if seq % 512 == 0 else seq
    chunks = seq // block

    attn_rows = jnp.transpose(pad_to(attn_in, width, 2), (1, 0, 2)).reshape(cut, 4 * width)
    gate_rows = jnp.transpose(pad_to(head_gates, heads, 2), (1, 0, 2)).reshape(cut, 3 * heads)
    gate_rows = pad_to(jnp.concatenate([gate_rows, jnp.transpose(norm_gains)], 1), 128, 1)
    attn_rows = jnp.concatenate([attn_rows, gate_rows], 1)
    out_own = pad_to(jnp.transpose(out_proj), width, 1)
    ffn_rows = jnp.concatenate([gate_up[0], gate_up[1], jnp.transpose(down_proj)], 1)

    bias = lax.dynamic_slice_in_dim(forget_bias.astype(F32), me_t * heads_real, heads_real, 0)
    offset = lax.dynamic_slice_in_dim(carried_offset[0], me_t * heads_real, heads_real, 0)
    bias = bias + (1 - reset_flag[0]).astype(F32) * offset
    bias_row = jnp.pad(bias, (2 * heads, 128 - 2 * heads - heads_real))[None, :]
    gqk = pad_to(jnp.tile(qk_gains.astype(F32), (1, heads)), 8, 0)
    at = me_t.astype(jnp.int32)[None]

    here = me_d.astype(jnp.int32)[None]
    x, cot = tokens[0], cotangent[0]

    def token_part(values, s):
        return lax.dynamic_slice_in_dim(values, lax.rem(me_t - s + tp, tp) * own, own, 0)

    def product(left, right):
        return dot(left, right, TN).astype(BF)

    attn_p = gather_1(attn_rows)
    out_rows = [out_own, turn(out_own)]
    while len(out_rows) < tp - 1:
        out_rows.append(turn(out_rows[-1]))
    attn_p, out_rows, ffn_rows = tie((attn_p, out_rows, ffn_rows))
    attn_p = gather_2(attn_p)
    out_rows.append(turn(out_rows[-1]))
    attn_p, out_rows, ffn_rows = tie((attn_p, out_rows, ffn_rows))
    out_whole = jnp.concatenate(out_rows, 1)
    attn_p, out_whole, ffn_rows = tie((attn_p, out_whole, ffn_rows))
    ffn_all = lax.all_gather(ffn_rows, "dp", axis=0, tiled=True)
    out_p = gather_1(out_whole)
    attn_p = gather_3(attn_p)
    hn, w, gains, q8, kn, vl, aq, ak, og, q, ks, kd, vd, lg = pre(x, here, attn_p, bias_row, gqk, heads)
    q8, out_p = tie((q8, out_p))
    out_p = gather_2(out_p)
    u, *kept_att = attend(0, block, q8, aq, kn, ak, vl, og, ())
    u, kept_att, q8 = tie((u, kept_att, q8))
    us = [[u]]

    first = tp - 1
    kept_ffn, gmids = (), []
    parts, got = [None] * chunks, [None] * chunks

    made = first + chunks
    sums = []
    out_all = None
    for t in range(first + chunks - 1 + first + 1):
        send = {}
        for c in range(chunks):
            step = t - first - c
            if 1 <= step <= first:
                send[c] = parts[c][1] if step == 1 else add(got[c], parts[c][step])
        y_send = token_part(kept_ffn[5], 1) if t == made + first - 1 else None
        send, q8, kept_ffn, x, y_send = tie((send, q8, kept_ffn, x, y_send))
        new_u = {c: turn(us[c][-1]) for c in range(len(us)) if 1 <= t - c + 1 <= first}
        new_du = {c: turn(value) for c, value in send.items()}
        fresh = None
        if t + 1 < chunks:
            fresh, *kept_att = attend(t + 1, block, q8, aq, kn, ak, vl, og, kept_att)
        if t == 1:
            out_p = gather_3(out_p)
        if t == 2:
            out_all = assemble(out_p, me_d)
        chunk = t - first
        if 0 <= chunk < chunks:
            outs = feed(chunk, block, own, at, x, cot, gains, out_all, ffn_all, us[chunk], kept_ffn)
            kept_ffn, parts[chunk] = outs[:6], outs[6:-1]
            gmids.append(outs[-1][0:1] + outs[-1][1:2])
        h2, hid, dgu, res, uc, part = kept_ffn if kept_ffn else [None] * 6
        if t == made + first - 1:
            y_acc = turn(y_send)
        fill = []
        if t == made:
            fill = [product(res, uc), rows_major(product(cot, hid))]
        if t == made + 1:
            fill = [product(h2, dgu)]
        out_q, out_p = out_p, None if t == 0 else out_p
        new_u, new_du, fresh, kept_att, kept_ffn, parts, fill, out_p, out_all, q8 = tie(
            (new_u, new_du, fresh, kept_att, kept_ffn, parts, fill, out_p, out_all, q8)
        )
        if t == 0:
            out_p = out_q
        sums += [scatter(value) for value in fill]
        for c, value in new_u.items():
            us[c].append(value)
        if fresh is not None:
            us.append([fresh])
        got = [new_du.get(c, got[c]) for c in range(chunks)]
    att, li = kept_att
    h2, hid, dgu, res, uc, part = kept_ffn

    du = jnp.concatenate([add(got[c], parts[c][0]) for c in range(chunks)], 0)
    du, gmid = tie((du, sum(gmids)))
    pairs, back_parts = width // 128, []
    cuts = [0, 1, pairs] if pairs > 1 else [0, pairs]
    y_step = 2
    ring = out_acc = None
    for begin, end in zip(cuts, cuts[1:]):
        back_parts.append(attend_back(begin, end, block, heads, q8, aq, kn, ak, vl, og, att, li, du))
        y_acc, back_parts, out_acc = tie((y_acc, back_parts, out_acc))
        if y_step < tp:
            if ring is None:
                ring = [sums[0][:, i * width : (i + 1) * width] for i in range(tp)]
                out_send, out_step = ring[1], 2
            else:
                out_send, out_step = add(out_acc, ring[out_step]), out_step + 1
            send, y_step = add(y_acc, token_part(part, y_step)), y_step + 1
            send, du, out_send = tie((send, du, out_send))
            y_acc, out_acc = turn(send), turn(out_send)
    dq, dk, dv, dc = zip(*back_parts)
    dp_all, gt, g0, gq, gb = post(
        heads, dq, dk, dv, dc, q, ks, kd, vd, lg, du, att, og, x, res, gains, w, bias_row, gqk
    )
    y_acc, dp_all, gt, g0, out_acc = tie((y_acc, dp_all, gt, g0, out_acc))

    send = token_part(gt, 1)
    send, dp_all, y_acc, out_acc = tie((send, dp_all, y_acc, out_acc))
    back = turn(send)
    attn_s = product(hn, dp_all)
    odd = odd_rows(attn_s, me_d)
    gq = gq[0:2].reshape(2, heads, 64).sum(1)
    gb = lax.dynamic_update_slice_in_dim(
        jnp.zeros(forget_bias.shape, F32), gb[0, 2 * heads : 2 * heads + heads_real], me_t * heads_real, 0
    )
    small = jnp.concatenate([gq.reshape(-1), gb])
    small = jnp.pad(small, (0, model - small.shape[0]))[None]
    flat = jnp.concatenate([g0[0:1], gmid, small, jnp.zeros((5, model), F32)], 0)
    back, attn_s, odd, flat = tie((back, attn_s, odd, flat))
    while y_step < tp:
        y_acc, y_step = turn(add(y_acc, token_part(part, y_step))), y_step + 1
    across = [1 << i for i in range(tp.bit_length() - 1)]
    along = [1 << i for i in range(dp.bit_length() - 1)]
    stage = 0
    for s in range(2, tp):
        send, out_send = add(back, token_part(gt, s)), None
        if out_step < tp:
            out_send, out_step = add(out_acc, ring[out_step]), out_step + 1
        if stage == 1:
            attn_s = scatter_3_add(attn_s)
        send, flat, out_send, attn_s, odd = tie((send, flat, out_send, attn_s, odd))
        back = turn(send)
        if out_send is not None:
            out_acc = turn(out_send)
        if stage == 0:
            attn_s, stage = scatter_2_send(scatter_2_add(attn_s, swap(odd, "dp", 1), me_d)), 1
        elif stage == 1:
            attn_s, stage = scatter_3_send(attn_s), 2
        for axis, bits in (("dp", along), ("tp", across)):
            for _ in range(2):
                if bits and (axis == "dp" or s > 2):
                    flat = flat + swap(flat, axis, bits.pop(0))
                    break
        back, flat, out_acc, attn_s = tie((back, flat, out_acc, attn_s))
    while out_step < tp:
        out_acc, out_step = turn(add(out_acc, ring[out_step])), out_step + 1
    if stage == 1:
        attn_s = scatter_3_send(scatter_3_add(attn_s))
    for axis, bits in (("dp", along), ("tp", across)):
        for bit in bits:
            flat = flat + swap(flat, axis, bit)
    result, back, gt = tie((total_of((y_acc, token_part(part, 0))).astype(BF), back, gt))
    grad_tokens = total_of((token_part(gt, 0), back))
    grad_attn = total_of(attn_s)
    grad_down, grad_gu = [value.astype(F32) for value in sums[1:]]
    grad_out_own = total_of((ring[0], out_acc))
    norm_grad = flat[0:2]
    qk_grad = flat[2, : 2 * 64].reshape(2, 64)
    bias_grad = flat[2, 2 * 64 : 2 * 64 + forget_bias.shape[0]]

    grad_attn_in = jnp.transpose(grad_attn[:, : 4 * width].reshape(cut, 4, width)[:, :, :width_real], (1, 0, 2))
    grad_gates = grad_attn[:, 4 * width : 4 * width + 3 * heads].reshape(cut, 3, heads)[:, :, :heads_real]
    return (
        result[None],
        grad_tokens[None],
        grad_attn_in,
        jnp.transpose(grad_gates, (1, 0, 2)),
        jnp.transpose(grad_out_own[:, :width_real]),
        jnp.stack([grad_gu[:, :hidden], grad_gu[:, hidden:]]),
        jnp.transpose(grad_down),
        norm_grad,
        qk_grad,
        bias_grad,
    )


def solution(mesh):
    return jax.shard_map(
        shards,
        mesh=mesh,
        in_specs=(
            P("dp", None, None), P(None, "dp", "tp"), P(None, "dp", "tp"), P("tp", "dp"), P(None, "dp"), P(), P(),
            P(None, "dp", "tp"), P("tp", "dp"), P("dp", None), P("dp"), P("dp", None, None),
        ),
        out_specs=(
            P("dp", "tp", None), P("dp", "tp", None), P(None, "dp", "tp"), P(None, "dp", "tp"), P("tp", "dp"),
            P(None, "dp", "tp"), P("tp", "dp"), P(), P(), P(),
        ),
        check_vma=False,
    )
```

```python
import functools

import jax
import jax.numpy as jnp
import numpy as np
from jax import lax
from jax.experimental import pallas as pl
from jax.experimental.layout import Layout, with_layout_constraint
from jax.experimental.pallas import tpu as pltpu
from jax.sharding import PartitionSpec as P

EPS = 1e-06
BF = jnp.bfloat16
F32 = jnp.float32
VMEM_LIMIT = 58 * 1024 * 1024
NT = (((1,), (1,)), ((), ()))
TN = (((0,), (0,)), ((), ()))


COST = pl.CostEstimate(flops=1, bytes_accessed=1, transcendentals=0)


def dot(a, b, dims=(((1,), (0,)), ((), ()))):
    return lax.dot_general(a, b, dims, preferred_element_type=F32)


def params():
    return pltpu.CompilerParams(vmem_limit_bytes=VMEM_LIMIT)


def split2(v):
    hi = v.astype(BF)
    return hi, (v - hi.astype(F32)).astype(BF)


def split3(v):
    hi = v.astype(BF)
    rest = v - hi.astype(F32)
    mid = rest.astype(BF)
    return hi, mid, (rest - mid.astype(F32)).astype(BF)


def lanes(shape):
    return lax.broadcasted_iota(jnp.int32, shape, len(shape) - 1)


def rows_of(shape):
    return lax.broadcasted_iota(jnp.int32, shape, 0)


def const(array, dtype=BF):
    return jnp.asarray(array.astype(np.float32), dtype)


def full(shape):
    return pl.BlockSpec(shape, lambda *_: tuple(0 for _ in shape), pipeline_mode=pl.Buffered(1))


ANY = pl.BlockSpec(memory_space=pl.ANY)
SMEM = pl.BlockSpec(memory_space=pltpu.SMEM)


def pre_kernel(
    heads, spots, me_ref, x_ref, ba_ref, g64_ref, tri_ref, mq_ref, mk_ref, rows_ref, gqk_ref, *refs,
):
    pieces, refs = refs[: len(spots)], refs[len(spots) :]
    (hn_ref, w_ref, gain_ref, q8_ref, kn_ref, vl_ref, aq_ref, ak_ref, og_ref, q_ref, ks_ref, kd_ref, vd_ref, lg_ref,
     gain_s, carry_k, carry_v, carry_c, w_s, sems) = refs
    keep = pltpu.make_async_copy(w_s, w_ref, sems.at[len(spots)])
    step = pl.program_id(0)
    width = q8_ref.shape[1]
    wide = 4 * width

    @pl.when(step == 0)
    def _():
        copies = []
        for i, (far, start, count, cut) in enumerate(spots):
            row = pl.multiple_of((me_ref[0] ^ far) * cut + start, 16)
            copies.append(pltpu.make_async_copy(pieces[i], w_s.at[pl.ds(row, count), :], sems.at[i]))
        for copy in copies:
            copy.start()
        for copy in copies:
            copy.wait()
        keep.start()
        pick = (lanes((8, 128)) == 3 * heads + rows_of((8, 128))).astype(F32)
        pick = jnp.where(rows_of((8, 128)) < 2, pick, 0.0).astype(BF)
        gain_s[...] = dot(pick, w_s[:, wide:], NT)
        carry_k[...] = jnp.zeros_like(carry_k)
        carry_v[...] = jnp.zeros_like(carry_v)
        carry_c[...] = jnp.zeros_like(carry_c)
        gain_ref[...] = gain_s[...]

    x = x_ref[...].astype(F32)
    factor = lax.rsqrt(jnp.mean(x * x, -1, keepdims=True) + EPS)
    hn = (x * factor * gain_s[0:1, :]).astype(BF)
    hn_ref[...] = hn
    proj = dot(hn, w_s[...])
    q = proj[:, :width]
    k = proj[:, width : 2 * width]
    v = proj[:, 2 * width : 3 * width]
    og_ref[...] = jax.nn.sigmoid(proj[:, 3 * width : wide])
    logits = proj[:, wide:]
    lg_ref[...] = logits
    mix = dot(jnp.concatenate(split2(jax.nn.sigmoid(logits)), 1), ba_ref[...])
    first = rows_of(k.shape) == 0
    kd = jnp.where(first, carry_k[0:1, :], pltpu.roll(k, 1, 0)) - k
    vd = jnp.where(first, carry_v[0:1, :], pltpu.roll(v, 1, 0)) - v
    last = k.shape[0] - 1
    carry_k[0:1, :] = k[last:, :]
    carry_v[0:1, :] = v[last:, :]
    ks = k + mix[:, :width] * kd
    vl_ref[...] = (v + mix[:, width:] * vd).astype(BF)
    q_ref[...] = q.astype(BF)
    ks_ref[...] = ks.astype(BF)
    kd_ref[...] = kd.astype(BF)
    vd_ref[...] = vd.astype(BF)
    rq = lax.rsqrt(dot((q * q).astype(BF), g64_ref[...]) + EPS)
    rk = lax.rsqrt(dot((ks * ks).astype(BF), g64_ref[...]) + EPS)
    q8_ref[...] = ((q * rq * gqk_ref[0:1, :]).astype(BF).astype(F32) * 0.125).astype(BF)
    kn_ref[...] = (ks * rk * gqk_ref[1:2, :]).astype(BF)
    z = logits + rows_ref[0:1, :]
    ls = jnp.minimum(z, 0.0) - jnp.log1p(jnp.exp(-jnp.abs(z)))
    sums = dot(tri_ref[...], jnp.concatenate(split3(ls), 1))
    cum = sums[:, :128] + sums[:, 128:256] + sums[:, 256:] + carry_c[0:1, :]
    carry_c[0:1, :] = cum[last:, :]
    parts = jnp.concatenate(split3(cum), 1)
    aq_ref[...] = (dot(parts, mq_ref[...]) + rows_ref[1:2, :]).astype(BF)
    ak_ref[...] = (dot(parts, mk_ref[...]) + rows_ref[2:3, :]).astype(BF)

    @pl.when(step == pl.num_programs(0) - 1)
    def _():
        keep.wait()


def pre(x, place, pieces, bias_row, gqk, heads):
    seq, model = x.shape
    cut = pieces[0, 0].shape[0]
    spots = [(far, start, p.shape[0], cut) for (far, start), p in sorted(pieces.items())]
    wide = pieces[0, 0].shape[1]
    width = (wide - 128) // 4
    block = min(256, seq)
    ba = np.zeros((256, 2 * width))
    for lane in range(2 * width):
        head = (lane % width) // 64 + (lane // width) * heads
        ba[head, lane] = ba[128 + head, lane] = 1.0
    g64 = np.kron(np.eye(width // 64), np.full((64, 64), 1 / 64))
    tri = np.tril(np.ones((block, block)))
    mq, mk = np.zeros((384, 128)), np.zeros((384, 128))
    ones_q, ones_k = np.zeros((1, 128)), np.zeros((1, 128))
    for head in range(heads):
        for piece in range(3):
            mq[128 * piece + 2 * heads + head, 6 * head + piece] = 1.0
            mk[128 * piece + 2 * heads + head, 6 * head + 3 + piece] = -1.0
            ones_q[0, 6 * head + 3 + piece] = 1.0
            ones_k[0, 6 * head + piece] = 1.0
    rows = jnp.concatenate([bias_row, const(ones_q, F32), const(ones_k, F32), jnp.zeros((5, 128), F32)], 0)

    def row(cols):
        return pl.BlockSpec((block, cols), lambda i: (i, 0))

    def shape(cols, dtype):
        return jax.ShapeDtypeStruct((seq, cols), dtype)

    return pl.pallas_call(
        functools.partial(pre_kernel, heads, spots),
        grid=(seq // block,),
        in_specs=[SMEM, row(model), full(ba.shape), full(g64.shape), full(tri.shape), full(mq.shape), full(mk.shape),
                  full((8, 128)), full(gqk.shape)] + [ANY] * len(spots),
        out_specs=[row(model), ANY, full((8, model))] + [row(width)] * 3 + [row(128)] * 2 + [row(width)] * 5 + [row(128)],
        out_shape=[shape(model, BF), jax.ShapeDtypeStruct((model, wide), BF), jax.ShapeDtypeStruct((8, model), F32)]
        + [shape(width, BF)] * 3
        + [shape(128, BF)] * 2 + [shape(width, F32)] + [shape(width, BF)] * 4 + [shape(128, F32)],
        scratch_shapes=[pltpu.VMEM((8, model), F32), pltpu.VMEM((8, width), F32), pltpu.VMEM((8, width), F32),
                        pltpu.VMEM((8, 128), F32), pltpu.VMEM((model, wide), BF),
                        pltpu.SemaphoreType.DMA((len(spots) + 1,))],
        compiler_params=params(),
        cost_estimate=COST,
        name="pre",
    )(place, x, const(ba), const(g64), const(tri), const(mq), const(mk), rows, gqk,
      *[p for _, p in sorted(pieces.items())])


def fwd_kernel(chunk, block, q_ref, aq_ref, k_ref, ak_ref, v_ref, og_ref, *refs):
    u_ref, att_ref, li_ref = refs[-3:]
    pair = pl.program_id(0)
    q, aq = q_ref[...], aq_ref[...]
    lane = lanes(q.shape)
    ones = jnp.ones((block, 128), BF)
    fine = block // 2
    out = []
    for side in range(2):
        head = 2 * pair + side
        mine = (lane >= 64 * side) & (lane < 64 * side + 64)
        aug = (lane >= 6 * head) & (lane < 6 * head + 6)
        zero = jnp.zeros_like(q)
        qa = jnp.concatenate([jnp.where(mine, q, zero), jnp.where(aug, aq, zero)], 1)
        acc = jnp.zeros((block, 256), F32)
        for j in range(chunk):
            at = slice(j * block, (j + 1) * block)
            e = jnp.exp(dot(qa, jnp.concatenate([k_ref[at, :], ak_ref[at, :]], 1), NT))
            acc = acc + dot(e.astype(BF), jnp.concatenate([v_ref[at, :], ones], 1))
        tops = []
        for begin in range(0, block, fine):
            at = slice(chunk * block, chunk * block + begin + fine)
            rows = slice(begin, begin + fine)
            e = jnp.exp(dot(qa[rows], jnp.concatenate([k_ref[at, :], ak_ref[at, :]], 1), NT))
            e = jnp.where(rows_of(e.shape) + begin >= lanes(e.shape), e, 0.0)
            tops.append(acc[rows] + dot(e.astype(BF), jnp.concatenate([v_ref[at, :], ones[: begin + fine]], 1)))
        out.append(jnp.concatenate(tops, 0))
    low = lane < 64
    total = jnp.where(low, out[0][:, 128:], out[1][:, 128:])
    inverse = 1.0 / total
    att = jnp.where(low, out[0][:, :128], out[1][:, :128]) * inverse
    u_ref[...] = (att * og_ref[...]).astype(BF)
    att_ref[...] = att
    li_ref[...] = inverse


def attend(chunk, block, q8, aq, kn, ak, vl, og, kept):
    seq, width = q8.shape
    keys = (chunk + 1) * block
    grid = (width // 128,)
    mine = pl.BlockSpec((block, 128), lambda p: (chunk, p))
    other = pl.BlockSpec((keys, 128), lambda p: (0, p))
    return pl.pallas_call(
        functools.partial(fwd_kernel, chunk, block),
        grid=grid,
        in_specs=[mine, pl.BlockSpec((block, 128), lambda p: (chunk, 0)), other,
                  pl.BlockSpec((keys, 128), lambda p: (0, 0)), other, mine] + [ANY] * len(kept),
        out_specs=[pl.BlockSpec((block, 128), lambda p: (0, p)), mine, mine],
        out_shape=[jax.ShapeDtypeStruct((block, width), BF)] + [jax.ShapeDtypeStruct((seq, width), F32)] * 2,
        input_output_aliases={6 + i: 1 + i for i in range(len(kept))},
        compiler_params=params(),
        cost_estimate=COST,
        name="attend",
    )(q8, aq, kn, ak, vl, og, *kept)


def ffn_kernel(
    count, chunk, block, step_rows, own, at_ref, x_ref, cot_ref, gain_ref, o_any, f_any, *refs
):
    us, outs = refs[:count], refs[-10 - count : -3]
    o_ref, f_ref, sems = refs[-3:]
    copies = [pltpu.make_async_copy(a, b, sems.at[i]) for i, (a, b) in enumerate(((o_any, o_ref), (f_any, f_ref)))]

    copies[0].start()
    copies[1].start()
    h2_ref, hid_ref, dgu_ref, res_ref, uc_ref, part_ref = outs[:6]
    dus, gmid_ref = outs[6:-1], outs[-1]
    hidden = hid_ref.shape[1]
    gain = gain_ref[1:2, :]
    rows = x_ref.shape[0]
    size = rows // 2
    width = o_ref.shape[1] // count
    subs = [slice(i * size, (i + 1) * size) for i in range(2)]
    y1, n, factor, h2, gu, dhid, hid, dgu, dh2, res = [[None, None] for _ in range(10)]

    def first(i):
        u = jnp.concatenate([r[subs[i], :] for r in us], 1)
        uc_ref[subs[i], :] = u
        y1[i] = x_ref[subs[i], :].astype(F32) + dot(u, o_ref[...], NT)

    def normed(i):
        factor[i] = lax.rsqrt(jnp.mean(y1[i] * y1[i], -1, keepdims=True) + EPS)
        n[i] = y1[i] * factor[i]
        h2[i] = (n[i] * gain).astype(BF)
        h2_ref[subs[i], :] = h2[i]

    def gates(i):
        gu[i] = dot(h2[i], f_ref[:, : 2 * hidden])

    def hidden_back(i):
        dhid[i] = dot(cot_ref[subs[i], :], f_ref[:, 2 * hidden :])

    def activated(i):
        g, up = gu[i][:, :hidden], gu[i][:, hidden:]
        sg = jax.nn.sigmoid(g)
        act = g * sg
        hid[i] = (act * up).astype(BF)
        hid_ref[subs[i], :] = hid[i]
        dg = dhid[i] * up * sg * (1.0 + g * (1.0 - sg))
        dgu[i] = jnp.concatenate([dg.astype(BF), (dhid[i] * act).astype(BF)], 1)
        dgu_ref[subs[i], :] = dgu[i]

    def normed_back(i):
        dh2[i] = dot(dgu[i], f_ref[:, : 2 * hidden], NT)

    def part(i):
        token = chunk * block + pl.program_id(0) * step_rows + i * size + rows_of((size, 1))
        owned = (token >= at_ref[0] * own) & (token < (at_ref[0] + 1) * own)
        total = dot(hid[i], f_ref[:, 2 * hidden :], NT) + jnp.where(owned, y1[i], 0.0)
        part_ref[subs[i], :] = total.astype(BF)

    def residual(i):
        gmid_ref[i : i + 1, :] = jnp.sum(dh2[i] * n[i], 0, keepdims=True)
        wd = gain * dh2[i]
        back = factor[i] * (wd - n[i] * jnp.mean(wd * n[i], -1, keepdims=True))
        res[i] = jnp.where(at_ref[0] == 0, back + cot_ref[subs[i], :].astype(F32), back).astype(BF)
        res_ref[subs[i], :] = res[i]

    def last(i):
        du = dot(res[i], o_ref[...]).astype(BF)
        for s in range(count):
            dus[s][subs[i], :] = du[:, s * width : (s + 1) * width]

    gmid_ref[...] = jnp.zeros_like(gmid_ref)
    copies[0].wait()
    first(0)
    first(1)
    copies[1].wait()
    normed(0)
    hidden_back(0)
    gates(0)
    normed(1)
    hidden_back(1)
    gates(1)
    activated(0)
    normed_back(0)
    activated(1)
    normed_back(1)
    residual(0)
    part(0)
    last(0)
    residual(1)
    part(1)
    last(1)


def feed(chunk, block, own, place, x, cot, gains, o, f, us, kept):
    seq, model = x.shape
    hidden = f.shape[1] // 3
    count = len(us)
    width = us[0].shape[1]
    step_rows = block
    per = 1

    def mine(cols):
        return pl.BlockSpec((step_rows, cols), lambda i: (chunk * per + i, 0))

    def local(cols):
        return pl.BlockSpec((step_rows, cols), lambda i: (i, 0))

    kept_cols = [model, hidden, 2 * hidden, model, count * width, model]
    return pl.pallas_call(
        functools.partial(ffn_kernel, count, chunk, block, step_rows, own),
        grid=(per,),
        in_specs=[SMEM, mine(model), mine(model), full(gains.shape), ANY, ANY]
        + [local(width)] * count + [ANY] * len(kept),
        out_specs=[mine(c) for c in kept_cols] + [local(width)] * count + [full((8, model))],
        out_shape=[jax.ShapeDtypeStruct((seq, c), BF) for c in kept_cols]
        + [jax.ShapeDtypeStruct((block, width), BF)] * count + [jax.ShapeDtypeStruct((8, model), F32)],
        scratch_shapes=[pltpu.VMEM(o.shape, BF), pltpu.VMEM(f.shape, BF), pltpu.SemaphoreType.DMA((2,))],
        input_output_aliases={6 + count + i: i for i in range(len(kept))},
        compiler_params=params(),
        cost_estimate=COST,
        name="feed",
    )(place, x, cot, gains, o, f, *us, *kept)


def bwd_kernel(
    begin, heads, block, q_ref, aq_ref, k_ref, ak_ref, v_ref, og_ref, att_ref, li_ref, du_ref, ms_ref,
    dq_ref, dk_ref, dv_ref, dc_ref, da_s, ad_s,
):
    pair = begin + pl.program_id(0)
    seq = q_ref.shape[0]
    count = seq // block
    lane = lanes((block, 128))
    zero = jnp.zeros((block, 128), BF)
    ones = jnp.ones((block, 128), BF)
    third = lane - 3 * (lane // 3)
    for i in range(count):
        at = slice(i * block, (i + 1) * block)
        da = (du_ref[at, :].astype(F32) * og_ref[at, :] * li_ref[at, :]).astype(BF)
        da_s[at, :] = da
        delta = dot(jnp.concatenate(split2(da.astype(F32) * att_ref[at, :]), 1), ms_ref[...])
        hi, mid, rest = split3(-delta)
        ad_s[at, :] = jnp.where(third == 0, hi, jnp.where(third == 1, mid, rest))
    dk_ref[...] = jnp.zeros_like(dk_ref)
    dv_ref[...] = jnp.zeros_like(dv_ref)

    @pl.when(pl.program_id(0) == 0)
    def _():
        dc_ref[...] = jnp.zeros_like(dc_ref)


    vone = jnp.where(lane < 6, ones, zero)
    for i in range(count):
        at = slice(i * block, (i + 1) * block)
        q, aq, da, ad = q_ref[at, :], aq_ref[at, :], da_s[at, :], ad_s[at, :]
        dq = []
        for side in range(2):
            head = 2 * pair + side
            mine = (lane >= 64 * side) & (lane < 64 * side + 64)
            aug = (lane >= 6 * head) & (lane < 6 * head + 6)
            column = lane == 2 * heads + head
            qh = jnp.where(mine, q, zero)
            qa = jnp.concatenate([qh, jnp.where(aug, aq, zero)], 1)
            qo = jnp.concatenate([qh, ones], 1)
            dah = jnp.where(mine, da, zero)
            daa = jnp.concatenate([dah, jnp.where((lane >= 3 * side) & (lane < 3 * side + 3), ad, zero)], 1)
            acc = jnp.zeros((block, 256), F32)

            def pair_of(to, first):
                size = to.stop - to.start
                k = k_ref[to, :]
                e = jnp.exp(dot(jnp.concatenate([k, ak_ref[to, :]], 1), qa[first:], NT))
                if to.stop > i * block:
                    shift = to.start - i * block - first
                    e = jnp.where(rows_of(e.shape) + shift <= lanes(e.shape), e, 0.0)
                dv_ref[to, :] += dot(e.astype(BF), dah[first:])
                ds = (e * dot(jnp.concatenate([v_ref[to, :], vone[:size]], 1), daa[first:], NT)).astype(BF)
                dk = dot(ds, qo[first:])
                dk_ref[to, :] += dk[:, :128]
                dc_ref[to, :] -= jnp.where(column[:size], dk[:, 128:], 0.0)
                return dot(ds, jnp.concatenate([k, ones[:size]], 1), TN)

            for j in range(i):
                acc = acc + pair_of(slice(j * block, (j + 1) * block), 0)
            half = block // 2
            acc = acc + pair_of(slice(i * block, i * block + half), 0)
            acc = jnp.concatenate(
                [acc[:half], acc[half:] + pair_of(slice(i * block + half, (i + 1) * block), half)], 0
            )
            dq.append(acc[:, :128])
            dc_ref[at, :] += jnp.where(column, acc[:, 128:], 0.0)
        dq_ref[at, :] = jnp.where(lane < 64, dq[0], dq[1]) * 0.125


def attend_back(begin, end, block, heads, q8, aq, kn, ak, vl, og, att, li, du):
    seq, width = q8.shape
    ms = np.zeros((256, 128))
    for lane in range(256):
        ms[lane, 3 * ((lane % 128) // 64) : 3 * ((lane % 128) // 64) + 3] = 1.0
    mine = pl.BlockSpec((seq, 128), lambda p: (0, begin + p))
    own = pl.BlockSpec((seq, 128), lambda p: (0, p))
    one = pl.BlockSpec((seq, 128), lambda p: (0, 0))
    return pl.pallas_call(
        functools.partial(bwd_kernel, begin, heads, block),
        grid=(end - begin,),
        in_specs=[mine, one, mine, one, mine, mine, mine, mine, mine, full((256, 128))],
        out_specs=[own, own, own, one],
        out_shape=[jax.ShapeDtypeStruct((seq, 128 * (end - begin)), F32)] * 3 + [jax.ShapeDtypeStruct((seq, 128), F32)],
        scratch_shapes=[pltpu.VMEM((seq, 128), BF), pltpu.VMEM((seq, 128), BF)],
        compiler_params=params(),
        cost_estimate=COST,
        name="attend_back",
    )(q8, aq, kn, ak, vl, og, att, li, du, const(ms))


def post_kernel(
    heads, groups, q_ref, ks_ref, kd_ref, vd_ref, lg_ref, du_ref, att_ref, og_ref, x_ref,
    res_ref, gain_ref, w_ref, ba_ref, g64_ref, tri_ref, ms_ref, rows_ref, gqk_ref, *refs,
):
    grads, refs = refs[: 4 * groups], refs[4 * groups :]
    dp_ref, gt_ref, g0_ref, gq_ref, gb_ref, carry_k, carry_v, carry_c, w_s, sem = refs
    dq_raw, dk_raw, dvs = [
        jnp.concatenate([r[...] for r in grads[i * groups : (i + 1) * groups]], 1) for i in range(3)
    ]
    dc = sum(r[...] for r in grads[3 * groups :])
    step = pl.program_id(0)
    rows, width = q_ref.shape

    move = pltpu.make_async_copy(w_ref, w_s, sem)

    @pl.when(step == 0)
    def _():
        move.start()
        carry_k[...] = jnp.zeros_like(carry_k)
        carry_v[...] = jnp.zeros_like(carry_v)
        carry_c[...] = jnp.zeros_like(carry_c)
        g0_ref[...] = jnp.zeros_like(g0_ref)
        gq_ref[...] = jnp.zeros_like(gq_ref)
        gb_ref[...] = jnp.zeros_like(gb_ref)

    def norm_back(raw, gain, grad):
        r = lax.rsqrt(dot((raw * raw).astype(BF), g64_ref[...]) + EPS)
        n = raw * r
        wd = grad * gain
        return r * (wd - n * dot((wd * n).astype(BF), g64_ref[...])), jnp.sum(grad * n, 0, keepdims=True)

    dq, gq = norm_back(q_ref[...].astype(F32), gqk_ref[0:1, :], dq_raw)
    dks, gk = norm_back(ks_ref[...].astype(F32), gqk_ref[1:2, :], dk_raw)
    gq_ref[0:1, :] += gq
    gq_ref[1:2, :] += gk
    logits = lg_ref[...]
    sg = jax.nn.sigmoid(logits)
    mix = dot(jnp.concatenate(split2(sg), 1), ba_ref[...])
    end = rows_of(dks.shape) == rows - 1

    def shift_back(grad, part, carry):
        w = part * grad
        later = jnp.where(end, carry[0:1, :], pltpu.roll(w, rows - 1, 0))
        carry[0:1, :] = w[0:1, :]
        return grad - w + later

    dk = shift_back(dks, mix[:, :width], carry_k)
    dv = shift_back(dvs, mix[:, width:], carry_v)
    terms = jnp.concatenate([dks * kd_ref[...].astype(F32), dvs * vd_ref[...].astype(F32)], 1)
    hi, rest = split2(terms)
    dmix = dot(hi, ms_ref[...]) + dot(rest, ms_ref[...])
    sums = dot(tri_ref[...], jnp.concatenate(split3(dc), 1))
    dls = sums[:, :128] + sums[:, 128:256] + sums[:, 256:] + carry_c[0:1, :]
    carry_c[0:1, :] = dls[0:1, :]
    lane = lanes(logits.shape)
    dz = dls * jax.nn.sigmoid(-(logits + rows_ref[0:1, :]))
    dgl = jnp.where(lane < 2 * heads, dmix * sg * (1.0 - sg), jnp.where(lane < 3 * heads, dz, 0.0))
    gb_ref[0:1, :] += jnp.sum(dgl, 0, keepdims=True)
    og = og_ref[...]
    do = du_ref[...].astype(F32) * att_ref[...] * og * (1.0 - og)
    dp = jnp.concatenate([dq.astype(BF), dk.astype(BF), dv.astype(BF), do.astype(BF), dgl.astype(BF)], 1)
    dp_ref[...] = dp

    @pl.when(step == 0)
    def _():
        move.wait()

    dhn = dot(dp, w_s[...], NT)
    x = x_ref[...].astype(F32)
    factor = lax.rsqrt(jnp.mean(x * x, -1, keepdims=True) + EPS)
    n = x * factor
    g0_ref[0:1, :] += jnp.sum(dhn * n, 0, keepdims=True)
    wd = dhn * gain_ref[0:1, :]
    back = factor * (wd - n * jnp.mean(wd * n, -1, keepdims=True))
    gt_ref[...] = (back + res_ref[...].astype(F32)).astype(BF)


def post(heads, dq, dk, dv, dc, q, ks, kd, vd, lg, du, att, og, x, res, gains, w, bias_row, gqk):
    seq, width = q.shape
    groups = len(dq)
    model = x.shape[1]
    wide = w.shape[1]
    block = min(256, seq)
    count = seq // block
    ba = np.zeros((256, 2 * width))
    ms = np.zeros((2 * width, 128))
    for lane in range(2 * width):
        head = (lane % width) // 64 + (lane // width) * heads
        ba[head, lane] = ba[128 + head, lane] = 1.0
        ms[lane, head] = 1.0
    g64 = np.kron(np.eye(width // 64), np.full((64, 64), 1 / 64))
    tri = np.triu(np.ones((block, block)))
    rows = jnp.concatenate([bias_row, jnp.zeros((7, 128), F32)], 0)

    def row(cols):
        return pl.BlockSpec((block, cols), lambda i: (count - 1 - i, 0))

    return pl.pallas_call(
        functools.partial(post_kernel, heads, groups),
        grid=(count,),
        in_specs=[row(width)] * 4 + [row(128)] + [row(width)] * 3 + [row(model)] * 2
        + [full(gains.shape), ANY, full(ba.shape), full(g64.shape), full(tri.shape),
           full(ms.shape), full((8, 128)), full(gqk.shape)] + [row(g.shape[1]) for g in dq + dk + dv + dc],
        out_specs=[row(wide), row(model), full((8, model)), full((8, width)), full((8, 128))],
        out_shape=[jax.ShapeDtypeStruct((seq, wide), BF), jax.ShapeDtypeStruct((seq, model), BF),
                   jax.ShapeDtypeStruct((8, model), F32), jax.ShapeDtypeStruct((8, width), F32),
                   jax.ShapeDtypeStruct((8, 128), F32)],
        scratch_shapes=[pltpu.VMEM((8, width), F32), pltpu.VMEM((8, width), F32), pltpu.VMEM((8, 128), F32),
                        pltpu.VMEM(w.shape, BF), pltpu.SemaphoreType.DMA],
        compiler_params=params(),
        cost_estimate=COST,
        name="post",
    )(q, ks, kd, vd, lg, du, att, og, x, res, gains, w, const(ba), const(g64), const(tri),
      const(ms), rows, gqk, *dq, *dk, *dv, *dc)


def swap(value, axis, bit):
    size = lax.axis_size(axis)
    return lax.ppermute(value, axis, [(i, i ^ bit) for i in range(size)])


def turn(value):
    size = lax.axis_size("tp")
    return lax.ppermute(value, "tp", [(i, (i + 1) % size) for i in range(size)])


def add(a, b):
    return (a.astype(F32) + b.astype(F32)).astype(BF)


def high_bits(size):
    bits, bit = [], 2
    while bit < size:
        bits.append(bit)
        bit *= 2
    return bits


def gather_1(shard):
    pieces = {(0, 0): shard, (2, 0): swap(shard, "dp", 2)}
    if lax.axis_size("dp") == 8:
        pieces[4, 0] = swap(shard, "dp", 4)
    pieces[1, 0] = swap(shard, "dp", 1)
    return pieces


def gather_2(pieces):
    size = lax.axis_size("dp")
    pieces = dict(pieces)
    if size == 8:
        half = pieces[0, 0].shape[0] // 2
        pieces[6, 0] = swap(pieces[2, 0][:half], "dp", 4)
        pieces[6, half] = swap(pieces[4, 0][half:], "dp", 2)
        pieces[3, 0] = swap(pieces[2, 0], "dp", 1)
        pieces[5, 0] = swap(pieces[4, 0], "dp", 1)
        return pieces
    for bit in high_bits(size)[1:]:
        pieces.update({(r | bit, 0): swap(p, "dp", bit) for (r, _), p in list(pieces.items()) if not r & 1})
    return pieces


def gather_3(pieces):
    pieces = dict(pieces)
    pieces.update({(r | 1, s): swap(p, "dp", 1) for (r, s), p in list(pieces.items()) if (r | 1, s) not in pieces})
    return pieces


def assemble(pieces, me):
    cut, cols = pieces[0, 0].shape
    whole = jnp.zeros((cut * lax.axis_size("dp"), cols), BF)
    for (far, start), piece in sorted(pieces.items()):
        whole = lax.dynamic_update_slice_in_dim(whole, piece, (me ^ far) * cut + start, 0)
    return whole


def rows_major(value):
    return with_layout_constraint(value, Layout(major_to_minor=(0, 1)))


def scatter(whole):
    return lax.psum_scatter(whole, "dp", scatter_dimension=0, tiled=True)


def total_of(terms):
    return sum(term.astype(F32) for term in terms)


tie = lax.optimization_barrier


def pad_to(value, size, axis):
    extra = size - value.shape[axis]
    if not extra:
        return value
    return jnp.pad(value, [(0, extra if a == axis else 0) for a in range(value.ndim)])


def shards(
    tokens, attn_in, head_gates, out_proj, norm_gains, qk_gains, forget_bias, gate_up, down_proj, carried_offset,
    reset_flag, cotangent,
):
    dp, tp = lax.axis_size("dp"), lax.axis_size("tp")
    me_d, me_t = lax.axis_index("dp"), lax.axis_index("tp")
    _, seq, model = tokens.shape
    own = seq // tp
    cut = attn_in.shape[1]
    width_real = attn_in.shape[2]
    heads_real = head_gates.shape[2]
    heads = heads_real + heads_real % 2
    width = 64 * heads
    hidden = gate_up.shape[2]
    block = 512 if seq % 512 == 0 else seq
    chunks = seq // block

    attn_rows = jnp.transpose(pad_to(attn_in, width, 2), (1, 0, 2)).reshape(cut, 4 * width)
    gate_rows = jnp.transpose(pad_to(head_gates, heads, 2), (1, 0, 2)).reshape(cut, 3 * heads)
    gate_rows = pad_to(jnp.concatenate([gate_rows, jnp.transpose(norm_gains)], 1), 128, 1)
    attn_rows = jnp.concatenate([attn_rows, gate_rows], 1)
    out_own = pad_to(jnp.transpose(out_proj), width, 1)
    ffn_rows = jnp.concatenate([gate_up[0], gate_up[1], jnp.transpose(down_proj)], 1)

    bias = lax.dynamic_slice_in_dim(forget_bias.astype(F32), me_t * heads_real, heads_real, 0)
    offset = lax.dynamic_slice_in_dim(carried_offset[0], me_t * heads_real, heads_real, 0)
    bias = bias + (1 - reset_flag[0]).astype(F32) * offset
    bias_row = jnp.pad(bias, (2 * heads, 128 - 2 * heads - heads_real))[None, :]
    gqk = pad_to(jnp.tile(qk_gains.astype(F32), (1, heads)), 8, 0)
    at = me_t.astype(jnp.int32)[None]

    here = me_d.astype(jnp.int32)[None]
    x, cot = tokens[0], cotangent[0]

    def token_part(values, s):
        return lax.dynamic_slice_in_dim(values, lax.rem(me_t - s + tp, tp) * own, own, 0)

    def product(left, right):
        return dot(left, right, TN).astype(BF)

    attn_p = gather_1(attn_rows)
    out_rows = [out_own, turn(out_own)]
    while len(out_rows) < tp - 1:
        out_rows.append(turn(out_rows[-1]))
    attn_p, out_rows, ffn_rows = tie((attn_p, out_rows, ffn_rows))
    attn_p = gather_2(attn_p)
    out_rows.append(turn(out_rows[-1]))
    attn_p, out_rows, ffn_rows = tie((attn_p, out_rows, ffn_rows))
    out_whole = jnp.concatenate(out_rows, 1)
    attn_p, out_whole, ffn_rows = tie((attn_p, out_whole, ffn_rows))
    ffn_all = lax.all_gather(ffn_rows, "dp", axis=0, tiled=True)
    out_p = gather_1(out_whole)
    attn_p = gather_3(attn_p)
    hn, w, gains, q8, kn, vl, aq, ak, og, q, ks, kd, vd, lg = pre(x, here, attn_p, bias_row, gqk, heads)
    q8, out_p = tie((q8, out_p))
    out_p = gather_2(out_p)
    u, *kept_att = attend(0, block, q8, aq, kn, ak, vl, og, ())
    u, kept_att, q8 = tie((u, kept_att, q8))
    us = [[u]]

    first = tp - 1
    kept_ffn, gmids = (), []
    parts, got = [None] * chunks, [None] * chunks

    made = first + chunks
    sums = []
    out_all = None
    for t in range(first + chunks - 1 + first + 1):
        send = {}
        for c in range(chunks):
            step = t - first - c
            if 1 <= step <= first:
                send[c] = parts[c][1] if step == 1 else add(got[c], parts[c][step])
        y_send = token_part(kept_ffn[5], 1) if t == made + first - 1 else None
        send, q8, kept_ffn, x, y_send = tie((send, q8, kept_ffn, x, y_send))
        new_u = {c: turn(us[c][-1]) for c in range(len(us)) if 1 <= t - c + 1 <= first}
        new_du = {c: turn(value) for c, value in send.items()}
        fresh = None
        if t + 1 < chunks:
            fresh, *kept_att = attend(t + 1, block, q8, aq, kn, ak, vl, og, kept_att)
        if t == 1:
            out_p = gather_3(out_p)
        if t == 2:
            out_all = assemble(out_p, me_d)
        chunk = t - first
        if 0 <= chunk < chunks:
            outs = feed(chunk, block, own, at, x, cot, gains, out_all, ffn_all, us[chunk], kept_ffn)
            kept_ffn, parts[chunk] = outs[:6], outs[6:-1]
            gmids.append(outs[-1][0:1] + outs[-1][1:2])
        h2, hid, dgu, res, uc, part = kept_ffn if kept_ffn else [None] * 6
        if t == made + first - 1:
            y_acc = turn(y_send)
        fill = []
        if t == made:
            fill = [product(res, uc), rows_major(product(cot, hid))]
        if t == made + 1:
            fill = [product(h2, dgu)]
        out_q, out_p = out_p, None if t == 0 else out_p
        new_u, new_du, fresh, kept_att, kept_ffn, parts, fill, out_p, out_all, q8 = tie(
            (new_u, new_du, fresh, kept_att, kept_ffn, parts, fill, out_p, out_all, q8)
        )
        if t == 0:
            out_p = out_q
        sums += [scatter(value) for value in fill]
        for c, value in new_u.items():
            us[c].append(value)
        if fresh is not None:
            us.append([fresh])
        got = [new_du.get(c, got[c]) for c in range(chunks)]
    att, li = kept_att
    h2, hid, dgu, res, uc, part = kept_ffn

    du = jnp.concatenate([add(got[c], parts[c][0]) for c in range(chunks)], 0)
    du, gmid = tie((du, sum(gmids)))
    pairs, back_parts = width // 128, []
    cuts = [0, 1, pairs] if pairs > 1 else [0, pairs]
    y_step = 2
    ring = out_acc = None
    for begin, end in zip(cuts, cuts[1:]):
        back_parts.append(attend_back(begin, end, block, heads, q8, aq, kn, ak, vl, og, att, li, du))
        y_acc, back_parts = tie((y_acc, back_parts))
        if y_step < tp:
            send, y_step = add(y_acc, token_part(part, y_step)), y_step + 1
            if ring is None:
                ring, out_step = [sums[0][:, i * width : (i + 1) * width] for i in range(tp)], 2
                send, du, ring = tie((send, du, ring))
                out_acc = turn(ring[1])
            else:
                send, du = tie((send, du))
            y_acc = turn(send)
    dq, dk, dv, dc = zip(*back_parts)
    dp_all, gt, g0, gq, gb = post(
        heads, dq, dk, dv, dc, q, ks, kd, vd, lg, du, att, og, x, res, gains, w, bias_row, gqk
    )
    y_acc, dp_all, gt, g0, out_acc = tie((y_acc, dp_all, gt, g0, out_acc))

    send = token_part(gt, 1)
    send, dp_all, y_acc, out_acc = tie((send, dp_all, y_acc, out_acc))
    back = turn(send)
    fill = product(hn, dp_all)
    back, fill, g0, gq, gb = tie((back, fill, g0, gq, gb))
    sums.append(scatter(fill))
    while y_step < tp:
        y_acc, y_step = turn(add(y_acc, token_part(part, y_step))), y_step + 1
    gq = gq[0:2].reshape(2, heads, 64).sum(1)
    gb = lax.dynamic_update_slice_in_dim(
        jnp.zeros(forget_bias.shape, F32), gb[0, 2 * heads : 2 * heads + heads_real], me_t * heads_real, 0
    )
    small = jnp.concatenate([gq.reshape(-1), gb])
    small = jnp.pad(small, (0, model - small.shape[0]))[None]
    hops = [("dp", 1 << i) for i in range(dp.bit_length() - 1)]
    flat = None
    for s in range(2, tp):
        send = add(back, token_part(gt, s))
        out_send = None
        if flat is None:
            flat = jnp.concatenate([g0[0:1], gmid, small, jnp.zeros((5, model), F32)], 0)
        elif out_step < tp:
            out_send, out_step = add(out_acc, ring[out_step]), out_step + 1
        send, flat, out_send, y_acc = tie((send, flat, out_send, y_acc))
        back = turn(send)
        if out_send is not None:
            out_acc = turn(out_send)
        for _ in range(2):
            if hops:
                flat = flat + swap(flat, *hops.pop(0))
        back, flat, out_acc = tie((back, flat, out_acc))
    while out_step < tp:
        out_acc, out_step = turn(add(out_acc, ring[out_step])), out_step + 1
    for axis, bit in hops + [("tp", 1 << i) for i in range(tp.bit_length() - 1)]:
        flat = flat + swap(flat, axis, bit)
    result, back, gt = tie((total_of((y_acc, token_part(part, 0))).astype(BF), back, gt))
    grad_tokens = total_of((token_part(gt, 0), back))
    grad_down, grad_gu, grad_attn = [value.astype(F32) for value in sums[1:]]
    grad_out_own = total_of((ring[0], out_acc))
    norm_grad = flat[0:2]
    qk_grad = flat[2, : 2 * 64].reshape(2, 64)
    bias_grad = flat[2, 2 * 64 : 2 * 64 + forget_bias.shape[0]]

    grad_attn_in = jnp.transpose(grad_attn[:, : 4 * width].reshape(cut, 4, width)[:, :, :width_real], (1, 0, 2))
    grad_gates = grad_attn[:, 4 * width : 4 * width + 3 * heads].reshape(cut, 3, heads)[:, :, :heads_real]
    return (
        result[None],
        grad_tokens[None],
        grad_attn_in,
        jnp.transpose(grad_gates, (1, 0, 2)),
        jnp.transpose(grad_out_own[:, :width_real]),
        jnp.stack([grad_gu[:, :hidden], grad_gu[:, hidden:]]),
        jnp.transpose(grad_down),
        norm_grad,
        qk_grad,
        bias_grad,
    )


def solution(mesh):
    return jax.shard_map(
        shards,
        mesh=mesh,
        in_specs=(
            P("dp", None, None), P(None, "dp", "tp"), P(None, "dp", "tp"), P("tp", "dp"), P(None, "dp"), P(), P(),
            P(None, "dp", "tp"), P("tp", "dp"), P("dp", None), P("dp"), P("dp", None, None),
        ),
        out_specs=(
            P("dp", "tp", None), P("dp", "tp", None), P(None, "dp", "tp"), P(None, "dp", "tp"), P("tp", "dp"),
            P(None, "dp", "tp"), P("tp", "dp"), P(), P(), P(),
        ),
        check_vma=False,
    )
```

```python
import functools

import jax
import jax.numpy as jnp
import numpy as np
from jax import lax
from jax.experimental import pallas as pl
from jax.experimental.layout import Layout, with_layout_constraint
from jax.experimental.pallas import tpu as pltpu
from jax.sharding import PartitionSpec as P

EPS = 1e-06
BF = jnp.bfloat16
F32 = jnp.float32
VMEM_LIMIT = 58 * 1024 * 1024
NT = (((1,), (1,)), ((), ()))
TN = (((0,), (0,)), ((), ()))


COST = pl.CostEstimate(flops=1, bytes_accessed=1, transcendentals=0)


def dot(a, b, dims=(((1,), (0,)), ((), ()))):
    return lax.dot_general(a, b, dims, preferred_element_type=F32)


def params():
    return pltpu.CompilerParams(vmem_limit_bytes=VMEM_LIMIT)


def split2(v):
    hi = v.astype(BF)
    return hi, (v - hi.astype(F32)).astype(BF)


def split3(v):
    hi = v.astype(BF)
    rest = v - hi.astype(F32)
    mid = rest.astype(BF)
    return hi, mid, (rest - mid.astype(F32)).astype(BF)


def lanes(shape):
    return lax.broadcasted_iota(jnp.int32, shape, len(shape) - 1)


def rows_of(shape):
    return lax.broadcasted_iota(jnp.int32, shape, 0)


def const(array, dtype=BF):
    return jnp.asarray(array.astype(np.float32), dtype)


def full(shape):
    return pl.BlockSpec(shape, lambda *_: tuple(0 for _ in shape), pipeline_mode=pl.Buffered(1))


ANY = pl.BlockSpec(memory_space=pl.ANY)
SMEM = pl.BlockSpec(memory_space=pltpu.SMEM)


def pre_kernel(
    heads, spots, me_ref, x_ref, ba_ref, g64_ref, tri_ref, mq_ref, mk_ref, rows_ref, gqk_ref, *refs,
):
    pieces, refs = refs[: len(spots)], refs[len(spots) :]
    (hn_ref, w_ref, gain_ref, q8_ref, kn_ref, vl_ref, aq_ref, ak_ref, og_ref, q_ref, ks_ref, kd_ref, vd_ref, lg_ref,
     gain_s, carry_k, carry_v, carry_c, w_s, sems) = refs
    keep = pltpu.make_async_copy(w_s, w_ref, sems.at[len(spots)])
    step = pl.program_id(0)
    width = q8_ref.shape[1]
    wide = 4 * width

    @pl.when(step == 0)
    def _():
        copies = []
        for i, (far, start, count, cut) in enumerate(spots):
            row = pl.multiple_of((me_ref[0] ^ far) * cut + start, 16)
            copies.append(pltpu.make_async_copy(pieces[i], w_s.at[pl.ds(row, count), :], sems.at[i]))
        for copy in copies:
            copy.start()
        for copy in copies:
            copy.wait()
        keep.start()
        pick = (lanes((8, 128)) == 3 * heads + rows_of((8, 128))).astype(F32)
        pick = jnp.where(rows_of((8, 128)) < 2, pick, 0.0).astype(BF)
        gain_s[...] = dot(pick, w_s[:, wide:], NT)
        carry_k[...] = jnp.zeros_like(carry_k)
        carry_v[...] = jnp.zeros_like(carry_v)
        carry_c[...] = jnp.zeros_like(carry_c)
        gain_ref[...] = gain_s[...]

    x = x_ref[...].astype(F32)
    factor = lax.rsqrt(jnp.mean(x * x, -1, keepdims=True) + EPS)
    hn = (x * factor * gain_s[0:1, :]).astype(BF)
    hn_ref[...] = hn
    proj = dot(hn, w_s[...])
    q = proj[:, :width]
    k = proj[:, width : 2 * width]
    v = proj[:, 2 * width : 3 * width]
    og_ref[...] = jax.nn.sigmoid(proj[:, 3 * width : wide])
    logits = proj[:, wide:]
    lg_ref[...] = logits
    mix = dot(jnp.concatenate(split2(jax.nn.sigmoid(logits)), 1), ba_ref[...])
    first = rows_of(k.shape) == 0
    kd = jnp.where(first, carry_k[0:1, :], pltpu.roll(k, 1, 0)) - k
    vd = jnp.where(first, carry_v[0:1, :], pltpu.roll(v, 1, 0)) - v
    last = k.shape[0] - 1
    carry_k[0:1, :] = k[last:, :]
    carry_v[0:1, :] = v[last:, :]
    ks = k + mix[:, :width] * kd
    vl_ref[...] = (v + mix[:, width:] * vd).astype(BF)
    q_ref[...] = q.astype(BF)
    ks_ref[...] = ks.astype(BF)
    kd_ref[...] = kd.astype(BF)
    vd_ref[...] = vd.astype(BF)
    rq = lax.rsqrt(dot((q * q).astype(BF), g64_ref[...]) + EPS)
    rk = lax.rsqrt(dot((ks * ks).astype(BF), g64_ref[...]) + EPS)
    q8_ref[...] = ((q * rq * gqk_ref[0:1, :]).astype(BF).astype(F32) * 0.125).astype(BF)
    kn_ref[...] = (ks * rk * gqk_ref[1:2, :]).astype(BF)
    z = logits + rows_ref[0:1, :]
    ls = jnp.minimum(z, 0.0) - jnp.log1p(jnp.exp(-jnp.abs(z)))
    sums = dot(tri_ref[...], jnp.concatenate(split3(ls), 1))
    cum = sums[:, :128] + sums[:, 128:256] + sums[:, 256:] + carry_c[0:1, :]
    carry_c[0:1, :] = cum[last:, :]
    parts = jnp.concatenate(split3(cum), 1)
    aq_ref[...] = (dot(parts, mq_ref[...]) + rows_ref[1:2, :]).astype(BF)
    ak_ref[...] = (dot(parts, mk_ref[...]) + rows_ref[2:3, :]).astype(BF)

    @pl.when(step == pl.num_programs(0) - 1)
    def _():
        keep.wait()


def pre(x, place, pieces, bias_row, gqk, heads):
    seq, model = x.shape
    cut = pieces[0, 0].shape[0]
    spots = [(far, start, p.shape[0], cut) for (far, start), p in sorted(pieces.items())]
    wide = pieces[0, 0].shape[1]
    width = (wide - 128) // 4
    block = min(256, seq)
    ba = np.zeros((256, 2 * width))
    for lane in range(2 * width):
        head = (lane % width) // 64 + (lane // width) * heads
        ba[head, lane] = ba[128 + head, lane] = 1.0
    g64 = np.kron(np.eye(width // 64), np.full((64, 64), 1 / 64))
    tri = np.tril(np.ones((block, block)))
    mq, mk = np.zeros((384, 128)), np.zeros((384, 128))
    ones_q, ones_k = np.zeros((1, 128)), np.zeros((1, 128))
    for head in range(heads):
        for piece in range(3):
            mq[128 * piece + 2 * heads + head, 6 * head + piece] = 1.0
            mk[128 * piece + 2 * heads + head, 6 * head + 3 + piece] = -1.0
            ones_q[0, 6 * head + 3 + piece] = 1.0
            ones_k[0, 6 * head + piece] = 1.0
    rows = jnp.concatenate([bias_row, const(ones_q, F32), const(ones_k, F32), jnp.zeros((5, 128), F32)], 0)

    def row(cols):
        return pl.BlockSpec((block, cols), lambda i: (i, 0))

    def shape(cols, dtype):
        return jax.ShapeDtypeStruct((seq, cols), dtype)

    return pl.pallas_call(
        functools.partial(pre_kernel, heads, spots),
        grid=(seq // block,),
        in_specs=[SMEM, row(model), full(ba.shape), full(g64.shape), full(tri.shape), full(mq.shape), full(mk.shape),
                  full((8, 128)), full(gqk.shape)] + [ANY] * len(spots),
        out_specs=[row(model), ANY, full((8, model))] + [row(width)] * 3 + [row(128)] * 2 + [row(width)] * 5 + [row(128)],
        out_shape=[shape(model, BF), jax.ShapeDtypeStruct((model, wide), BF), jax.ShapeDtypeStruct((8, model), F32)]
        + [shape(width, BF)] * 3
        + [shape(128, BF)] * 2 + [shape(width, F32)] + [shape(width, BF)] * 4 + [shape(128, F32)],
        scratch_shapes=[pltpu.VMEM((8, model), F32), pltpu.VMEM((8, width), F32), pltpu.VMEM((8, width), F32),
                        pltpu.VMEM((8, 128), F32), pltpu.VMEM((model, wide), BF),
                        pltpu.SemaphoreType.DMA((len(spots) + 1,))],
        compiler_params=params(),
        cost_estimate=COST,
        name="pre",
    )(place, x, const(ba), const(g64), const(tri), const(mq), const(mk), rows, gqk,
      *[p for _, p in sorted(pieces.items())])


def fwd_kernel(chunk, block, q_ref, aq_ref, k_ref, ak_ref, v_ref, og_ref, *refs):
    u_ref, att_ref, li_ref = refs[-3:]
    pair = pl.program_id(0)
    q, aq = q_ref[...], aq_ref[...]
    lane = lanes(q.shape)
    ones = jnp.ones((block, 128), BF)
    fine = block // 2
    out = []
    for side in range(2):
        head = 2 * pair + side
        mine = (lane >= 64 * side) & (lane < 64 * side + 64)
        aug = (lane >= 6 * head) & (lane < 6 * head + 6)
        zero = jnp.zeros_like(q)
        qa = jnp.concatenate([jnp.where(mine, q, zero), jnp.where(aug, aq, zero)], 1)
        acc = jnp.zeros((block, 256), F32)
        for j in range(chunk):
            at = slice(j * block, (j + 1) * block)
            e = jnp.exp(dot(qa, jnp.concatenate([k_ref[at, :], ak_ref[at, :]], 1), NT))
            acc = acc + dot(e.astype(BF), jnp.concatenate([v_ref[at, :], ones], 1))
        tops = []
        for begin in range(0, block, fine):
            at = slice(chunk * block, chunk * block + begin + fine)
            rows = slice(begin, begin + fine)
            e = jnp.exp(dot(qa[rows], jnp.concatenate([k_ref[at, :], ak_ref[at, :]], 1), NT))
            e = jnp.where(rows_of(e.shape) + begin >= lanes(e.shape), e, 0.0)
            tops.append(acc[rows] + dot(e.astype(BF), jnp.concatenate([v_ref[at, :], ones[: begin + fine]], 1)))
        out.append(jnp.concatenate(tops, 0))
    low = lane < 64
    total = jnp.where(low, out[0][:, 128:], out[1][:, 128:])
    inverse = 1.0 / total
    att = jnp.where(low, out[0][:, :128], out[1][:, :128]) * inverse
    u_ref[...] = (att * og_ref[...]).astype(BF)
    att_ref[...] = att
    li_ref[...] = inverse


def attend(chunk, block, q8, aq, kn, ak, vl, og, kept):
    seq, width = q8.shape
    keys = (chunk + 1) * block
    grid = (width // 128,)
    mine = pl.BlockSpec((block, 128), lambda p: (chunk, p))
    other = pl.BlockSpec((keys, 128), lambda p: (0, p))
    return pl.pallas_call(
        functools.partial(fwd_kernel, chunk, block),
        grid=grid,
        in_specs=[mine, pl.BlockSpec((block, 128), lambda p: (chunk, 0)), other,
                  pl.BlockSpec((keys, 128), lambda p: (0, 0)), other, mine] + [ANY] * len(kept),
        out_specs=[pl.BlockSpec((block, 128), lambda p: (0, p)), mine, mine],
        out_shape=[jax.ShapeDtypeStruct((block, width), BF)] + [jax.ShapeDtypeStruct((seq, width), F32)] * 2,
        input_output_aliases={6 + i: 1 + i for i in range(len(kept))},
        compiler_params=params(),
        cost_estimate=COST,
        name="attend",
    )(q8, aq, kn, ak, vl, og, *kept)


def ffn_kernel(
    count, chunk, block, step_rows, own, at_ref, x_ref, cot_ref, gain_ref, o_any, f_any, *refs
):
    us, outs = refs[:count], refs[-10 - count : -3]
    o_ref, f_ref, sems = refs[-3:]
    copies = [pltpu.make_async_copy(a, b, sems.at[i]) for i, (a, b) in enumerate(((o_any, o_ref), (f_any, f_ref)))]

    copies[0].start()
    copies[1].start()
    h2_ref, hid_ref, dgu_ref, res_ref, uc_ref, part_ref = outs[:6]
    dus, gmid_ref = outs[6:-1], outs[-1]
    hidden = hid_ref.shape[1]
    gain = gain_ref[1:2, :]
    rows = x_ref.shape[0]
    size = rows // 2
    width = o_ref.shape[1] // count
    subs = [slice(i * size, (i + 1) * size) for i in range(2)]
    y1, n, factor, h2, gu, dhid, hid, dgu, dh2, res = [[None, None] for _ in range(10)]

    def first(i):
        u = jnp.concatenate([r[subs[i], :] for r in us], 1)
        uc_ref[subs[i], :] = u
        y1[i] = x_ref[subs[i], :].astype(F32) + dot(u, o_ref[...], NT)

    def normed(i):
        factor[i] = lax.rsqrt(jnp.mean(y1[i] * y1[i], -1, keepdims=True) + EPS)
        n[i] = y1[i] * factor[i]
        h2[i] = (n[i] * gain).astype(BF)
        h2_ref[subs[i], :] = h2[i]

    def gates(i):
        gu[i] = dot(h2[i], f_ref[:, : 2 * hidden])

    def hidden_back(i):
        dhid[i] = dot(cot_ref[subs[i], :], f_ref[:, 2 * hidden :])

    def activated(i):
        g, up = gu[i][:, :hidden], gu[i][:, hidden:]
        sg = jax.nn.sigmoid(g)
        act = g * sg
        hid[i] = (act * up).astype(BF)
        hid_ref[subs[i], :] = hid[i]
        dg = dhid[i] * up * sg * (1.0 + g * (1.0 - sg))
        dgu[i] = jnp.concatenate([dg.astype(BF), (dhid[i] * act).astype(BF)], 1)
        dgu_ref[subs[i], :] = dgu[i]

    def normed_back(i):
        dh2[i] = dot(dgu[i], f_ref[:, : 2 * hidden], NT)

    def part(i):
        token = chunk * block + pl.program_id(0) * step_rows + i * size + rows_of((size, 1))
        owned = (token >= at_ref[0] * own) & (token < (at_ref[0] + 1) * own)
        total = dot(hid[i], f_ref[:, 2 * hidden :], NT) + jnp.where(owned, y1[i], 0.0)
        part_ref[subs[i], :] = total.astype(BF)

    def residual(i):
        gmid_ref[i : i + 1, :] = jnp.sum(dh2[i] * n[i], 0, keepdims=True)
        wd = gain * dh2[i]
        back = factor[i] * (wd - n[i] * jnp.mean(wd * n[i], -1, keepdims=True))
        res[i] = jnp.where(at_ref[0] == 0, back + cot_ref[subs[i], :].astype(F32), back).astype(BF)
        res_ref[subs[i], :] = res[i]

    def last(i):
        du = dot(res[i], o_ref[...]).astype(BF)
        for s in range(count):
            dus[s][subs[i], :] = du[:, s * width : (s + 1) * width]

    gmid_ref[...] = jnp.zeros_like(gmid_ref)
    copies[0].wait()
    first(0)
    first(1)
    copies[1].wait()
    normed(0)
    hidden_back(0)
    gates(0)
    normed(1)
    hidden_back(1)
    gates(1)
    activated(0)
    normed_back(0)
    activated(1)
    normed_back(1)
    residual(0)
    part(0)
    last(0)
    residual(1)
    part(1)
    last(1)


def feed(chunk, block, own, place, x, cot, gains, o, f, us, kept):
    seq, model = x.shape
    hidden = f.shape[1] // 3
    count = len(us)
    width = us[0].shape[1]
    step_rows = block
    per = 1

    def mine(cols):
        return pl.BlockSpec((step_rows, cols), lambda i: (chunk * per + i, 0))

    def local(cols):
        return pl.BlockSpec((step_rows, cols), lambda i: (i, 0))

    kept_cols = [model, hidden, 2 * hidden, model, count * width, model]
    return pl.pallas_call(
        functools.partial(ffn_kernel, count, chunk, block, step_rows, own),
        grid=(per,),
        in_specs=[SMEM, mine(model), mine(model), full(gains.shape), ANY, ANY]
        + [local(width)] * count + [ANY] * len(kept),
        out_specs=[mine(c) for c in kept_cols] + [local(width)] * count + [full((8, model))],
        out_shape=[jax.ShapeDtypeStruct((seq, c), BF) for c in kept_cols]
        + [jax.ShapeDtypeStruct((block, width), BF)] * count + [jax.ShapeDtypeStruct((8, model), F32)],
        scratch_shapes=[pltpu.VMEM(o.shape, BF), pltpu.VMEM(f.shape, BF), pltpu.SemaphoreType.DMA((2,))],
        input_output_aliases={6 + count + i: i for i in range(len(kept))},
        compiler_params=params(),
        cost_estimate=COST,
        name="feed",
    )(place, x, cot, gains, o, f, *us, *kept)


def bwd_kernel(
    begin, heads, block, q_ref, aq_ref, k_ref, ak_ref, v_ref, og_ref, att_ref, li_ref, du_ref, ms_ref,
    dq_ref, dk_ref, dv_ref, dc_ref, da_s, ad_s,
):
    pair = begin + pl.program_id(0)
    seq = q_ref.shape[0]
    count = seq // block
    lane = lanes((block, 128))
    zero = jnp.zeros((block, 128), BF)
    ones = jnp.ones((block, 128), BF)
    third = lane - 3 * (lane // 3)
    for i in range(count):
        at = slice(i * block, (i + 1) * block)
        da = (du_ref[at, :].astype(F32) * og_ref[at, :] * li_ref[at, :]).astype(BF)
        da_s[at, :] = da
        delta = dot(jnp.concatenate(split2(da.astype(F32) * att_ref[at, :]), 1), ms_ref[...])
        hi, mid, rest = split3(-delta)
        ad_s[at, :] = jnp.where(third == 0, hi, jnp.where(third == 1, mid, rest))
    dk_ref[...] = jnp.zeros_like(dk_ref)
    dv_ref[...] = jnp.zeros_like(dv_ref)

    @pl.when(pl.program_id(0) == 0)
    def _():
        dc_ref[...] = jnp.zeros_like(dc_ref)


    vone = jnp.where(lane < 6, ones, zero)
    for i in range(count):
        at = slice(i * block, (i + 1) * block)
        q, aq, da, ad = q_ref[at, :], aq_ref[at, :], da_s[at, :], ad_s[at, :]
        dq = []
        for side in range(2):
            head = 2 * pair + side
            mine = (lane >= 64 * side) & (lane < 64 * side + 64)
            aug = (lane >= 6 * head) & (lane < 6 * head + 6)
            column = lane == 2 * heads + head
            qh = jnp.where(mine, q, zero)
            qa = jnp.concatenate([qh, jnp.where(aug, aq, zero)], 1)
            qo = jnp.concatenate([qh, ones], 1)
            dah = jnp.where(mine, da, zero)
            daa = jnp.concatenate([dah, jnp.where((lane >= 3 * side) & (lane < 3 * side + 3), ad, zero)], 1)
            acc = jnp.zeros((block, 256), F32)

            def pair_of(to, first):
                size = to.stop - to.start
                k = k_ref[to, :]
                e = jnp.exp(dot(jnp.concatenate([k, ak_ref[to, :]], 1), qa[first:], NT))
                if to.stop > i * block:
                    shift = to.start - i * block - first
                    e = jnp.where(rows_of(e.shape) + shift <= lanes(e.shape), e, 0.0)
                dv_ref[to, :] += dot(e.astype(BF), dah[first:])
                ds = (e * dot(jnp.concatenate([v_ref[to, :], vone[:size]], 1), daa[first:], NT)).astype(BF)
                dk = dot(ds, qo[first:])
                dk_ref[to, :] += dk[:, :128]
                dc_ref[to, :] -= jnp.where(column[:size], dk[:, 128:], 0.0)
                return dot(ds, jnp.concatenate([k, ones[:size]], 1), TN)

            for j in range(i):
                acc = acc + pair_of(slice(j * block, (j + 1) * block), 0)
            half = block // 2
            acc = acc + pair_of(slice(i * block, i * block + half), 0)
            acc = jnp.concatenate(
                [acc[:half], acc[half:] + pair_of(slice(i * block + half, (i + 1) * block), half)], 0
            )
            dq.append(acc[:, :128])
            dc_ref[at, :] += jnp.where(column, acc[:, 128:], 0.0)
        dq_ref[at, :] = jnp.where(lane < 64, dq[0], dq[1]) * 0.125


def attend_back(begin, end, block, heads, q8, aq, kn, ak, vl, og, att, li, du):
    seq, width = q8.shape
    ms = np.zeros((256, 128))
    for lane in range(256):
        ms[lane, 3 * ((lane % 128) // 64) : 3 * ((lane % 128) // 64) + 3] = 1.0
    mine = pl.BlockSpec((seq, 128), lambda p: (0, begin + p))
    own = pl.BlockSpec((seq, 128), lambda p: (0, p))
    one = pl.BlockSpec((seq, 128), lambda p: (0, 0))
    return pl.pallas_call(
        functools.partial(bwd_kernel, begin, heads, block),
        grid=(end - begin,),
        in_specs=[mine, one, mine, one, mine, mine, mine, mine, mine, full((256, 128))],
        out_specs=[own, own, own, one],
        out_shape=[jax.ShapeDtypeStruct((seq, 128 * (end - begin)), F32)] * 3 + [jax.ShapeDtypeStruct((seq, 128), F32)],
        scratch_shapes=[pltpu.VMEM((seq, 128), BF), pltpu.VMEM((seq, 128), BF)],
        compiler_params=params(),
        cost_estimate=COST,
        name="attend_back",
    )(q8, aq, kn, ak, vl, og, att, li, du, const(ms))


def post_kernel(
    heads, groups, q_ref, ks_ref, kd_ref, vd_ref, lg_ref, du_ref, att_ref, og_ref, x_ref,
    res_ref, gain_ref, w_ref, ba_ref, g64_ref, tri_ref, ms_ref, rows_ref, gqk_ref, *refs,
):
    grads, refs = refs[: 4 * groups], refs[4 * groups :]
    dp_ref, gt_ref, g0_ref, gq_ref, gb_ref, carry_k, carry_v, carry_c, w_s, sem = refs
    dq_raw, dk_raw, dvs = [
        jnp.concatenate([r[...] for r in grads[i * groups : (i + 1) * groups]], 1) for i in range(3)
    ]
    dc = sum(r[...] for r in grads[3 * groups :])
    step = pl.program_id(0)
    rows, width = q_ref.shape

    move = pltpu.make_async_copy(w_ref, w_s, sem)

    @pl.when(step == 0)
    def _():
        move.start()
        carry_k[...] = jnp.zeros_like(carry_k)
        carry_v[...] = jnp.zeros_like(carry_v)
        carry_c[...] = jnp.zeros_like(carry_c)
        g0_ref[...] = jnp.zeros_like(g0_ref)
        gq_ref[...] = jnp.zeros_like(gq_ref)
        gb_ref[...] = jnp.zeros_like(gb_ref)

    def norm_back(raw, gain, grad):
        r = lax.rsqrt(dot((raw * raw).astype(BF), g64_ref[...]) + EPS)
        n = raw * r
        wd = grad * gain
        return r * (wd - n * dot((wd * n).astype(BF), g64_ref[...])), jnp.sum(grad * n, 0, keepdims=True)

    dq, gq = norm_back(q_ref[...].astype(F32), gqk_ref[0:1, :], dq_raw)
    dks, gk = norm_back(ks_ref[...].astype(F32), gqk_ref[1:2, :], dk_raw)
    gq_ref[0:1, :] += gq
    gq_ref[1:2, :] += gk
    logits = lg_ref[...]
    sg = jax.nn.sigmoid(logits)
    mix = dot(jnp.concatenate(split2(sg), 1), ba_ref[...])
    end = rows_of(dks.shape) == rows - 1

    def shift_back(grad, part, carry):
        w = part * grad
        later = jnp.where(end, carry[0:1, :], pltpu.roll(w, rows - 1, 0))
        carry[0:1, :] = w[0:1, :]
        return grad - w + later

    dk = shift_back(dks, mix[:, :width], carry_k)
    dv = shift_back(dvs, mix[:, width:], carry_v)
    terms = jnp.concatenate([dks * kd_ref[...].astype(F32), dvs * vd_ref[...].astype(F32)], 1)
    hi, rest = split2(terms)
    dmix = dot(hi, ms_ref[...]) + dot(rest, ms_ref[...])
    sums = dot(tri_ref[...], jnp.concatenate(split3(dc), 1))
    dls = sums[:, :128] + sums[:, 128:256] + sums[:, 256:] + carry_c[0:1, :]
    carry_c[0:1, :] = dls[0:1, :]
    lane = lanes(logits.shape)
    dz = dls * jax.nn.sigmoid(-(logits + rows_ref[0:1, :]))
    dgl = jnp.where(lane < 2 * heads, dmix * sg * (1.0 - sg), jnp.where(lane < 3 * heads, dz, 0.0))
    gb_ref[0:1, :] += jnp.sum(dgl, 0, keepdims=True)
    og = og_ref[...]
    do = du_ref[...].astype(F32) * att_ref[...] * og * (1.0 - og)
    dp = jnp.concatenate([dq.astype(BF), dk.astype(BF), dv.astype(BF), do.astype(BF), dgl.astype(BF)], 1)
    dp_ref[...] = dp

    @pl.when(step == 0)
    def _():
        move.wait()

    dhn = dot(dp, w_s[...], NT)
    x = x_ref[...].astype(F32)
    factor = lax.rsqrt(jnp.mean(x * x, -1, keepdims=True) + EPS)
    n = x * factor
    g0_ref[0:1, :] += jnp.sum(dhn * n, 0, keepdims=True)
    wd = dhn * gain_ref[0:1, :]
    back = factor * (wd - n * jnp.mean(wd * n, -1, keepdims=True))
    gt_ref[...] = (back + res_ref[...].astype(F32)).astype(BF)


def post(heads, dq, dk, dv, dc, q, ks, kd, vd, lg, du, att, og, x, res, gains, w, bias_row, gqk):
    seq, width = q.shape
    groups = len(dq)
    model = x.shape[1]
    wide = w.shape[1]
    block = min(256, seq)
    count = seq // block
    ba = np.zeros((256, 2 * width))
    ms = np.zeros((2 * width, 128))
    for lane in range(2 * width):
        head = (lane % width) // 64 + (lane // width) * heads
        ba[head, lane] = ba[128 + head, lane] = 1.0
        ms[lane, head] = 1.0
    g64 = np.kron(np.eye(width // 64), np.full((64, 64), 1 / 64))
    tri = np.triu(np.ones((block, block)))
    rows = jnp.concatenate([bias_row, jnp.zeros((7, 128), F32)], 0)

    def row(cols):
        return pl.BlockSpec((block, cols), lambda i: (count - 1 - i, 0))

    return pl.pallas_call(
        functools.partial(post_kernel, heads, groups),
        grid=(count,),
        in_specs=[row(width)] * 4 + [row(128)] + [row(width)] * 3 + [row(model)] * 2
        + [full(gains.shape), ANY, full(ba.shape), full(g64.shape), full(tri.shape),
           full(ms.shape), full((8, 128)), full(gqk.shape)] + [row(g.shape[1]) for g in dq + dk + dv + dc],
        out_specs=[row(wide), row(model), full((8, model)), full((8, width)), full((8, 128))],
        out_shape=[jax.ShapeDtypeStruct((seq, wide), BF), jax.ShapeDtypeStruct((seq, model), BF),
                   jax.ShapeDtypeStruct((8, model), F32), jax.ShapeDtypeStruct((8, width), F32),
                   jax.ShapeDtypeStruct((8, 128), F32)],
        scratch_shapes=[pltpu.VMEM((8, width), F32), pltpu.VMEM((8, width), F32), pltpu.VMEM((8, 128), F32),
                        pltpu.VMEM(w.shape, BF), pltpu.SemaphoreType.DMA],
        compiler_params=params(),
        cost_estimate=COST,
        name="post",
    )(q, ks, kd, vd, lg, du, att, og, x, res, gains, w, const(ba), const(g64), const(tri),
      const(ms), rows, gqk, *dq, *dk, *dv, *dc)


def swap(value, axis, bit):
    size = lax.axis_size(axis)
    return lax.ppermute(value, axis, [(i, i ^ bit) for i in range(size)])


def turn(value):
    size = lax.axis_size("tp")
    return lax.ppermute(value, "tp", [(i, (i + 1) % size) for i in range(size)])


def add(a, b):
    return (a.astype(F32) + b.astype(F32)).astype(BF)


def high_bits(size):
    bits, bit = [], 2
    while bit < size:
        bits.append(bit)
        bit *= 2
    return bits


def gather_1(shard):
    pieces = {(0, 0): shard, (2, 0): swap(shard, "dp", 2)}
    if lax.axis_size("dp") == 8:
        pieces[4, 0] = swap(shard, "dp", 4)
    pieces[1, 0] = swap(shard, "dp", 1)
    return pieces


def gather_2(pieces):
    size = lax.axis_size("dp")
    pieces = dict(pieces)
    if size == 8:
        half = pieces[0, 0].shape[0] // 2
        pieces[6, 0] = swap(pieces[2, 0][:half], "dp", 4)
        pieces[6, half] = swap(pieces[4, 0][half:], "dp", 2)
        pieces[3, 0] = swap(pieces[2, 0], "dp", 1)
        pieces[5, 0] = swap(pieces[4, 0], "dp", 1)
        return pieces
    for bit in high_bits(size)[1:]:
        pieces.update({(r | bit, 0): swap(p, "dp", bit) for (r, _), p in list(pieces.items()) if not r & 1})
    return pieces


def gather_3(pieces):
    pieces = dict(pieces)
    pieces.update({(r | 1, s): swap(p, "dp", 1) for (r, s), p in list(pieces.items()) if (r | 1, s) not in pieces})
    return pieces


def assemble(pieces, me):
    cut, cols = pieces[0, 0].shape
    whole = jnp.zeros((cut * lax.axis_size("dp"), cols), BF)
    for (far, start), piece in sorted(pieces.items()):
        whole = lax.dynamic_update_slice_in_dim(whole, piece, (me ^ far) * cut + start, 0)
    return whole


def sides():
    size = lax.axis_size("dp")
    return [list(range(0, size, 2)), list(range(1, size, 2))]


def by_side(whole, me):
    rows = whole.shape[0] // lax.axis_size("dp")
    split = whole.reshape(-1, 2, rows, whole.shape[1])
    return [
        lax.dynamic_index_in_dim(split, side, 1, keepdims=False).reshape(-1, whole.shape[1])
        for side in (me % 2, 1 - me % 2)
    ]


def side_scatter(whole):
    return lax.psum_scatter(whole, "dp", scatter_dimension=0, tiled=True, axis_index_groups=sides())


def rows_major(value):
    return with_layout_constraint(value, Layout(major_to_minor=(0, 1)))


def scatter(whole):
    return lax.psum_scatter(whole, "dp", scatter_dimension=0, tiled=True)


def total_of(terms):
    return sum(term.astype(F32) for term in terms)


tie = lax.optimization_barrier


def pad_to(value, size, axis):
    extra = size - value.shape[axis]
    if not extra:
        return value
    return jnp.pad(value, [(0, extra if a == axis else 0) for a in range(value.ndim)])


def shards(
    tokens, attn_in, head_gates, out_proj, norm_gains, qk_gains, forget_bias, gate_up, down_proj, carried_offset,
    reset_flag, cotangent,
):
    dp, tp = lax.axis_size("dp"), lax.axis_size("tp")
    me_d, me_t = lax.axis_index("dp"), lax.axis_index("tp")
    _, seq, model = tokens.shape
    own = seq // tp
    cut = attn_in.shape[1]
    width_real = attn_in.shape[2]
    heads_real = head_gates.shape[2]
    heads = heads_real + heads_real % 2
    width = 64 * heads
    hidden = gate_up.shape[2]
    block = 512 if seq % 512 == 0 else seq
    chunks = seq // block

    attn_rows = jnp.transpose(pad_to(attn_in, width, 2), (1, 0, 2)).reshape(cut, 4 * width)
    gate_rows = jnp.transpose(pad_to(head_gates, heads, 2), (1, 0, 2)).reshape(cut, 3 * heads)
    gate_rows = pad_to(jnp.concatenate([gate_rows, jnp.transpose(norm_gains)], 1), 128, 1)
    attn_rows = jnp.concatenate([attn_rows, gate_rows], 1)
    out_own = pad_to(jnp.transpose(out_proj), width, 1)
    ffn_rows = jnp.concatenate([gate_up[0], gate_up[1], jnp.transpose(down_proj)], 1)

    bias = lax.dynamic_slice_in_dim(forget_bias.astype(F32), me_t * heads_real, heads_real, 0)
    offset = lax.dynamic_slice_in_dim(carried_offset[0], me_t * heads_real, heads_real, 0)
    bias = bias + (1 - reset_flag[0]).astype(F32) * offset
    bias_row = jnp.pad(bias, (2 * heads, 128 - 2 * heads - heads_real))[None, :]
    gqk = pad_to(jnp.tile(qk_gains.astype(F32), (1, heads)), 8, 0)
    at = me_t.astype(jnp.int32)[None]

    here = me_d.astype(jnp.int32)[None]
    x, cot = tokens[0], cotangent[0]

    def token_part(values, s):
        return lax.dynamic_slice_in_dim(values, lax.rem(me_t - s + tp, tp) * own, own, 0)

    def product(left, right):
        return dot(left, right, TN).astype(BF)

    attn_p = gather_1(attn_rows)
    out_rows = [out_own, turn(out_own)]
    while len(out_rows) < tp - 1:
        out_rows.append(turn(out_rows[-1]))
    attn_p, out_rows, ffn_rows = tie((attn_p, out_rows, ffn_rows))
    attn_p = gather_2(attn_p)
    out_rows.append(turn(out_rows[-1]))
    attn_p, out_rows, ffn_rows = tie((attn_p, out_rows, ffn_rows))
    out_whole = jnp.concatenate(out_rows, 1)
    attn_p, out_whole, ffn_rows = tie((attn_p, out_whole, ffn_rows))
    ffn_all = lax.all_gather(ffn_rows, "dp", axis=0, tiled=True)
    out_p = gather_1(out_whole)
    attn_p = gather_3(attn_p)
    hn, w, gains, q8, kn, vl, aq, ak, og, q, ks, kd, vd, lg = pre(x, here, attn_p, bias_row, gqk, heads)
    q8, out_p = tie((q8, out_p))
    out_p = gather_2(out_p)
    u, *kept_att = attend(0, block, q8, aq, kn, ak, vl, og, ())
    u, kept_att, q8 = tie((u, kept_att, q8))
    us = [[u]]

    first = tp - 1
    kept_ffn, gmids = (), []
    parts, got = [None] * chunks, [None] * chunks

    made = first + chunks
    sums = []
    out_all = None
    for t in range(first + chunks - 1 + first + 1):
        send = {}
        for c in range(chunks):
            step = t - first - c
            if 1 <= step <= first:
                send[c] = parts[c][1] if step == 1 else add(got[c], parts[c][step])
        y_send = token_part(kept_ffn[5], 1) if t == made + first - 1 else None
        send, q8, kept_ffn, x, y_send = tie((send, q8, kept_ffn, x, y_send))
        new_u = {c: turn(us[c][-1]) for c in range(len(us)) if 1 <= t - c + 1 <= first}
        new_du = {c: turn(value) for c, value in send.items()}
        fresh = None
        if t + 1 < chunks:
            fresh, *kept_att = attend(t + 1, block, q8, aq, kn, ak, vl, og, kept_att)
        if t == 2:
            out_all = assemble(gather_3(out_p), me_d)
        chunk = t - first
        if 0 <= chunk < chunks:
            outs = feed(chunk, block, own, at, x, cot, gains, out_all, ffn_all, us[chunk], kept_ffn)
            kept_ffn, parts[chunk] = outs[:6], outs[6:-1]
            gmids.append(outs[-1][0:1] + outs[-1][1:2])
        h2, hid, dgu, res, uc, part = kept_ffn if kept_ffn else [None] * 6
        if t == made + first - 1:
            y_acc = turn(y_send)
        fill = []
        if t == made:
            fill = [product(res, uc), rows_major(product(cot, hid))]
        if t == made + 1:
            fill = [product(h2, dgu)]
        out_q, out_p = out_p, None if t == 0 else out_p
        new_u, new_du, fresh, kept_att, kept_ffn, parts, fill, out_p, out_all, q8 = tie(
            (new_u, new_du, fresh, kept_att, kept_ffn, parts, fill, out_p, out_all, q8)
        )
        if t == 0:
            out_p = out_q
        sums += [scatter(value) for value in fill]
        for c, value in new_u.items():
            us[c].append(value)
        if fresh is not None:
            us.append([fresh])
        got = [new_du.get(c, got[c]) for c in range(chunks)]
    att, li = kept_att
    h2, hid, dgu, res, uc, part = kept_ffn

    du = jnp.concatenate([add(got[c], parts[c][0]) for c in range(chunks)], 0)
    du, gmid = tie((du, sum(gmids)))
    pairs, back_parts = width // 128, []
    cuts = [0, 1, pairs] if pairs > 1 else [0, pairs]
    y_step = 2
    ring = out_acc = None
    for begin, end in zip(cuts, cuts[1:]):
        back_parts.append(attend_back(begin, end, block, heads, q8, aq, kn, ak, vl, og, att, li, du))
        y_acc, back_parts = tie((y_acc, back_parts))
        if y_step < tp:
            send, y_step = add(y_acc, token_part(part, y_step)), y_step + 1
            if ring is None:
                ring, out_step = [sums[0][:, i * width : (i + 1) * width] for i in range(tp)], 2
                send, du, ring = tie((send, du, ring))
                out_acc = turn(ring[1])
            else:
                send, du = tie((send, du))
            y_acc = turn(send)
    dq, dk, dv, dc = zip(*back_parts)
    dp_all, gt, g0, gq, gb = post(
        heads, dq, dk, dv, dc, q, ks, kd, vd, lg, du, att, og, x, res, gains, w, bias_row, gqk
    )
    y_acc, dp_all, gt, g0, out_acc = tie((y_acc, dp_all, gt, g0, out_acc))

    send, out_send = token_part(gt, 1), None
    if out_step < tp:
        out_send, out_step = add(out_acc, ring[out_step]), out_step + 1
    send, dp_all, y_acc, out_acc, out_send, sums[1] = tie((send, dp_all, y_acc, out_acc, out_send, sums[1]))
    back = turn(send)
    if out_send is not None:
        out_acc = turn(out_send)
    attn_mine, attn_other = by_side(product(hn, dp_all), me_d)
    while y_step < tp:
        y_acc, y_step = turn(add(y_acc, token_part(part, y_step))), y_step + 1
    result = total_of((y_acc, token_part(part, 0))).astype(BF)
    grad_down = jnp.transpose(sums[1].astype(F32))
    gq = gq[0:2].reshape(2, heads, 64).sum(1)
    gb = lax.dynamic_update_slice_in_dim(
        jnp.zeros(forget_bias.shape, F32), gb[0, 2 * heads : 2 * heads + heads_real], me_t * heads_real, 0
    )
    small = jnp.concatenate([gq.reshape(-1), gb])
    small = jnp.pad(small, (0, model - small.shape[0]))[None]
    flat = jnp.concatenate([g0[0:1], gmid, small, jnp.zeros((5, model), F32)], 0)
    back, attn_mine, attn_other, flat, result, grad_down, out_acc = tie(
        (back, attn_mine, attn_other, flat, result, grad_down, out_acc)
    )
    hops = [("dp", 1 << i) for i in range(dp.bit_length() - 1)] + [("tp", 1 << i) for i in range(tp.bit_length() - 1)]
    for s in range(2, tp):
        send = add(back, token_part(gt, s))
        out_send = None
        if out_step < tp:
            out_send, out_step = add(out_acc, ring[out_step]), out_step + 1
        send, flat, out_send, attn_other = tie((send, flat, out_send, attn_other))
        back = turn(send)
        if out_send is not None:
            out_acc = turn(out_send)
        attn_sum = add(attn_mine, swap(attn_other, "dp", 1)) if s == 2 else None
        for _ in range(2):
            if hops:
                flat = flat + swap(flat, *hops.pop(0))
        back, flat, out_acc, attn_sum = tie((back, flat, out_acc, attn_sum))
        if attn_sum is not None:
            sums.append(side_scatter(attn_sum))
    while out_step < tp:
        out_acc, out_step = turn(add(out_acc, ring[out_step])), out_step + 1
    for axis, bit in hops:
        flat = flat + swap(flat, axis, bit)
    grad_tokens = total_of((token_part(gt, 0), back))
    grad_gu, grad_attn = [value.astype(F32) for value in sums[2:]]
    grad_out_own = total_of((ring[0], out_acc))
    norm_grad = flat[0:2]
    qk_grad = flat[2, : 2 * 64].reshape(2, 64)
    bias_grad = flat[2, 2 * 64 : 2 * 64 + forget_bias.shape[0]]

    grad_attn_in = jnp.transpose(grad_attn[:, : 4 * width].reshape(cut, 4, width)[:, :, :width_real], (1, 0, 2))
    grad_gates = grad_attn[:, 4 * width : 4 * width + 3 * heads].reshape(cut, 3, heads)[:, :, :heads_real]
    return (
        result[None],
        grad_tokens[None],
        grad_attn_in,
        jnp.transpose(grad_gates, (1, 0, 2)),
        jnp.transpose(grad_out_own[:, :width_real]),
        jnp.stack([grad_gu[:, :hidden], grad_gu[:, hidden:]]),
        grad_down,
        norm_grad,
        qk_grad,
        bias_grad,
    )


def solution(mesh):
    return jax.shard_map(
        shards,
        mesh=mesh,
        in_specs=(
            P("dp", None, None), P(None, "dp", "tp"), P(None, "dp", "tp"), P("tp", "dp"), P(None, "dp"), P(), P(),
            P(None, "dp", "tp"), P("tp", "dp"), P("dp", None), P("dp"), P("dp", None, None),
        ),
        out_specs=(
            P("dp", "tp", None), P("dp", "tp", None), P(None, "dp", "tp"), P(None, "dp", "tp"), P("tp", "dp"),
            P(None, "dp", "tp"), P("tp", "dp"), P(), P(), P(),
        ),
        check_vma=False,
    )
```

```python
import functools

import jax
import jax.numpy as jnp
import numpy as np
from jax import lax
from jax.experimental import pallas as pl
from jax.experimental.layout import Layout, with_layout_constraint
from jax.experimental.pallas import tpu as pltpu
from jax.sharding import PartitionSpec as P

EPS = 1e-06
BF = jnp.bfloat16
F32 = jnp.float32
VMEM_LIMIT = 58 * 1024 * 1024
NT = (((1,), (1,)), ((), ()))
TN = (((0,), (0,)), ((), ()))


COST = pl.CostEstimate(flops=1, bytes_accessed=1, transcendentals=0)


def dot(a, b, dims=(((1,), (0,)), ((), ()))):
    return lax.dot_general(a, b, dims, preferred_element_type=F32)


def params():
    return pltpu.CompilerParams(vmem_limit_bytes=VMEM_LIMIT)


def split2(v):
    hi = v.astype(BF)
    return hi, (v - hi.astype(F32)).astype(BF)


def split3(v):
    hi = v.astype(BF)
    rest = v - hi.astype(F32)
    mid = rest.astype(BF)
    return hi, mid, (rest - mid.astype(F32)).astype(BF)


def lanes(shape):
    return lax.broadcasted_iota(jnp.int32, shape, len(shape) - 1)


def rows_of(shape):
    return lax.broadcasted_iota(jnp.int32, shape, 0)


def const(array, dtype=BF):
    return jnp.asarray(array.astype(np.float32), dtype)


def full(shape):
    return pl.BlockSpec(shape, lambda *_: tuple(0 for _ in shape), pipeline_mode=pl.Buffered(1))


ANY = pl.BlockSpec(memory_space=pl.ANY)
SMEM = pl.BlockSpec(memory_space=pltpu.SMEM)


def pre_kernel(
    heads, spots, me_ref, x_ref, ba_ref, g64_ref, tri_ref, mq_ref, mk_ref, rows_ref, gqk_ref, *refs,
):
    pieces, refs = refs[: len(spots)], refs[len(spots) :]
    (hn_ref, w_ref, gain_ref, q8_ref, kn_ref, vl_ref, aq_ref, ak_ref, og_ref, q_ref, ks_ref, kd_ref, vd_ref, lg_ref,
     gain_s, carry_k, carry_v, carry_c, w_s, sems) = refs
    keep = pltpu.make_async_copy(w_s, w_ref, sems.at[len(spots)])
    step = pl.program_id(0)
    width = q8_ref.shape[1]
    wide = 4 * width

    @pl.when(step == 0)
    def _():
        copies = []
        for i, (far, start, count, cut) in enumerate(spots):
            row = pl.multiple_of((me_ref[0] ^ far) * cut + start, 16)
            copies.append(pltpu.make_async_copy(pieces[i], w_s.at[pl.ds(row, count), :], sems.at[i]))
        for copy in copies:
            copy.start()
        for copy in copies:
            copy.wait()
        keep.start()
        pick = (lanes((8, 128)) == 3 * heads + rows_of((8, 128))).astype(F32)
        pick = jnp.where(rows_of((8, 128)) < 2, pick, 0.0).astype(BF)
        gain_s[...] = dot(pick, w_s[:, wide:], NT)
        carry_k[...] = jnp.zeros_like(carry_k)
        carry_v[...] = jnp.zeros_like(carry_v)
        carry_c[...] = jnp.zeros_like(carry_c)
        gain_ref[...] = gain_s[...]

    x = x_ref[...].astype(F32)
    factor = lax.rsqrt(jnp.mean(x * x, -1, keepdims=True) + EPS)
    hn = (x * factor * gain_s[0:1, :]).astype(BF)
    hn_ref[...] = hn
    proj = dot(hn, w_s[...])
    q = proj[:, :width]
    k = proj[:, width : 2 * width]
    v = proj[:, 2 * width : 3 * width]
    og_ref[...] = jax.nn.sigmoid(proj[:, 3 * width : wide])
    logits = proj[:, wide:]
    lg_ref[...] = logits
    mix = dot(jnp.concatenate(split2(jax.nn.sigmoid(logits)), 1), ba_ref[...])
    first = rows_of(k.shape) == 0
    kd = jnp.where(first, carry_k[0:1, :], pltpu.roll(k, 1, 0)) - k
    vd = jnp.where(first, carry_v[0:1, :], pltpu.roll(v, 1, 0)) - v
    last = k.shape[0] - 1
    carry_k[0:1, :] = k[last:, :]
    carry_v[0:1, :] = v[last:, :]
    ks = k + mix[:, :width] * kd
    vl_ref[...] = (v + mix[:, width:] * vd).astype(BF)
    q_ref[...] = q.astype(BF)
    ks_ref[...] = ks.astype(BF)
    kd_ref[...] = kd.astype(BF)
    vd_ref[...] = vd.astype(BF)
    rq = lax.rsqrt(dot((q * q).astype(BF), g64_ref[...]) + EPS)
    rk = lax.rsqrt(dot((ks * ks).astype(BF), g64_ref[...]) + EPS)
    q8_ref[...] = ((q * rq * gqk_ref[0:1, :]).astype(BF).astype(F32) * 0.125).astype(BF)
    kn_ref[...] = (ks * rk * gqk_ref[1:2, :]).astype(BF)
    z = logits + rows_ref[0:1, :]
    ls = jnp.minimum(z, 0.0) - jnp.log1p(jnp.exp(-jnp.abs(z)))
    sums = dot(tri_ref[...], jnp.concatenate(split3(ls), 1))
    cum = sums[:, :128] + sums[:, 128:256] + sums[:, 256:] + carry_c[0:1, :]
    carry_c[0:1, :] = cum[last:, :]
    parts = jnp.concatenate(split3(cum), 1)
    aq_ref[...] = (dot(parts, mq_ref[...]) + rows_ref[1:2, :]).astype(BF)
    ak_ref[...] = (dot(parts, mk_ref[...]) + rows_ref[2:3, :]).astype(BF)

    @pl.when(step == pl.num_programs(0) - 1)
    def _():
        keep.wait()


def pre(x, place, pieces, bias_row, gqk, heads):
    seq, model = x.shape
    cut = pieces[0, 0].shape[0]
    spots = [(far, start, p.shape[0], cut) for (far, start), p in sorted(pieces.items())]
    wide = pieces[0, 0].shape[1]
    width = (wide - 128) // 4
    block = min(256, seq)
    ba = np.zeros((256, 2 * width))
    for lane in range(2 * width):
        head = (lane % width) // 64 + (lane // width) * heads
        ba[head, lane] = ba[128 + head, lane] = 1.0
    g64 = np.kron(np.eye(width // 64), np.full((64, 64), 1 / 64))
    tri = np.tril(np.ones((block, block)))
    mq, mk = np.zeros((384, 128)), np.zeros((384, 128))
    ones_q, ones_k = np.zeros((1, 128)), np.zeros((1, 128))
    for head in range(heads):
        for piece in range(3):
            mq[128 * piece + 2 * heads + head, 6 * head + piece] = 1.0
            mk[128 * piece + 2 * heads + head, 6 * head + 3 + piece] = -1.0
            ones_q[0, 6 * head + 3 + piece] = 1.0
            ones_k[0, 6 * head + piece] = 1.0
    rows = jnp.concatenate([bias_row, const(ones_q, F32), const(ones_k, F32), jnp.zeros((5, 128), F32)], 0)

    def row(cols):
        return pl.BlockSpec((block, cols), lambda i: (i, 0))

    def shape(cols, dtype):
        return jax.ShapeDtypeStruct((seq, cols), dtype)

    return pl.pallas_call(
        functools.partial(pre_kernel, heads, spots),
        grid=(seq // block,),
        in_specs=[SMEM, row(model), full(ba.shape), full(g64.shape), full(tri.shape), full(mq.shape), full(mk.shape),
                  full((8, 128)), full(gqk.shape)] + [ANY] * len(spots),
        out_specs=[row(model), ANY, full((8, model))] + [row(width)] * 3 + [row(128)] * 2 + [row(width)] * 5 + [row(128)],
        out_shape=[shape(model, BF), jax.ShapeDtypeStruct((model, wide), BF), jax.ShapeDtypeStruct((8, model), F32)]
        + [shape(width, BF)] * 3
        + [shape(128, BF)] * 2 + [shape(width, F32)] + [shape(width, BF)] * 4 + [shape(128, F32)],
        scratch_shapes=[pltpu.VMEM((8, model), F32), pltpu.VMEM((8, width), F32), pltpu.VMEM((8, width), F32),
                        pltpu.VMEM((8, 128), F32), pltpu.VMEM((model, wide), BF),
                        pltpu.SemaphoreType.DMA((len(spots) + 1,))],
        compiler_params=params(),
        cost_estimate=COST,
        name="pre",
    )(place, x, const(ba), const(g64), const(tri), const(mq), const(mk), rows, gqk,
      *[p for _, p in sorted(pieces.items())])


def fwd_kernel(chunk, block, q_ref, aq_ref, k_ref, ak_ref, v_ref, og_ref, *refs):
    u_ref, att_ref, li_ref = refs[-3:]
    pair = pl.program_id(0)
    q, aq = q_ref[...], aq_ref[...]
    lane = lanes(q.shape)
    ones = jnp.ones((block, 128), BF)
    fine = block // 2
    out = []
    for side in range(2):
        head = 2 * pair + side
        mine = (lane >= 64 * side) & (lane < 64 * side + 64)
        aug = (lane >= 6 * head) & (lane < 6 * head + 6)
        zero = jnp.zeros_like(q)
        qa = jnp.concatenate([jnp.where(mine, q, zero), jnp.where(aug, aq, zero)], 1)
        acc = jnp.zeros((block, 256), F32)
        for j in range(chunk):
            at = slice(j * block, (j + 1) * block)
            e = jnp.exp(dot(qa, jnp.concatenate([k_ref[at, :], ak_ref[at, :]], 1), NT))
            acc = acc + dot(e.astype(BF), jnp.concatenate([v_ref[at, :], ones], 1))
        tops = []
        for begin in range(0, block, fine):
            at = slice(chunk * block, chunk * block + begin + fine)
            rows = slice(begin, begin + fine)
            e = jnp.exp(dot(qa[rows], jnp.concatenate([k_ref[at, :], ak_ref[at, :]], 1), NT))
            e = jnp.where(rows_of(e.shape) + begin >= lanes(e.shape), e, 0.0)
            tops.append(acc[rows] + dot(e.astype(BF), jnp.concatenate([v_ref[at, :], ones[: begin + fine]], 1)))
        out.append(jnp.concatenate(tops, 0))
    low = lane < 64
    total = jnp.where(low, out[0][:, 128:], out[1][:, 128:])
    inverse = 1.0 / total
    att = jnp.where(low, out[0][:, :128], out[1][:, :128]) * inverse
    u_ref[...] = (att * og_ref[...]).astype(BF)
    att_ref[...] = att
    li_ref[...] = inverse


def attend(chunk, block, q8, aq, kn, ak, vl, og, kept):
    seq, width = q8.shape
    keys = (chunk + 1) * block
    grid = (width // 128,)
    mine = pl.BlockSpec((block, 128), lambda p: (chunk, p))
    other = pl.BlockSpec((keys, 128), lambda p: (0, p))
    return pl.pallas_call(
        functools.partial(fwd_kernel, chunk, block),
        grid=grid,
        in_specs=[mine, pl.BlockSpec((block, 128), lambda p: (chunk, 0)), other,
                  pl.BlockSpec((keys, 128), lambda p: (0, 0)), other, mine] + [ANY] * len(kept),
        out_specs=[pl.BlockSpec((block, 128), lambda p: (0, p)), mine, mine],
        out_shape=[jax.ShapeDtypeStruct((block, width), BF)] + [jax.ShapeDtypeStruct((seq, width), F32)] * 2,
        input_output_aliases={6 + i: 1 + i for i in range(len(kept))},
        compiler_params=params(),
        cost_estimate=COST,
        name="attend",
    )(q8, aq, kn, ak, vl, og, *kept)


def ffn_kernel(
    count, chunk, block, step_rows, own, at_ref, x_ref, cot_ref, gain_ref, o_any, f_any, *refs
):
    us, outs = refs[:count], refs[-10 - count : -3]
    o_ref, f_ref, sems = refs[-3:]
    copies = [pltpu.make_async_copy(a, b, sems.at[i]) for i, (a, b) in enumerate(((o_any, o_ref), (f_any, f_ref)))]

    copies[0].start()
    copies[1].start()
    h2_ref, hid_ref, dgu_ref, res_ref, uc_ref, part_ref = outs[:6]
    dus, gmid_ref = outs[6:-1], outs[-1]
    hidden = hid_ref.shape[1]
    gain = gain_ref[1:2, :]
    rows = x_ref.shape[0]
    size = rows // 2
    width = o_ref.shape[1] // count
    subs = [slice(i * size, (i + 1) * size) for i in range(2)]
    y1, n, factor, h2, gu, dhid, hid, dgu, dh2, res = [[None, None] for _ in range(10)]

    def first(i):
        u = jnp.concatenate([r[subs[i], :] for r in us], 1)
        uc_ref[subs[i], :] = u
        y1[i] = x_ref[subs[i], :].astype(F32) + dot(u, o_ref[...], NT)

    def normed(i):
        factor[i] = lax.rsqrt(jnp.mean(y1[i] * y1[i], -1, keepdims=True) + EPS)
        n[i] = y1[i] * factor[i]
        h2[i] = (n[i] * gain).astype(BF)
        h2_ref[subs[i], :] = h2[i]

    def gates(i):
        gu[i] = dot(h2[i], f_ref[:, : 2 * hidden])

    def hidden_back(i):
        dhid[i] = dot(cot_ref[subs[i], :], f_ref[:, 2 * hidden :])

    def activated(i):
        g, up = gu[i][:, :hidden], gu[i][:, hidden:]
        sg = jax.nn.sigmoid(g)
        act = g * sg
        hid[i] = (act * up).astype(BF)
        hid_ref[subs[i], :] = hid[i]
        dg = dhid[i] * up * sg * (1.0 + g * (1.0 - sg))
        dgu[i] = jnp.concatenate([dg.astype(BF), (dhid[i] * act).astype(BF)], 1)
        dgu_ref[subs[i], :] = dgu[i]

    def normed_back(i):
        dh2[i] = dot(dgu[i], f_ref[:, : 2 * hidden], NT)

    def part(i):
        token = chunk * block + pl.program_id(0) * step_rows + i * size + rows_of((size, 1))
        owned = (token >= at_ref[0] * own) & (token < (at_ref[0] + 1) * own)
        total = dot(hid[i], f_ref[:, 2 * hidden :], NT) + jnp.where(owned, y1[i], 0.0)
        part_ref[subs[i], :] = total.astype(BF)

    def residual(i):
        gmid_ref[i : i + 1, :] = jnp.sum(dh2[i] * n[i], 0, keepdims=True)
        wd = gain * dh2[i]
        back = factor[i] * (wd - n[i] * jnp.mean(wd * n[i], -1, keepdims=True))
        res[i] = jnp.where(at_ref[0] == 0, back + cot_ref[subs[i], :].astype(F32), back).astype(BF)
        res_ref[subs[i], :] = res[i]

    def last(i):
        du = dot(res[i], o_ref[...]).astype(BF)
        for s in range(count):
            dus[s][subs[i], :] = du[:, s * width : (s + 1) * width]

    gmid_ref[...] = jnp.zeros_like(gmid_ref)
    copies[0].wait()
    first(0)
    first(1)
    copies[1].wait()
    normed(0)
    hidden_back(0)
    gates(0)
    normed(1)
    hidden_back(1)
    gates(1)
    activated(0)
    normed_back(0)
    activated(1)
    normed_back(1)
    residual(0)
    part(0)
    last(0)
    residual(1)
    part(1)
    last(1)


def feed(chunk, block, own, place, x, cot, gains, o, f, us, kept):
    seq, model = x.shape
    hidden = f.shape[1] // 3
    count = len(us)
    width = us[0].shape[1]
    step_rows = block
    per = 1

    def mine(cols):
        return pl.BlockSpec((step_rows, cols), lambda i: (chunk * per + i, 0))

    def local(cols):
        return pl.BlockSpec((step_rows, cols), lambda i: (i, 0))

    kept_cols = [model, hidden, 2 * hidden, model, count * width, model]
    return pl.pallas_call(
        functools.partial(ffn_kernel, count, chunk, block, step_rows, own),
        grid=(per,),
        in_specs=[SMEM, mine(model), mine(model), full(gains.shape), ANY, ANY]
        + [local(width)] * count + [ANY] * len(kept),
        out_specs=[mine(c) for c in kept_cols] + [local(width)] * count + [full((8, model))],
        out_shape=[jax.ShapeDtypeStruct((seq, c), BF) for c in kept_cols]
        + [jax.ShapeDtypeStruct((block, width), BF)] * count + [jax.ShapeDtypeStruct((8, model), F32)],
        scratch_shapes=[pltpu.VMEM(o.shape, BF), pltpu.VMEM(f.shape, BF), pltpu.SemaphoreType.DMA((2,))],
        input_output_aliases={6 + count + i: i for i in range(len(kept))},
        compiler_params=params(),
        cost_estimate=COST,
        name="feed",
    )(place, x, cot, gains, o, f, *us, *kept)


def bwd_kernel(
    begin, heads, block, q_ref, aq_ref, k_ref, ak_ref, v_ref, og_ref, att_ref, li_ref, du_ref, ms_ref,
    dq_ref, dk_ref, dv_ref, dc_ref, da_s, ad_s,
):
    pair = begin + pl.program_id(0)
    seq = q_ref.shape[0]
    count = seq // block
    lane = lanes((block, 128))
    zero = jnp.zeros((block, 128), BF)
    ones = jnp.ones((block, 128), BF)
    third = lane - 3 * (lane // 3)
    for i in range(count):
        at = slice(i * block, (i + 1) * block)
        da = (du_ref[at, :].astype(F32) * og_ref[at, :] * li_ref[at, :]).astype(BF)
        da_s[at, :] = da
        delta = dot(jnp.concatenate(split2(da.astype(F32) * att_ref[at, :]), 1), ms_ref[...])
        hi, mid, rest = split3(-delta)
        ad_s[at, :] = jnp.where(third == 0, hi, jnp.where(third == 1, mid, rest))
    dk_ref[...] = jnp.zeros_like(dk_ref)
    dv_ref[...] = jnp.zeros_like(dv_ref)

    @pl.when(pl.program_id(0) == 0)
    def _():
        dc_ref[...] = jnp.zeros_like(dc_ref)


    vone = jnp.where(lane < 6, ones, zero)
    for i in range(count):
        at = slice(i * block, (i + 1) * block)
        q, aq, da, ad = q_ref[at, :], aq_ref[at, :], da_s[at, :], ad_s[at, :]
        dq = []
        for side in range(2):
            head = 2 * pair + side
            mine = (lane >= 64 * side) & (lane < 64 * side + 64)
            aug = (lane >= 6 * head) & (lane < 6 * head + 6)
            column = lane == 2 * heads + head
            qh = jnp.where(mine, q, zero)
            qa = jnp.concatenate([qh, jnp.where(aug, aq, zero)], 1)
            qo = jnp.concatenate([qh, ones], 1)
            dah = jnp.where(mine, da, zero)
            daa = jnp.concatenate([dah, jnp.where((lane >= 3 * side) & (lane < 3 * side + 3), ad, zero)], 1)
            acc = jnp.zeros((block, 256), F32)

            def pair_of(to, first):
                size = to.stop - to.start
                k = k_ref[to, :]
                e = jnp.exp(dot(jnp.concatenate([k, ak_ref[to, :]], 1), qa[first:], NT))
                if to.stop > i * block:
                    shift = to.start - i * block - first
                    e = jnp.where(rows_of(e.shape) + shift <= lanes(e.shape), e, 0.0)
                dv_ref[to, :] += dot(e.astype(BF), dah[first:])
                ds = (e * dot(jnp.concatenate([v_ref[to, :], vone[:size]], 1), daa[first:], NT)).astype(BF)
                dk = dot(ds, qo[first:])
                dk_ref[to, :] += dk[:, :128]
                dc_ref[to, :] -= jnp.where(column[:size], dk[:, 128:], 0.0)
                return dot(ds, jnp.concatenate([k, ones[:size]], 1), TN)

            for j in range(i):
                acc = acc + pair_of(slice(j * block, (j + 1) * block), 0)
            half = block // 2
            acc = acc + pair_of(slice(i * block, i * block + half), 0)
            acc = jnp.concatenate(
                [acc[:half], acc[half:] + pair_of(slice(i * block + half, (i + 1) * block), half)], 0
            )
            dq.append(acc[:, :128])
            dc_ref[at, :] += jnp.where(column, acc[:, 128:], 0.0)
        dq_ref[at, :] = jnp.where(lane < 64, dq[0], dq[1]) * 0.125


def attend_back(begin, end, block, heads, q8, aq, kn, ak, vl, og, att, li, du):
    seq, width = q8.shape
    ms = np.zeros((256, 128))
    for lane in range(256):
        ms[lane, 3 * ((lane % 128) // 64) : 3 * ((lane % 128) // 64) + 3] = 1.0
    mine = pl.BlockSpec((seq, 128), lambda p: (0, begin + p))
    own = pl.BlockSpec((seq, 128), lambda p: (0, p))
    one = pl.BlockSpec((seq, 128), lambda p: (0, 0))
    return pl.pallas_call(
        functools.partial(bwd_kernel, begin, heads, block),
        grid=(end - begin,),
        in_specs=[mine, one, mine, one, mine, mine, mine, mine, mine, full((256, 128))],
        out_specs=[own, own, own, one],
        out_shape=[jax.ShapeDtypeStruct((seq, 128 * (end - begin)), F32)] * 3 + [jax.ShapeDtypeStruct((seq, 128), F32)],
        scratch_shapes=[pltpu.VMEM((seq, 128), BF), pltpu.VMEM((seq, 128), BF)],
        compiler_params=params(),
        cost_estimate=COST,
        name="attend_back",
    )(q8, aq, kn, ak, vl, og, att, li, du, const(ms))


def post_kernel(
    heads, groups, q_ref, ks_ref, kd_ref, vd_ref, lg_ref, du_ref, att_ref, og_ref, x_ref,
    res_ref, gain_ref, w_ref, ba_ref, g64_ref, tri_ref, ms_ref, rows_ref, gqk_ref, *refs,
):
    grads, refs = refs[: 4 * groups], refs[4 * groups :]
    dp_ref, gt_ref, g0_ref, gq_ref, gb_ref, carry_k, carry_v, carry_c, w_s, sem = refs
    dq_raw, dk_raw, dvs = [
        jnp.concatenate([r[...] for r in grads[i * groups : (i + 1) * groups]], 1) for i in range(3)
    ]
    dc = sum(r[...] for r in grads[3 * groups :])
    step = pl.program_id(0)
    rows, width = q_ref.shape

    move = pltpu.make_async_copy(w_ref, w_s, sem)

    @pl.when(step == 0)
    def _():
        move.start()
        carry_k[...] = jnp.zeros_like(carry_k)
        carry_v[...] = jnp.zeros_like(carry_v)
        carry_c[...] = jnp.zeros_like(carry_c)
        g0_ref[...] = jnp.zeros_like(g0_ref)
        gq_ref[...] = jnp.zeros_like(gq_ref)
        gb_ref[...] = jnp.zeros_like(gb_ref)

    def norm_back(raw, gain, grad):
        r = lax.rsqrt(dot((raw * raw).astype(BF), g64_ref[...]) + EPS)
        n = raw * r
        wd = grad * gain
        return r * (wd - n * dot((wd * n).astype(BF), g64_ref[...])), jnp.sum(grad * n, 0, keepdims=True)

    dq, gq = norm_back(q_ref[...].astype(F32), gqk_ref[0:1, :], dq_raw)
    dks, gk = norm_back(ks_ref[...].astype(F32), gqk_ref[1:2, :], dk_raw)
    gq_ref[0:1, :] += gq
    gq_ref[1:2, :] += gk
    logits = lg_ref[...]
    sg = jax.nn.sigmoid(logits)
    mix = dot(jnp.concatenate(split2(sg), 1), ba_ref[...])
    end = rows_of(dks.shape) == rows - 1

    def shift_back(grad, part, carry):
        w = part * grad
        later = jnp.where(end, carry[0:1, :], pltpu.roll(w, rows - 1, 0))
        carry[0:1, :] = w[0:1, :]
        return grad - w + later

    dk = shift_back(dks, mix[:, :width], carry_k)
    dv = shift_back(dvs, mix[:, width:], carry_v)
    terms = jnp.concatenate([dks * kd_ref[...].astype(F32), dvs * vd_ref[...].astype(F32)], 1)
    hi, rest = split2(terms)
    dmix = dot(hi, ms_ref[...]) + dot(rest, ms_ref[...])
    sums = dot(tri_ref[...], jnp.concatenate(split3(dc), 1))
    dls = sums[:, :128] + sums[:, 128:256] + sums[:, 256:] + carry_c[0:1, :]
    carry_c[0:1, :] = dls[0:1, :]
    lane = lanes(logits.shape)
    dz = dls * jax.nn.sigmoid(-(logits + rows_ref[0:1, :]))
    dgl = jnp.where(lane < 2 * heads, dmix * sg * (1.0 - sg), jnp.where(lane < 3 * heads, dz, 0.0))
    gb_ref[0:1, :] += jnp.sum(dgl, 0, keepdims=True)
    og = og_ref[...]
    do = du_ref[...].astype(F32) * att_ref[...] * og * (1.0 - og)
    dp = jnp.concatenate([dq.astype(BF), dk.astype(BF), dv.astype(BF), do.astype(BF), dgl.astype(BF)], 1)
    dp_ref[...] = dp

    @pl.when(step == 0)
    def _():
        move.wait()

    dhn = dot(dp, w_s[...], NT)
    x = x_ref[...].astype(F32)
    factor = lax.rsqrt(jnp.mean(x * x, -1, keepdims=True) + EPS)
    n = x * factor
    g0_ref[0:1, :] += jnp.sum(dhn * n, 0, keepdims=True)
    wd = dhn * gain_ref[0:1, :]
    back = factor * (wd - n * jnp.mean(wd * n, -1, keepdims=True))
    gt_ref[...] = (back + res_ref[...].astype(F32)).astype(BF)


def post(heads, dq, dk, dv, dc, q, ks, kd, vd, lg, du, att, og, x, res, gains, w, bias_row, gqk):
    seq, width = q.shape
    groups = len(dq)
    model = x.shape[1]
    wide = w.shape[1]
    block = min(256, seq)
    count = seq // block
    ba = np.zeros((256, 2 * width))
    ms = np.zeros((2 * width, 128))
    for lane in range(2 * width):
        head = (lane % width) // 64 + (lane // width) * heads
        ba[head, lane] = ba[128 + head, lane] = 1.0
        ms[lane, head] = 1.0
    g64 = np.kron(np.eye(width // 64), np.full((64, 64), 1 / 64))
    tri = np.triu(np.ones((block, block)))
    rows = jnp.concatenate([bias_row, jnp.zeros((7, 128), F32)], 0)

    def row(cols):
        return pl.BlockSpec((block, cols), lambda i: (count - 1 - i, 0))

    return pl.pallas_call(
        functools.partial(post_kernel, heads, groups),
        grid=(count,),
        in_specs=[row(width)] * 4 + [row(128)] + [row(width)] * 3 + [row(model)] * 2
        + [full(gains.shape), ANY, full(ba.shape), full(g64.shape), full(tri.shape),
           full(ms.shape), full((8, 128)), full(gqk.shape)] + [row(g.shape[1]) for g in dq + dk + dv + dc],
        out_specs=[row(wide), row(model), full((8, model)), full((8, width)), full((8, 128))],
        out_shape=[jax.ShapeDtypeStruct((seq, wide), BF), jax.ShapeDtypeStruct((seq, model), BF),
                   jax.ShapeDtypeStruct((8, model), F32), jax.ShapeDtypeStruct((8, width), F32),
                   jax.ShapeDtypeStruct((8, 128), F32)],
        scratch_shapes=[pltpu.VMEM((8, width), F32), pltpu.VMEM((8, width), F32), pltpu.VMEM((8, 128), F32),
                        pltpu.VMEM(w.shape, BF), pltpu.SemaphoreType.DMA],
        compiler_params=params(),
        cost_estimate=COST,
        name="post",
    )(q, ks, kd, vd, lg, du, att, og, x, res, gains, w, const(ba), const(g64), const(tri),
      const(ms), rows, gqk, *dq, *dk, *dv, *dc)


def swap(value, axis, bit):
    size = lax.axis_size(axis)
    return lax.ppermute(value, axis, [(i, i ^ bit) for i in range(size)])


def turn(value):
    size = lax.axis_size("tp")
    return lax.ppermute(value, "tp", [(i, (i + 1) % size) for i in range(size)])


def add(a, b):
    return (a.astype(F32) + b.astype(F32)).astype(BF)


def high_bits(size):
    bits, bit = [], 2
    while bit < size:
        bits.append(bit)
        bit *= 2
    return bits


def gather_1(shard):
    pieces = {(0, 0): shard, (2, 0): swap(shard, "dp", 2)}
    if lax.axis_size("dp") == 8:
        pieces[4, 0] = swap(shard, "dp", 4)
    pieces[1, 0] = swap(shard, "dp", 1)
    return pieces


def gather_2(pieces):
    size = lax.axis_size("dp")
    pieces = dict(pieces)
    if size == 8:
        half = pieces[0, 0].shape[0] // 2
        pieces[6, 0] = swap(pieces[2, 0][:half], "dp", 4)
        pieces[6, half] = swap(pieces[4, 0][half:], "dp", 2)
        pieces[3, 0] = swap(pieces[2, 0], "dp", 1)
        pieces[5, 0] = swap(pieces[4, 0], "dp", 1)
        return pieces
    for bit in high_bits(size)[1:]:
        pieces.update({(r | bit, 0): swap(p, "dp", bit) for (r, _), p in list(pieces.items()) if not r & 1})
    return pieces


def gather_3(pieces):
    pieces = dict(pieces)
    pieces.update({(r | 1, s): swap(p, "dp", 1) for (r, s), p in list(pieces.items()) if (r | 1, s) not in pieces})
    return pieces


def assemble(pieces, me):
    cut, cols = pieces[0, 0].shape
    whole = jnp.zeros((cut * lax.axis_size("dp"), cols), BF)
    for (far, start), piece in sorted(pieces.items()):
        whole = lax.dynamic_update_slice_in_dim(whole, piece, (me ^ far) * cut + start, 0)
    return whole


def sides():
    size = lax.axis_size("dp")
    return [list(range(0, size, 2)), list(range(1, size, 2))]


def by_side(whole, me):
    rows = whole.shape[0] // lax.axis_size("dp")
    split = whole.reshape(-1, 2, rows, whole.shape[1])
    return [
        lax.dynamic_index_in_dim(split, side, 1, keepdims=False).reshape(-1, whole.shape[1])
        for side in (me % 2, 1 - me % 2)
    ]


def side_scatter(whole):
    return lax.psum_scatter(whole, "dp", scatter_dimension=0, tiled=True, axis_index_groups=sides())


def rows_major(value):
    return with_layout_constraint(value, Layout(major_to_minor=(0, 1)))


def scatter(whole):
    return lax.psum_scatter(whole, "dp", scatter_dimension=0, tiled=True)


def total_of(terms):
    return sum(term.astype(F32) for term in terms)


tie = lax.optimization_barrier


def pad_to(value, size, axis):
    extra = size - value.shape[axis]
    if not extra:
        return value
    return jnp.pad(value, [(0, extra if a == axis else 0) for a in range(value.ndim)])


def shards(
    tokens, attn_in, head_gates, out_proj, norm_gains, qk_gains, forget_bias, gate_up, down_proj, carried_offset,
    reset_flag, cotangent,
):
    dp, tp = lax.axis_size("dp"), lax.axis_size("tp")
    me_d, me_t = lax.axis_index("dp"), lax.axis_index("tp")
    _, seq, model = tokens.shape
    own = seq // tp
    cut = attn_in.shape[1]
    width_real = attn_in.shape[2]
    heads_real = head_gates.shape[2]
    heads = heads_real + heads_real % 2
    width = 64 * heads
    hidden = gate_up.shape[2]
    block = 512 if seq % 512 == 0 else seq
    chunks = seq // block

    attn_rows = jnp.transpose(pad_to(attn_in, width, 2), (1, 0, 2)).reshape(cut, 4 * width)
    gate_rows = jnp.transpose(pad_to(head_gates, heads, 2), (1, 0, 2)).reshape(cut, 3 * heads)
    gate_rows = pad_to(jnp.concatenate([gate_rows, jnp.transpose(norm_gains)], 1), 128, 1)
    attn_rows = jnp.concatenate([attn_rows, gate_rows], 1)
    out_own = pad_to(jnp.transpose(out_proj), width, 1)
    ffn_rows = jnp.concatenate([gate_up[0], gate_up[1], jnp.transpose(down_proj)], 1)

    bias = lax.dynamic_slice_in_dim(forget_bias.astype(F32), me_t * heads_real, heads_real, 0)
    offset = lax.dynamic_slice_in_dim(carried_offset[0], me_t * heads_real, heads_real, 0)
    bias = bias + (1 - reset_flag[0]).astype(F32) * offset
    bias_row = jnp.pad(bias, (2 * heads, 128 - 2 * heads - heads_real))[None, :]
    gqk = pad_to(jnp.tile(qk_gains.astype(F32), (1, heads)), 8, 0)
    at = me_t.astype(jnp.int32)[None]

    here = me_d.astype(jnp.int32)[None]
    x, cot = tokens[0], cotangent[0]

    def token_part(values, s):
        return lax.dynamic_slice_in_dim(values, lax.rem(me_t - s + tp, tp) * own, own, 0)

    def product(left, right):
        return dot(left, right, TN).astype(BF)

    def attn_outputs(rows):
        rows = rows.astype(F32)
        proj = rows[:, : 4 * width].reshape(cut, 4, width)[:, :, :width_real]
        gates = rows[:, 4 * width : 4 * width + 3 * heads].reshape(cut, 3, heads)[:, :, :heads_real]
        return jnp.transpose(proj, (1, 0, 2)), jnp.transpose(gates, (1, 0, 2))

    attn_p = gather_1(attn_rows)
    out_rows = [out_own, turn(out_own)]
    while len(out_rows) < tp - 1:
        out_rows.append(turn(out_rows[-1]))
    attn_p, out_rows, ffn_rows = tie((attn_p, out_rows, ffn_rows))
    attn_p = gather_2(attn_p)
    out_rows.append(turn(out_rows[-1]))
    attn_p, out_rows, ffn_rows = tie((attn_p, out_rows, ffn_rows))
    out_whole = jnp.concatenate(out_rows, 1)
    attn_p, out_whole, ffn_rows = tie((attn_p, out_whole, ffn_rows))
    ffn_all = lax.all_gather(ffn_rows, "dp", axis=0, tiled=True)
    out_p = gather_1(out_whole)
    attn_p = gather_3(attn_p)
    hn, w, gains, q8, kn, vl, aq, ak, og, q, ks, kd, vd, lg = pre(x, here, attn_p, bias_row, gqk, heads)
    q8, out_p = tie((q8, out_p))
    out_p = gather_2(out_p)
    u, *kept_att = attend(0, block, q8, aq, kn, ak, vl, og, ())
    u, kept_att, q8 = tie((u, kept_att, q8))
    us = [[u]]

    first = tp - 1
    kept_ffn, gmids = (), []
    parts, got = [None] * chunks, [None] * chunks

    made = first + chunks
    sums = []
    out_all = None
    for t in range(first + chunks - 1 + first + 1):
        send = {}
        for c in range(chunks):
            step = t - first - c
            if 1 <= step <= first:
                send[c] = parts[c][1] if step == 1 else add(got[c], parts[c][step])
        y_send = token_part(kept_ffn[5], 1) if t == made + first - 1 else None
        send, q8, kept_ffn, x, y_send = tie((send, q8, kept_ffn, x, y_send))
        new_u = {c: turn(us[c][-1]) for c in range(len(us)) if 1 <= t - c + 1 <= first}
        new_du = {c: turn(value) for c, value in send.items()}
        fresh = None
        if t + 1 < chunks:
            fresh, *kept_att = attend(t + 1, block, q8, aq, kn, ak, vl, og, kept_att)
        if t == 2:
            out_all = assemble(gather_3(out_p), me_d)
        chunk = t - first
        if 0 <= chunk < chunks:
            outs = feed(chunk, block, own, at, x, cot, gains, out_all, ffn_all, us[chunk], kept_ffn)
            kept_ffn, parts[chunk] = outs[:6], outs[6:-1]
            gmids.append(outs[-1][0:1] + outs[-1][1:2])
        h2, hid, dgu, res, uc, part = kept_ffn if kept_ffn else [None] * 6
        if t == made + first - 1:
            y_acc = turn(y_send)
        fill = []
        if t == made:
            fill = [product(res, uc), rows_major(product(cot, hid))]
        if t == made + 1:
            fill = [product(h2, dgu)]
        out_q, out_p = out_p, None if t == 0 else out_p
        new_u, new_du, fresh, kept_att, kept_ffn, parts, fill, out_p, out_all, q8 = tie(
            (new_u, new_du, fresh, kept_att, kept_ffn, parts, fill, out_p, out_all, q8)
        )
        if t == 0:
            out_p = out_q
        sums += [scatter(value) for value in fill]
        for c, value in new_u.items():
            us[c].append(value)
        if fresh is not None:
            us.append([fresh])
        got = [new_du.get(c, got[c]) for c in range(chunks)]
    att, li = kept_att
    h2, hid, dgu, res, uc, part = kept_ffn

    du = jnp.concatenate([add(got[c], parts[c][0]) for c in range(chunks)], 0)
    du, gmid = tie((du, sum(gmids)))
    pairs, back_parts = width // 128, []
    cuts = [0, 1, pairs] if pairs > 1 else [0, pairs]
    y_step = 2
    ring = out_acc = None
    for begin, end in zip(cuts, cuts[1:]):
        back_parts.append(attend_back(begin, end, block, heads, q8, aq, kn, ak, vl, og, att, li, du))
        y_acc, back_parts = tie((y_acc, back_parts))
        if y_step < tp:
            send, y_step = add(y_acc, token_part(part, y_step)), y_step + 1
            if ring is None:
                ring, out_step = [sums[0][:, i * width : (i + 1) * width] for i in range(tp)], 2
                send, du, ring = tie((send, du, ring))
                out_acc = turn(ring[1])
            else:
                send, du = tie((send, du))
            y_acc = turn(send)
    dq, dk, dv, dc = zip(*back_parts)
    dp_all, gt, g0, gq, gb = post(
        heads, dq, dk, dv, dc, q, ks, kd, vd, lg, du, att, og, x, res, gains, w, bias_row, gqk
    )
    y_acc, dp_all, gt, g0, out_acc = tie((y_acc, dp_all, gt, g0, out_acc))

    send, out_send = token_part(gt, 1), None
    if out_step < tp:
        out_send, out_step = add(out_acc, ring[out_step]), out_step + 1
    send, dp_all, y_acc, out_acc, out_send, sums[1] = tie((send, dp_all, y_acc, out_acc, out_send, sums[1]))
    back = turn(send)
    if out_send is not None:
        out_acc = turn(out_send)
    attn_mine, attn_other = by_side(product(hn, dp_all), me_d)
    while y_step < tp:
        y_acc, y_step = turn(add(y_acc, token_part(part, y_step))), y_step + 1
    result = total_of((y_acc, token_part(part, 0))).astype(BF)
    grad_down = jnp.transpose(sums[1].astype(F32))
    gq = gq[0:2].reshape(2, heads, 64).sum(1)
    gb = lax.dynamic_update_slice_in_dim(
        jnp.zeros(forget_bias.shape, F32), gb[0, 2 * heads : 2 * heads + heads_real], me_t * heads_real, 0
    )
    small = jnp.concatenate([gq.reshape(-1), gb])
    small = jnp.pad(small, (0, model - small.shape[0]))[None]
    flat = jnp.concatenate([g0[0:1], gmid, small, jnp.zeros((5, model), F32)], 0)
    dp_hops = [("dp", 1 << i) for i in range(dp.bit_length() - 1)]
    tp_hops = [("tp", 1 << i) for i in range(tp.bit_length() - 1)]
    flat = flat + swap(flat, *dp_hops.pop(0))
    back, attn_mine, attn_other, flat, result, grad_down, out_acc = tie(
        (back, attn_mine, attn_other, flat, result, grad_down, out_acc)
    )
    finals = None
    for s in range(2, tp):
        send = add(back, token_part(gt, s))
        out_send = None
        if out_step < tp:
            out_send, out_step = add(out_acc, ring[out_step]), out_step + 1
        send, flat, out_send, attn_other = tie((send, flat, out_send, attn_other))
        back = turn(send)
        if out_send is not None:
            out_acc = turn(out_send)
        attn_sum = add(attn_mine, swap(attn_other, "dp", 1)) if s == 2 else None
        if dp_hops:
            flat = flat + swap(flat, *dp_hops.pop(0))
        if s == tp - 1 and s > 2:
            attn_rows, out_rows, _ = tie((sums[-1], out_acc, flat))
            finals = attn_outputs(attn_rows), jnp.transpose(total_of((ring[0], out_rows))[:, :width_real])
        if tp_hops:
            flat = flat + swap(flat, *tp_hops.pop(0))
        back, flat, out_acc, attn_sum, finals = tie((back, flat, out_acc, attn_sum, finals))
        if attn_sum is not None:
            sums.append(side_scatter(attn_sum))
    for axis, bit in dp_hops + tp_hops:
        flat = flat + swap(flat, axis, bit)
    grad_tokens = total_of((token_part(gt, 0), back))
    grad_gu = sums[2].astype(F32)
    (grad_attn_in, grad_gates), grad_out_own = finals
    norm_grad = flat[0:2]
    qk_grad = flat[2, : 2 * 64].reshape(2, 64)
    bias_grad = flat[2, 2 * 64 : 2 * 64 + forget_bias.shape[0]]

    return (
        result[None],
        grad_tokens[None],
        grad_attn_in,
        grad_gates,
        grad_out_own,
        jnp.stack([grad_gu[:, :hidden], grad_gu[:, hidden:]]),
        grad_down,
        norm_grad,
        qk_grad,
        bias_grad,
    )


def solution(mesh):
    return jax.shard_map(
        shards,
        mesh=mesh,
        in_specs=(
            P("dp", None, None), P(None, "dp", "tp"), P(None, "dp", "tp"), P("tp", "dp"), P(None, "dp"), P(), P(),
            P(None, "dp", "tp"), P("tp", "dp"), P("dp", None), P("dp"), P("dp", None, None),
        ),
        out_specs=(
            P("dp", "tp", None), P("dp", "tp", None), P(None, "dp", "tp"), P(None, "dp", "tp"), P("tp", "dp"),
            P(None, "dp", "tp"), P("tp", "dp"), P(), P(), P(),
        ),
        check_vma=False,
    )
```
